32 devices in a mesh: tok: 8 (over y, x, core), mlp: 4 (over z).
Axes of the slice: x: 2, y: 2, z: 4, core: 2. Of those that a mesh axis runs over, the one named last changes fastest.
Arguments:
- tokens: bfloat16 [37632, 384], P(('tok', 'mlp')), may hold values from -6 to 6
- action_mask: int32 [64, 588], P(('tok', 'mlp')), may hold values 0 or 1
- ln1_gain: bfloat16 [384], replicated, may hold values from 0.5 to 1.5
- ln1_bias: bfloat16 [384], replicated, may hold values from -3 to 3
- w_qkv: bfloat16 [384, 3072], P('tok'), may hold values from -0.3125 to 0.3125
- bias_qv: bfloat16 [2048], replicated, may hold values from -4 to 4
- w_out: bfloat16 [1024, 384], P('tok'), may hold values from -0.75 to 0.75
- bias_out: bfloat16 [384], replicated, may hold values from -3 to 3
- ln2_gain: bfloat16 [384], replicated, may hold values from 0.5 to 1.5
- ln2_bias: bfloat16 [384], replicated, may hold values from -3 to 3
- w_fc1: bfloat16 [384, 2048], P('tok', 'mlp'), may hold values from -0.3125 to 0.3125
- bias_fc1: bfloat16 [2048], P('mlp'), may hold values from -4 to 4
- w_fc2: bfloat16 [2048, 384], P('mlp', 'tok'), may hold values from -0.125 to 0.125
- bias_fc2: bfloat16 [384], replicated, may hold values from -3 to 3
- out_grad: bfloat16 [37632, 384], P(('tok', 'mlp')), may hold values from -6 to 6
Outputs:
- output: bfloat16 [37632, 384], P(('tok', 'mlp'))
- input_grad: float32 [37632, 384], P(('tok', 'mlp'))
- ln1_gain_grad: float32 [384], replicated
- ln1_bias_grad: float32 [384], replicated
- w_qkv_grad: float32 [384, 3072], P('tok')
- bias_qv_grad: float32 [2048], replicated
- w_out_grad: float32 [1024, 384], P('tok')
- bias_out_grad: float32 [384], replicated
- ln2_gain_grad: float32 [384], replicated
- ln2_bias_grad: float32 [384], replicated
- w_fc1_grad: float32 [384, 2048], P('tok', 'mlp')
- bias_fc1_grad: float32 [2048], P('mlp')
- w_fc2_grad: float32 [2048, 384], P('mlp', 'tok')
- bias_fc2_grad: float32 [384], replicated
The draws below stay inside these ranges and needn't reach their ends.
All inputs are finite; a program needn't handle non-finite values. No bound on the sum of `action_mask` on one device may be relied on, other than what follows from the above.
Results may differ from the reference program's by a relative error of at most 0.017.
Values may be sent and summed in bfloat16 or wider, within the bound.
No kernel may reach another device: no remote copies, remote signals or barrier semaphores. Data moves between devices by JAX's collectives and lax.ppermute only.
A program may use at most 192 MiB of HBM per device.

```python
import jax
import jax.numpy as jnp
from jax import lax

D = 384
HEADS = 16
HEAD_DIM = 64
FF = 2048
FRAME_LEN = 196
INNER = 1024
LEN = 588
SEQS = 64
TOKENS = 37632


def plant(array, rng, least, top_value):
    place = [jax.random.randint(jax.random.fold_in(rng, axis), (), 0, length) for axis, length in enumerate(array.shape)]
    longest = array.shape.index(max(array.shape))
    neighbour = place[:longest] + [(place[longest] + 1) % array.shape[longest]] + place[longest + 1:]
    return array.at[tuple(place)].set(least).at[tuple(neighbour)].set(top_value)


def shard_levels(key, shape, pieces, low, top_value):
    level, own = 1.0, jax.random.fold_in(key, 6)
    for position, blocks in pieces:
        steps = jnp.exp(jax.random.uniform(jax.random.fold_in(own, position), (blocks,), jnp.float32, low / len(pieces), top_value / len(pieces)))
        level = level * jnp.repeat(steps, shape[position] // blocks).reshape([-1 if axis == position else 1 for axis in range(len(shape))])
    return level


def centred(key, dims, deviation, limit, pieces=(), held_as=jnp.bfloat16):
    array = deviation * jax.random.normal(key, dims, jnp.float32)
    if pieces:
        array = array * shard_levels(key, dims, pieces, -0.22, 0.18)
    return jnp.clip(array, -limit, limit).astype(held_as)


def setup_inputs(seed: int = 0) -> dict:
    seeds = jax.random.split(jax.random.key(seed), 16)
    tokens = centred(seeds[0], (TOKENS, D), 1.0, 6.0, ((0, 32),))
    action_mask = plant((jax.random.randint(seeds[1], (SEQS, LEN), 0, 4) < 3).astype(jnp.int32), jax.random.fold_in(seeds[1], 1), 0, 1)
    ln1_gain = jnp.clip(1.0 + 0.1 * jax.random.normal(seeds[2], (D,), jnp.float32), 0.5, 1.5).astype(jnp.bfloat16)
    ln1_bias = centred(seeds[3], (D,), 0.3, 3.0)
    w_qkv = centred(seeds[4], (D, 3 * INNER), D ** -0.5, 0.3125, ((0, 8),))
    bias_qv = centred(seeds[5], (2 * INNER,), 0.5, 4.0)
    w_out = centred(seeds[6], (INNER, D), (INNER // 16) ** -0.5, 0.75, ((0, 8),))
    bias_out = centred(seeds[7], (D,), 0.3, 3.0)
    ln2_gain = jnp.clip(1.0 + 0.1 * jax.random.normal(seeds[8], (D,), jnp.float32), 0.5, 1.5).astype(jnp.bfloat16)
    ln2_bias = centred(seeds[9], (D,), 0.3, 3.0)
    w_fc1 = centred(seeds[10], (D, FF), D ** -0.5, 0.3125, ((0, 8), (1, 4)))
    bias_fc1 = centred(seeds[11], (FF,), 0.5, 4.0, ((0, 4),))
    w_fc2 = centred(seeds[12], (FF, D), FF ** -0.5, 0.125, ((0, 4), (1, 8)))
    bias_fc2 = centred(seeds[13], (D,), 0.3, 3.0)
    out_grad = centred(seeds[14], (TOKENS, D), 1.0, 6.0, ((0, 32),))
    return {"tokens": tokens, "action_mask": action_mask, "ln1_gain": ln1_gain, "ln1_bias": ln1_bias, "w_qkv": w_qkv, "bias_qv": bias_qv, "w_out": w_out, "bias_out": bias_out, "ln2_gain": ln2_gain, "ln2_bias": ln2_bias, "w_fc1": w_fc1, "bias_fc1": bias_fc1, "w_fc2": w_fc2, "bias_fc2": bias_fc2, "out_grad": out_grad}


epsilon = 1e-06
highest = lax.Precision.HIGHEST

@jax.custom_vjp
def low(v):
    return lax.optimization_barrier(v.astype(jnp.bfloat16)).astype(jnp.float32)

@jax.custom_vjp
def low_back(v):
    return v

def low_keep(v):
    return (low(v), None)

def low_pass(kept, grad):
    return (grad,)

def back_keep(v):
    return (v, None)

def back_low(kept, grad):
    return (low(grad),)
low.defvjp(low_keep, low_pass)
low_back.defvjp(back_keep, back_low)

def normalize(values, norm_gain, norm_shift):
    center = values - lax.optimization_barrier(jnp.mean(values, axis=-1, keepdims=True))
    inverse = lax.rsqrt(lax.optimization_barrier(jnp.mean(center * center, axis=-1, keepdims=True)) + epsilon)
    return center * inverse * norm_gain + norm_shift

def allowed_keys(mask_rows):
    length = mask_rows.shape[1]
    frame_row = jnp.arange(length, dtype=jnp.int32) // FRAME_LEN
    earlier = frame_row[None, :] <= frame_row[:, None]
    usable = earlier[None] & (mask_rows[:, None, :] == 1)
    return usable | jnp.eye(length, dtype=bool)[None]

def block_layer(inputs, ln1_gain, ln1_bias, w_qkv, bias_qv, w_out, bias_out, ln2_gain, ln2_bias, w_fc1, bias_fc1, w_fc2, bias_fc2, allowed):
    row_total = inputs.shape[0]
    seq_count = allowed.shape[0]
    length = row_total // seq_count
    inner = HEADS * HEAD_DIM
    first_norm = low(normalize(inputs, ln1_gain, ln1_bias))
    projected = jnp.dot(first_norm, w_qkv, precision=highest)
    queries = low(low_back(projected[:, :inner] + bias_qv[:inner]))
    keys_all = low(low_back(projected[:, inner:2 * inner]))
    values_all = low(low_back(projected[:, 2 * inner:] + bias_qv[inner:]))
    head_shape = (seq_count, length, HEADS, HEAD_DIM)
    query_heads = queries.reshape(head_shape)
    key_heads = keys_all.reshape(head_shape)
    value_heads = values_all.reshape(head_shape)
    scores = jnp.einsum('sqhd,skhd->shqk', query_heads, key_heads, precision=highest) * HEAD_DIM ** (-0.5)
    scores = low_back(scores)
    scores = jnp.where(allowed[:, None], scores, -1e+30)
    probabilities = jax.nn.softmax(scores, axis=-1)
    mixed_heads = jnp.einsum('shqk,skhd->sqhd', low(probabilities), value_heads, precision=highest)
    mixed_heads = low(low_back(mixed_heads.reshape(row_total, inner)))
    branch = low_back(jnp.dot(mixed_heads, w_out, precision=highest) + bias_out)
    middle = inputs + branch
    second_norm = low(normalize(middle, ln2_gain, ln2_bias))
    hidden_pre = low_back(jnp.dot(second_norm, w_fc1, precision=highest) + bias_fc1)
    hidden_act = low(jax.nn.gelu(hidden_pre, approximate=False))
    mlp_out = low_back(jnp.dot(hidden_act, w_fc2, precision=highest) + bias_fc2)
    return middle + mlp_out

def reference(tokens, action_mask, ln1_gain, ln1_bias, w_qkv, bias_qv, w_out, bias_out, ln2_gain, ln2_bias, w_fc1, bias_fc1, w_fc2, bias_fc2, out_grad):
    weights_float = tuple((member.astype(jnp.float32) for member in (ln1_gain, ln1_bias, w_qkv, bias_qv, w_out, bias_out, ln2_gain, ln2_bias, w_fc1, bias_fc1, w_fc2, bias_fc2)))
    group_count = SEQS // 4
    token_groups = tokens.astype(jnp.float32).reshape(group_count, 4 * LEN, D)
    cotangent_groups = out_grad.astype(jnp.float32).reshape(group_count, 4 * LEN, D)
    mask_groups = action_mask.reshape(group_count, 4, LEN)

    def group_step(totals, group_item):
        group_inputs, group_cotangent, group_mask = group_item
        allowed = allowed_keys(group_mask)

        def layer_call(inputs, *weight_list):
            return block_layer(inputs, *weight_list, allowed)
        layer_out, pullback = jax.vjp(layer_call, group_inputs, *weights_float)
        gradients = pullback(group_cotangent)
        totals = tuple((before + added for before, added in zip(totals, gradients[1:])))
        return (totals, (layer_out.astype(jnp.bfloat16), gradients[0]))
    zero_totals = tuple((jnp.zeros_like(member) for member in weights_float))
    totals, (outputs, input_grads) = lax.scan(group_step, zero_totals, (token_groups, cotangent_groups, mask_groups))
    output = outputs.reshape(TOKENS, D)
    input_grad = input_grads.reshape(TOKENS, D)
    return (output, input_grad, totals[0], totals[1], totals[2], totals[3], totals[4], totals[5], totals[6], totals[7], totals[8], totals[9], totals[10], totals[11])
```

```python
import functools

import jax
import jax.numpy as jnp
from jax import lax
from jax.experimental import pallas as pl
from jax.experimental.pallas import tpu as pltpu
from jax.sharding import PartitionSpec as P

HEADS = 16
HEAD_DIM = 64
FRAME_LEN = 196
LEN = 588
D = 384
FF = 2048
INNER = HEADS * HEAD_DIM
KEYS = 592
ROWS = 640
GROUP = 4
WIDE = GROUP * HEAD_DIM
GROUPS = HEADS // GROUP
QKV = 3 * WIDE
SMALL = 128
BLOCK = INNER + SMALL

epsilon = 1e-06
f32 = jnp.float32
bf16 = jnp.bfloat16

NN = (((1,), (0,)), ((), ()))
NT = (((1,), (1,)), ((), ()))
TN = (((0,), (0,)), ((), ()))

QUERY_BLOCKS = ((0, 128, 208), (128, 256, 400), (384, 256, 592))
KEY_RANGES = ((0, 208, 0), (208, 400, 128), (400, 592, 384))

VMEM = 56 * 1024 * 1024

BIAS_OUT, GAIN_TWO, SHIFT_TWO, BIAS_TWO, GAIN_ONE, SHIFT_ONE = (slice(k, k + 1) for k in range(6))


def dot(left, right, dims):
    return lax.dot_general(left, right, dims, preferred_element_type=f32)


def normalize(values):
    center = values - jnp.mean(values, axis=-1, keepdims=True)
    inverse = lax.rsqrt(jnp.mean(center * center, axis=-1, keepdims=True) + epsilon)
    return center * inverse, inverse


def normalize_back(grad_rows, norm_gain, scaled, inverse):
    scaled_grad = grad_rows * norm_gain
    return inverse * (
        scaled_grad
        - jnp.mean(scaled_grad, axis=-1, keepdims=True)
        - scaled * jnp.mean(scaled_grad * scaled, axis=-1, keepdims=True)
    )


def cost(micros):
    return pl.CostEstimate(flops=int(micros * 1.1e9), bytes_accessed=1024, transcendentals=0)


MASKS = (0, 2, 4, 6, 1, 3, 5, 7)


def owners(me, count):
    return [me ^ mask for mask in MASKS[:count]]


def whole(shape):
    return pl.BlockSpec(
        shape, lambda *step: (0,) * len(shape), pipeline_mode=pl.Buffered(buffer_count=1)
    )


def prepare_kernel(one_ref, two_ref, hidden_bias_ref, out_ref, bias_ref, *refs):
    row_refs, (pack_ref, block_ref, rows_ref, columns_ref, wide_bias_ref) = refs[:6], refs[6:]
    rows, slot = one_ref.shape
    pack_ref[:rows, :slot] = one_ref[...]
    pack_ref[:rows, slot:] = two_ref[...]
    pack_ref[rows:] = jnp.zeros_like(pack_ref[rows:])
    pack_ref[rows : rows + 1, :slot] = hidden_bias_ref[...].reshape(1, slot)
    turned = out_ref[...].T
    width = turned.shape[1]
    for r in range(D // rows):
        block_ref[:, r * width : (r + 1) * width] = turned[r * rows : (r + 1) * rows]
    rows_ref[...] = jnp.zeros_like(rows_ref)
    for k, ref in enumerate(row_refs):
        rows_ref[k : k + 1] = ref[...].astype(f32).reshape(1, D)
    columns_ref[...] = rows_ref[...].T
    wide_bias_ref[...] = bias_ref[...].astype(f32).reshape(1, 2 * INNER)


def prepare(w_fc1, w_fc2, bias_fc1, w_out, bias_qv, vectors):
    rows, slot = w_fc1.shape
    return pl.pallas_call(
        prepare_kernel,
        out_shape=[
            jax.ShapeDtypeStruct((rows + 16, 2 * slot), bf16),
            jax.ShapeDtypeStruct((rows, INNER), bf16),
            jax.ShapeDtypeStruct((8, D), f32),
            jax.ShapeDtypeStruct((D, 8), f32),
            jax.ShapeDtypeStruct((1, 2 * INNER), f32),
        ],
        cost_estimate=cost(2),
        name="prepare",
    )(w_fc1, w_fc2.T, bias_fc1, w_out, bias_qv, *vectors)


def norm_kernel(tokens_ref, rows_ref, out_ref, scaled_ref):
    for s in range(out_ref.shape[0]):
        values = tokens_ref[s * LEN : (s + 1) * LEN].astype(f32)
        scaled, _ = normalize(values)
        normed = scaled * rows_ref[GAIN_ONE] + rows_ref[SHIFT_ONE]
        for ref, rows in ((scaled_ref, scaled), (out_ref, normed)):
            ref[s, :LEN] = rows.astype(bf16)
            ref[s, LEN:] = jnp.zeros((ROWS - LEN, D), bf16)


def first_norm(tokens, rows_in):
    seqs = tokens.shape[0] // LEN
    shape = jax.ShapeDtypeStruct((seqs, ROWS, D), bf16)
    return pl.pallas_call(
        norm_kernel,
        out_shape=[shape, shape],
        compiler_params=pltpu.CompilerParams(vmem_limit_bytes=10 * 1024 * 1024),
        cost_estimate=cost(2.5),
        name="first_norm",
    )(tokens, rows_in)


def attend_kernel(pieces, me_ref, normed_ref, bias_ref, mask_ref, *refs):
    parts, refs = refs[:pieces], refs[pieces:]
    projected_ref, mixed_ref, exp_ref, inverse_ref, wide_ref = refs[:5]
    hide_scr, score_scr, mixed_scr, total_scr, mask_scr = refs[5:]
    group, seq = pl.program_id(0), pl.program_id(1)

    @pl.when((group == 0) & (seq == 0))
    def _():
        rows = D // pieces
        for j, owner in enumerate(owners(me_ref[0], pieces)):
            to = pl.ds(pl.multiple_of(owner * rows, 16), rows)
            for g in range(GROUPS):
                for k in range(3):
                    left = k * INNER + g * WIDE
                    at = g * QKV + k * WIDE
                    wide_ref[to, at : at + WIDE] = parts[j][:, left : left + WIDE]
        total_scr[...] = jnp.ones_like(total_scr)
        mask_scr[...] = jnp.zeros_like(mask_scr)
        count = hide_scr.shape[0]
        mask_scr[:count, :LEN] = mask_ref[...].astype(f32)
        turned = mask_scr[...].T
        key = lax.broadcasted_iota(jnp.int32, (KEYS, ROWS), 0)
        query = lax.broadcasted_iota(jnp.int32, (KEYS, ROWS), 1)
        later = ((query < FRAME_LEN) & (key >= FRAME_LEN)) | (
            (query < 2 * FRAME_LEN) & (key >= 2 * FRAME_LEN)
        )
        for s in range(count):
            usable = jnp.logical_not(later) & (turned[:KEYS, s : s + 1] > 0.5)
            hide_scr[s] = jnp.where(usable | (key == query), 0.0, -1e30)

    columns = pl.ds(pl.multiple_of(group * QKV, 128), QKV)
    projected = dot(normed_ref[seq, :KEYS], wide_ref[:, columns], NN)
    at = pl.multiple_of(group * WIDE, 128)
    queries = (projected[:, :WIDE] + bias_ref[:, pl.ds(at, WIDE)]).astype(bf16)
    projected_ref[0, :KEYS, :WIDE] = queries * bf16(HEAD_DIM**-0.5)
    projected_ref[0, :KEYS, WIDE : 2 * WIDE] = projected[:, WIDE : 2 * WIDE].astype(bf16)
    values = projected[:, 2 * WIDE :] + bias_ref[:, pl.ds(at + INNER, WIDE)]
    projected_ref[0, :KEYS, 2 * WIDE :] = values.astype(bf16)
    projected_ref[0, KEYS:] = jnp.zeros((ROWS - KEYS, QKV), bf16)
    from_ref = projected_ref.at[0]

    lane = lax.broadcasted_iota(jnp.int32, (1, 128), 1)
    row = lax.broadcasted_iota(jnp.int32, (128, 1), 0)
    units = [(h, b) for h in range(GROUP) for b in QUERY_BLOCKS]

    largest = {}
    flipped = {}

    def scores(unit):
        head, (start, width, keys) = units[unit]
        pair = head // 2 * 128
        mine = (lane < 64) if head % 2 == 0 else (lane >= 64)
        own_keys = from_ref[:keys, WIDE + pair : WIDE + pair + 128]
        own_keys = jnp.where(mine, own_keys, bf16(0))
        score = dot(own_keys, from_ref[start : start + width, pair : pair + 128], NT)
        score = score + hide_scr[seq, :keys, start : start + width]
        score_scr[unit % 2, :keys, :width] = score
        top = jnp.max(score.reshape(-1, 8, width), axis=0)
        largest[unit] = jnp.max(top, axis=0, keepdims=True)

    def exponents(unit):
        head, (start, width, keys) = units[unit]
        exponent = jnp.exp(score_scr[unit % 2, :keys, :width] - largest[unit])
        exp_ref[0, head, :keys, start : start + width] = exponent.astype(bf16)

    def mix(unit):
        head, (start, width, keys) = units[unit]
        pair = head // 2 * 128
        if head not in flipped:
            turned = from_ref[:KEYS, 2 * WIDE + pair : 2 * WIDE + pair + 128].T
            mine = (row < 64) if head % 2 == 0 else (row >= 64)
            flipped[head] = jnp.where(mine, turned, bf16(1))
        exponent = exp_ref[0, head, :keys, start : start + width]
        summed = dot(flipped[head][:, :keys], exponent, NN)
        if head % 2 == 0:
            values, total = summed[:64], summed[64:65]
        else:
            values, total = summed[64:], summed[0:1]
        inverse = 1.0 / total
        mixed_scr[head * 64 : (head + 1) * 64, start : start + width] = values * inverse
        total_scr[head : head + 1, start : start + width] = inverse

    count = len(units)
    scores(0)
    for unit in range(count + 1):
        if unit + 1 < count:
            scores(unit + 1)
        if unit < count:
            exponents(unit)
        if unit > 0:
            mix(unit - 1)
    mixed_ref[0] = mixed_scr[...].T.astype(bf16)
    inverse_ref[0, 0] = total_scr[...]


def attend(me, normed, parts, bias, mask):
    seqs = normed.shape[0]
    return pl.pallas_call(
        functools.partial(attend_kernel, len(parts)),
        grid=(GROUPS, seqs),
        in_specs=[
            pl.BlockSpec(memory_space=pltpu.SMEM),
            whole(normed.shape),
            whole(bias.shape),
            whole(mask.shape),
        ]
        + [whole(part.shape) for part in parts],
        out_specs=[
            pl.BlockSpec((1, ROWS, QKV), lambda g, s: (s, 0, g)),
            pl.BlockSpec((1, ROWS, WIDE), lambda g, s: (s, 0, g)),
            pl.BlockSpec((1, GROUP, KEYS, ROWS), lambda g, s: (s, g, 0, 0)),
            pl.BlockSpec((1, 1, 8, ROWS), lambda g, s: (s, g, 0, 0)),
            whole((D, GROUPS * QKV)),
        ],
        out_shape=[
            pltpu.HBM((seqs, ROWS, GROUPS * QKV), bf16),
            pltpu.HBM((seqs, ROWS, INNER), bf16),
            pltpu.HBM((seqs, HEADS, KEYS, ROWS), bf16),
            pltpu.HBM((seqs, GROUPS, 8, ROWS), f32),
            pltpu.HBM((D, GROUPS * QKV), bf16),
        ],
        scratch_shapes=[
            pltpu.VMEM((seqs, KEYS, ROWS), f32),
            pltpu.VMEM((2, KEYS, 256), f32),
            pltpu.VMEM((WIDE, ROWS), f32),
            pltpu.VMEM((8, ROWS), f32),
            pltpu.VMEM((8, ROWS), f32),
        ],
        compiler_params=pltpu.CompilerParams(vmem_limit_bytes=24 * 1024 * 1024),
        cost_estimate=cost(22),
        name="attend",
    )(me, normed, bias, mask, *parts)


def forward_kernel(pieces, n_bias, chunk, me_ref, tokens_ref, grad_ref, rows_ref, *refs):
    bias_refs, refs = refs[:n_bias], refs[n_bias:]
    mixed_ref, refs = refs[0], refs[1:]
    parts, refs = refs[:pieces], refs[pieces:]
    out_ref, middle_grad_ref, branch_ref, out_wide_ref = refs[:4]
    n_out = 2 if pieces > 1 else 1
    send_refs, refs = refs[4 : 4 + n_out], refs[4 + n_out :]
    one_scr, two_scr, middle_scr, scaled_scr, inverse_scr, second_scr, second_t, grad_scr = refs[:8]
    grad_t, total_scr, back_scr, weight_scr, small_scr, bias_scr = refs[8:14]
    stage_scrs = (refs[14:16], refs[16:18])
    seqs = branch_ref.shape[0]
    step = pl.program_id(0)
    rows = D // pieces
    per_slot = FF // 4
    ones = jnp.ones((16, seqs * KEYS), bf16)

    def send(value_ref, at, width, left):
        if pieces == 1:
            send_refs[0][0, :, left : left + width] = value_ref[:, at : at + width].astype(bf16)
            return
        for j, owner in enumerate(owners(me_ref[0], pieces)):
            first = pl.multiple_of(owner * rows, 16)
            send_refs[j // 4][j % 4, 0, :, left : left + width] = value_ref[
                pl.ds(first, rows), at : at + width
            ].astype(bf16)

    def send_vectors():
        vectors = small_scr[...].astype(bf16)
        if pieces == 1:
            send_refs[0][0, :48, INNER:] = vectors
        else:
            for j in range(pieces):
                send_refs[j // 4][j % 4, 0, :, INNER:] = vectors

    def produce(index, stage):
        act_scr, pre_scr = stage_scrs[stage]
        hidden = pl.ds(pl.multiple_of(index * chunk, 128), chunk)
        pre = dot(second_scr[...], one_scr[:, hidden], NN) + bias_scr[:, hidden]
        half = 0.5 + 0.5 * lax.erf(pre * (0.5**0.5))
        act_scr[...] = (pre * half).astype(bf16)
        slope = half + pre * (jnp.exp2(pre * pre * -0.7213475204444817) * 0.3989422804014327)
        grad_act = dot(grad_scr[...], two_scr[:, hidden], NN)
        pre_scr[...] = (grad_act * slope).astype(bf16)

    def consume(index, stage):
        act_scr, pre_scr = stage_scrs[stage]
        hidden = pl.ds(pl.multiple_of(index * chunk, 128), chunk)
        total_scr[...] += dot(act_scr[...], two_scr[:, hidden], NT)
        back_scr[...] += dot(pre_scr[...], one_scr[:, hidden], NT)
        left = stage * chunk
        weight_scr[:, :chunk] = dot(second_t[...], pre_scr[...], NN)
        send(weight_scr, 0, chunk, left)
        weight_scr[:, chunk : 2 * chunk] = dot(grad_t[...], act_scr[...], NN)
        send(weight_scr, chunk, chunk, left + per_slot)
        hidden_sum = dot(ones, pre_scr[...], NN)[0:1]
        for r in range(chunk // 128):
            at = stage * (chunk // 128) + r
            small_scr[at : at + 1] = hidden_sum[:, r * 128 : (r + 1) * 128]

    @pl.when(step == 0)
    def _():
        for j, owner in enumerate(owners(me_ref[0], pieces)):
            first = pl.multiple_of(owner * rows, 16)
            if pieces == 1:
                out_wide_ref[...] = parts[0][:, :INNER]
            else:
                to = pl.ds(pl.multiple_of(owner * 128, 128), 128)
                for r in range(pieces):
                    out_wide_ref[r * rows : (r + 1) * rows, to] = parts[j][
                        :, r * 128 : (r + 1) * 128
                    ]
            for z in range(4):
                left = INNER + 2 * per_slot * z
                slot = slice(z * per_slot, (z + 1) * per_slot)
                one_scr[pl.ds(first, rows), slot] = parts[j][:, left : left + per_slot]
                two_scr[pl.ds(first, rows), slot] = parts[j][
                    :, left + per_slot : left + 2 * per_slot
                ]
        if n_bias == 1:
            bias_scr[...] = bias_refs[0][...].astype(f32)
        else:
            for z in range(4):
                row = bias_refs[z][rows : rows + 1, :per_slot]
                bias_scr[:, z * per_slot : (z + 1) * per_slot] = row.astype(f32)
        for s in range(seqs):
            block = slice(s * KEYS, (s + 1) * KEYS)
            real = slice(s * KEYS, s * KEYS + LEN)
            spare = slice(s * KEYS + LEN, (s + 1) * KEYS)
            given = slice(s * LEN, (s + 1) * LEN)
            grad_scr[real] = grad_ref[given]
            grad_scr[spare] = jnp.zeros((KEYS - LEN, D), bf16)
            middle_scr[real] = tokens_ref[given].astype(f32) + rows_ref[BIAS_OUT]
            middle_scr[spare] = jnp.zeros((KEYS - LEN, D), f32)
            middle = middle_scr[block] + dot(mixed_ref[s, :KEYS], out_wide_ref[...], NT)
            middle_scr[block] = middle
            scaled, inverse = normalize(middle)
            scaled_scr[block] = scaled
            inverse_scr[block] = inverse
            second_scr[block] = (scaled * rows_ref[GAIN_TWO] + rows_ref[SHIFT_TWO]).astype(bf16)
        second_t[...] = second_scr[...].T
        grad_t[...] = grad_scr[...].T
        total_scr[...] = jnp.zeros_like(total_scr)
        back_scr[...] = jnp.zeros_like(back_scr)
        small_scr[...] = jnp.zeros_like(small_scr)
        produce(0, 0)

    @pl.when(step < 4)
    def _():
        produce(2 * step + 1, 1)
        consume(2 * step, 0)
        produce(jnp.minimum(2 * step + 2, FF // chunk - 1), 0)
        consume(2 * step + 1, 1)
        send_vectors()

    @pl.when(step == 4)
    def _():
        sums = [jnp.zeros((1, D), f32) for _ in range(2)]
        for s in range(seqs):
            block = slice(s * KEYS, (s + 1) * KEYS)
            given = slice(s * LEN, (s + 1) * LEN)
            output = (middle_scr[block] + total_scr[block] + rows_ref[BIAS_TWO]).astype(bf16)
            out_ref[given] = output[:LEN]
            scaled, inverse = scaled_scr[block], inverse_scr[block]
            grad_second = back_scr[block]
            grad_middle = grad_scr[block].astype(f32) + normalize_back(
                grad_second, rows_ref[GAIN_TWO], scaled, inverse
            )
            middle_grad_ref[s, :KEYS] = grad_middle
            branch_ref[s, :KEYS] = grad_middle.astype(bf16)
            branch_ref[s, KEYS:] = jnp.zeros((ROWS - KEYS, D), bf16)
            for k, term in enumerate((grad_second * scaled, grad_second)):
                sums[k] = sums[k] + jnp.sum(term, axis=0, keepdims=True)
        branch = jnp.concatenate([branch_ref[s, :KEYS] for s in range(seqs)], axis=0)
        sums.append(dot(ones, branch, NN)[0:1])
        sums.append(dot(ones, grad_scr[...], NN)[0:1])
        for k in range(4):
            for r in range(D // 128):
                at = 3 * k + r
                small_scr[at : at + 1] = sums[k][:, r * 128 : (r + 1) * 128]
        mixed = jnp.concatenate([mixed_ref[s, :KEYS] for s in range(seqs)], axis=0)
        weight_scr[...] = dot(branch, mixed, TN)
        if pieces == 1:
            send_refs[0][0, :, :INNER] = weight_scr[...].astype(bf16)
        else:
            for j, owner in enumerate(owners(me_ref[0], pieces)):
                to = pl.ds(pl.multiple_of(owner * 128, 128), 128)
                for r in range(pieces):
                    send_refs[j // 4][j % 4, 0, :, r * 128 : (r + 1) * 128] = weight_scr[
                        r * rows : (r + 1) * rows, to
                    ].astype(bf16)
        send_vectors()


def forward(me, tokens, cotangent, rows_in, biases, mixed, parts):
    seqs = tokens.shape[0] // LEN
    pieces = len(parts)
    chunk = 256
    if pieces > 1:
        send_shapes = [(pieces // 2, 5, D // pieces, BLOCK)] * 2
        send_specs = [pl.BlockSpec((pieces // 2, 1, D // pieces, BLOCK), lambda c: (0, c, 0, 0))] * 2
    else:
        send_shapes = [(5, D, BLOCK)]
        send_specs = [pl.BlockSpec((1, D, BLOCK), lambda c: (c, 0, 0))]
    rows3 = (seqs, ROWS, D)
    rows2 = (seqs * KEYS, D)
    mixed = pltpu.with_memory_space_constraint(mixed, pltpu.HBM)
    return pl.pallas_call(
        functools.partial(forward_kernel, pieces, len(biases), chunk),
        grid=(5,),
        in_specs=[
            pl.BlockSpec(memory_space=pltpu.SMEM),
            whole(tokens.shape),
            whole(tokens.shape),
            whole((8, D)),
        ]
        + [whole(b.shape) for b in biases]
        + [whole(mixed.shape)]
        + [whole(p.shape) for p in parts],
        out_specs=[whole(tokens.shape), whole(rows3), whole(rows3), whole((D, INNER))]
        + send_specs,
        out_shape=[
            jax.ShapeDtypeStruct(tokens.shape, bf16),
            jax.ShapeDtypeStruct(rows3, f32),
            jax.ShapeDtypeStruct(rows3, bf16),
            jax.ShapeDtypeStruct((D, INNER), bf16),
        ]
        + [jax.ShapeDtypeStruct(s, bf16) for s in send_shapes],
        scratch_shapes=[
            pltpu.VMEM((D, FF), bf16),
            pltpu.VMEM((D, FF), bf16),
            pltpu.VMEM(rows2, f32),
            pltpu.VMEM(rows2, f32),
            pltpu.VMEM((seqs * KEYS, 1), f32),
            pltpu.VMEM(rows2, bf16),
            pltpu.VMEM((D, seqs * KEYS), bf16),
            pltpu.VMEM(rows2, bf16),
            pltpu.VMEM((D, seqs * KEYS), bf16),
            pltpu.VMEM(rows2, f32),
            pltpu.VMEM(rows2, f32),
            pltpu.VMEM((D, INNER), f32),
            pltpu.VMEM((48, 128), f32),
            pltpu.VMEM((1, FF), f32),
        ]
        + [pltpu.VMEM((seqs * KEYS, chunk), bf16)] * 4,
        compiler_params=pltpu.CompilerParams(vmem_limit_bytes=36 * 1024 * 1024),
        cost_estimate=cost(30),
        name="forward",
    )(me, tokens, cotangent, rows_in, *biases, mixed, *parts)


def mixed_gradient_kernel(branch_ref, out_wide_ref, mixed_ref, grad_ref, delta_ref):
    lane = lax.broadcasted_iota(jnp.int32, (8, WIDE), 1)
    gather = (lane >> 6 == lax.broadcasted_iota(jnp.int32, (8, WIDE), 0)).astype(bf16)
    for g in range(delta_ref.shape[1]):
        columns = slice(g * WIDE, (g + 1) * WIDE)
        grad = dot(branch_ref[0], out_wide_ref[:, columns], NN).astype(bf16)
        grad_ref[0, :, columns] = grad
        product = grad.astype(f32) * mixed_ref[0, :, columns].astype(f32)
        first = product.astype(bf16)
        second = (product - first.astype(f32)).astype(bf16)
        delta_ref[0, g] = dot(gather, first, NT) + dot(gather, second, NT)


def mixed_gradient(branch, out_wide, mixed):
    seqs = branch.shape[0]
    each = 2
    columns = pl.BlockSpec((1, ROWS, each * WIDE), lambda s, g: (s, 0, g))
    return pl.pallas_call(
        mixed_gradient_kernel,
        grid=(seqs, GROUPS // each),
        in_specs=[
            pl.BlockSpec((1, ROWS, D), lambda s, g: (s, 0, 0)),
            pl.BlockSpec((D, each * WIDE), lambda s, g: (0, g)),
            columns,
        ],
        out_specs=[columns, pl.BlockSpec((1, each, 8, ROWS), lambda s, g: (s, g, 0, 0))],
        out_shape=[
            pltpu.HBM((seqs, ROWS, INNER), bf16),
            pltpu.HBM((seqs, GROUPS, 8, ROWS), f32),
        ],
        compiler_params=pltpu.CompilerParams(vmem_limit_bytes=16 * 1024 * 1024),
        cost_estimate=cost(5),
        name="mixed_gradient",
    )(branch, out_wide, mixed)


def backward_kernel(pieces, me_ref, *refs):
    grad_ref, delta_ref, scaled_ref, projected_ref, exp_ref, inverse_ref = refs[:6]
    wide_ref, norm_ref = refs[6:8]
    refs = refs[8:]
    n_out = 2 if pieces > 1 else 1
    back_ref = refs[0]
    send_refs = refs[1 : 1 + n_out]
    grad_scr, prob_scr, turned_scr, weight_scr, small_scr, sum_scr, norm_scr = refs[1 + n_out :]
    group, seq = pl.program_id(0), pl.program_id(1)
    groups, seqs = pl.num_programs(0), pl.num_programs(1)
    rows = D // pieces

    @pl.when((group == 0) & (seq == 0))
    def _():
        small_scr[...] = jnp.zeros_like(small_scr)
        norm_scr[...] = jnp.zeros_like(norm_scr)

    lane = lax.broadcasted_iota(jnp.int32, (1, 128), 1)
    low = lane < 64
    kept = {}
    for pair in range(GROUP // 2):
        columns = slice(pair * 128, pair * 128 + 128)
        grad = grad_ref[0, :, columns]
        query = projected_ref[0, :, columns]
        value = projected_ref[0, :KEYS, 2 * WIDE + pair * 128 : 2 * WIDE + pair * 128 + 128]
        turned = projected_ref[0, :KEYS, WIDE + pair * 128 : WIDE + pair * 128 + 128].T
        for half in range(2):
            head = 2 * pair + half
            mine = low if half == 0 else jnp.logical_not(low)
            own_value = jnp.where(mine, value, bf16(0))
            inverse = inverse_ref[0, 0, head : head + 1].astype(bf16)
            delta = delta_ref[0, 0, head : head + 1]
            side = slice(64 * half, 64 * half + 64)
            for start, width, keys in QUERY_BLOCKS:
                block = slice(start, start + width)
                change = dot(own_value[:keys], grad[block], NT) - delta[:, block]
                probability = exp_ref[0, head, :keys, block] * inverse[:, block]
                prob_scr[half, :keys, block] = probability
                grad_scr[half, :keys, block] = probability * change.astype(bf16)
            for start, width, keys in QUERY_BLOCKS:
                block = slice(start, start + width)
                turned_scr[head * 64 : (head + 1) * 64, block] = dot(
                    turned[side, :keys], grad_scr[half, :keys, block], NN
                ) * (HEAD_DIM**-0.5)
            for start, stop, seen in KEY_RANGES:
                value_grad = dot(prob_scr[half, start:stop, seen:], grad[seen:], NN)
                key_grad = dot(grad_scr[half, start:stop, seen:], query[seen:], NN)
                if half == 0:
                    kept[start] = (value_grad, key_grad)
                else:
                    at = slice(WIDE + pair * 128, WIDE + pair * 128 + 128)
                    back_ref[0, start:stop, at] = jnp.where(low, kept[start][1], key_grad).astype(
                        bf16
                    )
                    at = slice(2 * WIDE + pair * 128, 2 * WIDE + pair * 128 + 128)
                    back_ref[0, start:stop, at] = jnp.where(low, kept[start][0], value_grad).astype(
                        bf16
                    )
    back_ref[0, :KEYS, :WIDE] = turned_scr[...].T[:KEYS].astype(bf16)

    back = back_ref[0, :KEYS]
    weight = dot(scaled_ref[0, :KEYS], back, TN)
    total = dot(jnp.ones((16, KEYS), bf16), back, NN)[0:1]

    @pl.when(seq == 0)
    def _():
        weight_scr[...] = weight
        sum_scr[0:1] = total

    @pl.when(seq > 0)
    def _():
        weight_scr[...] += weight
        sum_scr[0:1] += total

    @pl.when(seq == seqs - 1)
    def _():
        sums = sum_scr[0:1]
        for r in range(WIDE // 128):
            at = group * (2 * WIDE // 128) + r
            small_scr[pl.ds(at, 1)] = sums[:, r * 128 : r * 128 + 128]
            at = at + WIDE // 128
            small_scr[pl.ds(at, 1)] = sums[:, 2 * WIDE + r * 128 : 2 * WIDE + r * 128 + 128]
        wide = wide_ref[...].astype(f32)
        scaled_weight = weight_scr[...]
        norm_scr[:, 0:1] += jnp.sum(scaled_weight * wide, axis=1, keepdims=True)
        norm_scr[:, 1:2] += jnp.sum(sums * wide, axis=1, keepdims=True)
        weight_scr[...] = scaled_weight * norm_ref[:, GAIN_ONE] + sums * norm_ref[:, SHIFT_ONE]
        start = pl.multiple_of(group * QKV, 128)
        if pieces == 1:
            send_refs[0][:, pl.ds(start, QKV)] = weight_scr[...].astype(bf16)
        else:
            for j, owner in enumerate(owners(me_ref[0], pieces)):
                first = pl.multiple_of(owner * rows, 16)
                send_refs[j // 4][j % 4, :, pl.ds(start, QKV)] = weight_scr[
                    pl.ds(first, rows)
                ].astype(bf16)

    @pl.when((group == groups - 1) & (seq == seqs - 1))
    def _():
        turned = norm_scr[...].T
        for k in range(2):
            for r in range(D // 128):
                small_scr[40 + 3 * k + r : 41 + 3 * k + r] = turned[
                    k : k + 1, r * 128 : (r + 1) * 128
                ]
        small = small_scr[...].astype(bf16)
        if pieces == 1:
            send_refs[0][:48, send_refs[0].shape[1] - SMALL :] = small
        else:
            for j in range(pieces):
                edge = send_refs[0].shape[2] - SMALL
                send_refs[j // 4][j % 4, :, edge:] = small


def backward(me, pieces, first_group, groups, grads, scaled, norm, saved):
    operands = [
        pltpu.with_memory_space_constraint(x, pltpu.HBM)
        for x in (*grads, scaled, saved[0], saved[2], saved[3], saved[4])
    ]
    seqs = scaled.shape[0]
    width = groups * QKV + SMALL
    if pieces > 1:
        send_shapes = [(pieces // 2, D // pieces, width)] * 2
    else:
        send_shapes = [(D, width)]
    columns = pl.BlockSpec((1, ROWS, WIDE), lambda g, s: (s, 0, g + first_group))
    heads = pl.BlockSpec((1, 1, 8, ROWS), lambda g, s: (s, g + first_group, 0, 0))
    rows_block = pl.BlockSpec((1, ROWS, D), lambda g, s: (s, 0, 0))
    return pl.pallas_call(
        functools.partial(backward_kernel, pieces),
        grid=(groups, seqs),
        in_specs=[
            pl.BlockSpec(memory_space=pltpu.SMEM),
            columns,
            heads,
            rows_block,
            pl.BlockSpec((1, ROWS, QKV), lambda g, s: (s, 0, g + first_group)),
            pl.BlockSpec((1, GROUP, KEYS, ROWS), lambda g, s: (s, g + first_group, 0, 0)),
            heads,
            pl.BlockSpec((D, QKV), lambda g, s: (0, g + first_group)),
            whole((D, 8)),
        ],
        out_specs=[pl.BlockSpec((1, ROWS, QKV), lambda g, s: (s, 0, g))]
        + [whole(s) for s in send_shapes],
        out_shape=[jax.ShapeDtypeStruct((seqs, ROWS, groups * QKV), bf16)]
        + [jax.ShapeDtypeStruct(s, bf16) for s in send_shapes],
        scratch_shapes=[
            pltpu.VMEM((2, KEYS, ROWS), bf16),
            pltpu.VMEM((2, KEYS, ROWS), bf16),
            pltpu.VMEM((WIDE, ROWS), f32),
            pltpu.VMEM((D, QKV), f32),
            pltpu.VMEM((48, 128), f32),
            pltpu.VMEM((8, QKV), f32),
            pltpu.VMEM((D, 128), f32),
        ],
        compiler_params=pltpu.CompilerParams(vmem_limit_bytes=20 * 1024 * 1024),
        cost_estimate=cost(11 * groups),
        name="backward",
    )(me, *operands, norm)


def input_kernel(tokens_ref, middle_grad_ref, rows_ref, early_ref, late_ref, wide_ref, out_ref, sum_scr):
    step, last = pl.program_id(0), pl.num_programs(0) - 1
    seqs = middle_grad_ref.shape[0]

    @pl.when(step < last)
    def _():
        for s in range(seqs):
            grad = dot(early_ref[s, :KEYS], wide_ref[...], NT)
            sum_scr[s] = jnp.where(step == 0, grad, sum_scr[s] + grad)

    @pl.when(step == last)
    def _():
        for s in range(seqs):
            grad_first = sum_scr[s] + dot(late_ref[s, :KEYS], wide_ref[...], NT)
            given = slice(s * LEN, (s + 1) * LEN)
            scaled, inverse = normalize(tokens_ref[given].astype(f32))
            out_ref[given] = middle_grad_ref[s, :LEN] + normalize_back(
                grad_first[:LEN], rows_ref[GAIN_ONE], scaled, inverse
            )


def input_gradient(tokens, middle_grad, rows_in, early, late, weights):
    seqs = middle_grad.shape[0]
    block = (seqs, ROWS, QKV)
    return pl.pallas_call(
        input_kernel,
        grid=(GROUPS,),
        in_specs=[
            whole(tokens.shape),
            whole(middle_grad.shape),
            whole(rows_in.shape),
            pl.BlockSpec(block, lambda g: (0, 0, jnp.minimum(g, GROUPS - 2))),
            whole(block),
            pl.BlockSpec((D, QKV), lambda g: (0, g)),
        ],
        out_specs=whole(tokens.shape),
        out_shape=jax.ShapeDtypeStruct(tokens.shape, f32),
        scratch_shapes=[pltpu.VMEM((seqs, KEYS, D), f32)],
        compiler_params=pltpu.CompilerParams(vmem_limit_bytes=16 * 1024 * 1024),
        cost_estimate=cost(8),
        name="input_gradient",
    )(tokens, middle_grad, rows_in, early, late, weights)


def swap(values, mask):
    size = lax.axis_size("tok")
    return lax.ppermute(values, "tok", [(i, i ^ mask) for i in range(size)])


def swap_half_line(values, stage):
    tok, mlp = lax.axis_size("tok"), lax.axis_size("mlp")
    pairs = []
    for t in range(tok):
        for z in range(mlp):
            far = (t % 2 == 0) == (stage == 0)
            pairs.append((t * mlp + z, t * mlp + (z ^ (2 if far else 1))))
    return lax.ppermute(values.astype(bf16), ("tok", "mlp"), pairs)


def after(values, *earlier):
    return lax.optimization_barrier((values,) + earlier)


def wide(values):
    return values.astype(f32)


def join(kept, arrived):
    return (wide(kept) + wide(arrived)).astype(bf16)


def body(
    tokens,
    action_mask,
    ln1_gain,
    ln1_bias,
    w_qkv,
    bias_qv,
    w_out,
    bias_out,
    ln2_gain,
    ln2_bias,
    w_fc1,
    bias_fc1,
    w_fc2,
    bias_fc2,
    out_grad,
):
    rows = w_qkv.shape[0]
    tok = lax.axis_size("tok")
    mlp = lax.axis_size("mlp")
    slot = w_fc1.shape[1]
    fast = tok == 8 and mlp == 4
    pieces = tok if fast else 1
    me = lax.axis_index("tok").astype(jnp.int32).reshape(1)
    chips = (2, 4, 6)
    odd = (me[0] & 1) == 1

    def pick(if_odd, if_even):
        return jnp.where(odd, if_odd, if_even)


    vectors = (bias_out, ln2_gain, ln2_bias, bias_fc2, ln1_gain, ln1_bias)
    me_a = me
    if fast:
        first_near = [swap(w_qkv, mask) for mask in chips]
        first_other = swap(w_qkv, 1)
        hidden_pack, out_block, rows_in, columns_in, bias_pair = prepare(
            w_fc1, w_fc2, bias_fc1, w_out, bias_qv, vectors
        )
        line = jnp.stack([hidden_pack, swap_half_line(hidden_pack, 0)])
        line = jnp.concatenate([line, swap_half_line(line, 1)])
        line = [line[0], pick(line[1], line[2]), pick(line[2], line[1]), line[3]]
        norm_tokens, first_near[0] = after(tokens, first_near[0])
        normed, scaled = first_norm(norm_tokens, rows_in)
        first_parts = [w_qkv] + first_near + [first_other] + [swap(p, 1) for p in first_near]
        hidden_own = jnp.concatenate([out_block] + [part[:rows] for part in line], axis=1)
        me_a, hidden_own = after(me, hidden_own)
        hidden_near = [swap(hidden_own, mask) for mask in chips + (1,)]
        biases = line
    else:
        rows_in = jnp.pad(wide(jnp.stack(vectors)), ((0, 2), (0, 0)))
        columns_in = rows_in.T
        bias_pair = wide(bias_qv).reshape(1, -1)
        normed, scaled = first_norm(tokens, rows_in)
        first_parts = [lax.all_gather(w_qkv, "tok", axis=0, tiled=True)]
        line = lax.all_gather(jnp.concatenate([w_fc1, w_fc2.T], axis=1), "mlp", axis=1, tiled=True)
        line = lax.all_gather(line, "tok", axis=0, tiled=True)
        biases = [lax.all_gather(bias_fc1, "mlp", axis=0, tiled=True).reshape(1, -1)]
        out_all = lax.all_gather(w_out, "tok", axis=0, tiled=True).T
        hidden_parts = [jnp.concatenate([out_all, line], axis=1)]

    saved = list(attend(me_a, normed, first_parts, bias_pair, action_mask))
    weights = saved[4]
    if fast:
        saved[1], *hidden_near = after(saved[1], *hidden_near)
        hidden_other = hidden_near.pop()
        hidden_parts = [hidden_own] + hidden_near + [hidden_other]
        hidden_parts = hidden_parts + [swap(part, 1) for part in hidden_near]

    output, middle_grad, branch, out_wide, *hidden_sends = forward(
        me, tokens, out_grad, rows_in, biases, saved[1], hidden_parts
    )

    grads = list(mixed_gradient(branch, out_wide, saved[1]))

    def back(me, group, count):
        return backward(me, pieces, group, count, grads, scaled, columns_in, saved)

    if not fast:
        back_a, sends_a = back(me, 0, 3)
        back_b, sends_b = back(me, 3, 1)
        input_grad = input_gradient(tokens, middle_grad, rows_in, back_a, back_b, weights)
        return slow_end(output, input_grad, hidden_sends[0], (sends_a, sends_b), slot)

    arrived = swap(hidden_sends[1], 1)
    grads[0], arrived = after(grads[0], arrived)
    hidden = join(hidden_sends[0], arrived)
    me_1, hidden = after(me, hidden)
    near = [swap(hidden[k], chips[k - 1]) for k in (1, 2, 3)]
    back_a, *sends_a = back(me_1, 0, 3)

    back_a, *near = after(back_a, *near)
    hidden = wide(hidden[0]) + wide(near[0]) + wide(near[1]) + wide(near[2])
    sent = jnp.stack([pick(hidden[1], hidden[2]), hidden[3], hidden[4]]).astype(bf16)
    group_a = join(sends_a[0], swap(sends_a[1], 1))
    me_2, group_a, sent = after(me, group_a, sent)
    line_1 = swap_half_line(sent, 0)
    near_a = [swap(group_a[k], chips[k - 1]) for k in (1, 2, 3)]
    back_b, *sends_b = back(me_2, 3, 1)

    back_b, line_1, *near_a = after(back_b, line_1, *near_a)
    total_a = wide(group_a[0]) + wide(near_a[0]) + wide(near_a[1]) + wide(near_a[2])
    block = hidden[0] + wide(line_1[0])
    middle_block = pick(hidden[2], hidden[1]) + wide(line_1[1])
    rest = hidden[4] + wide(line_1[2])
    sent = jnp.concatenate([middle_block, rest, total_a], axis=1).astype(bf16)
    sent, kept_b, sent_b = after(sent, *sends_b)
    line_2 = swap_half_line(sent, 1)
    group_b = join(kept_b, swap(sent_b, 1))
    near_b = [swap(group_b[k], chips[k - 1]) for k in (1, 2, 3)]
    block = block + wide(line_2[:, :BLOCK])
    rest = rest + wide(line_2[:, BLOCK : 2 * BLOCK])
    total_a = total_a + wide(line_2[:, 2 * BLOCK :])
    total_b = wide(group_b[0]) + wide(near_b[0]) + wide(near_b[1]) + wide(near_b[2])
    edge = total_a.shape[1]
    sent = jnp.concatenate([total_a, total_b], axis=1).astype(bf16)
    middle_grad, sent, block, rest = after(middle_grad, sent, block, rest)
    line_3 = swap_half_line(sent, 0)
    input_grad = input_gradient(tokens, middle_grad, rows_in, back_a, back_b, weights)

    input_grad, line_3 = after(input_grad, line_3)
    total_a = total_a + wide(line_3[:, :edge])
    total_b = total_b + wide(line_3[:, edge:])
    total_b = total_b + wide(swap_half_line(total_b, 1))

    out_rows = rest[:, :INNER].reshape(rows, tok, -1).transpose(1, 0, 2).reshape(D, -1).T
    return results(
        output,
        input_grad,
        [total_a[:, :-SMALL], total_b[:, :-SMALL]],
        [total_a[:, -SMALL:], total_b[:, -SMALL:]],
        out_rows,
        rest[:, INNER:],
        block[:, :INNER],
        block[: slot // 128, INNER:],
    )


def slow_end(output, input_grad, hidden, sends, slot):
    def scatter(values):
        values = lax.psum_scatter(wide(values), "tok", scatter_dimension=0, tiled=True)
        return lax.psum(values, "mlp")

    hidden = wide(hidden)
    blocks = jnp.concatenate([hidden[k, :, :INNER] for k in range(4)], axis=1)
    blocks = lax.psum_scatter(blocks, "tok", scatter_dimension=0, tiled=True)
    hidden_sum = lax.psum_scatter(blocks, "mlp", scatter_dimension=1, tiled=True)
    out_rows = scatter(hidden[4, :, :INNER].T)
    lines = slot // 128
    small = lax.psum(hidden[:, :48, INNER:], ("tok", "mlp"))
    bias_sum = lax.dynamic_index_in_dim(small[:4, :lines], lax.axis_index("mlp"), 0, False)
    small = small[4]
    weights = [scatter(s[:, :-SMALL]) for s in sends]
    smalls = [lax.psum(wide(s[:48, -SMALL:]), ("tok", "mlp")) for s in sends]
    return results(output, input_grad, weights, smalls, out_rows, small, hidden_sum, bias_sum)


def results(output, input_grad, weights, smalls, out_rows, small, hidden_sum, bias_sum):
    blocks = []
    for part in weights:
        blocks += [part[:, at : at + WIDE] for at in range(0, part.shape[1], WIDE)]
    qkv_grad = jnp.concatenate([block for k in range(3) for block in blocks[k::3]], axis=1)
    lines = WIDE // 128
    biases = []
    for part, weight in zip(smalls, weights):
        count = 2 * (weight.shape[1] // QKV)
        biases += [part[k * lines : (k + 1) * lines] for k in range(count)]
    bias_grad = jnp.concatenate(biases[0::2] + biases[1::2], axis=0).reshape(-1)
    norm_grad = smalls[0][40:46] + smalls[1][40:46]
    vectors = [small[3 * k : 3 * k + 3].reshape(-1) for k in range(4)]
    slot = hidden_sum.shape[1] // 2
    return (
        output,
        input_grad,
        norm_grad[:3].reshape(-1),
        norm_grad[3:].reshape(-1),
        qkv_grad,
        bias_grad,
        out_rows,
        vectors[2],
        vectors[0],
        vectors[1],
        hidden_sum[:, :slot],
        bias_sum.reshape(-1),
        hidden_sum[:, slot:].T,
        vectors[3],
    )


def solution(mesh):
    placed = (
        P(("tok", "mlp"), None),
        P(("tok", "mlp"), None),
        P(),
        P(),
        P("tok", None),
        P(),
        P("tok", None),
        P(),
        P(),
        P(),
        P("tok", "mlp"),
        P("mlp"),
        P("mlp", "tok"),
        P(),
        P(("tok", "mlp"), None),
    )
    return jax.shard_map(
        body,
        mesh=mesh,
        in_specs=placed,
        out_specs=(
            P(("tok", "mlp"), None),
            P(("tok", "mlp"), None),
            P(),
            P(),
            P("tok", None),
            P(),
            P("tok", None),
            P(),
            P(),
            P(),
            P("tok", "mlp"),
            P("mlp"),
            P("mlp", "tok"),
            P(),
        ),
        check_vma=False,
    )
```

```python
import functools

import jax
import jax.numpy as jnp
from jax import lax
from jax.experimental import pallas as pl
from jax.experimental.pallas import tpu as pltpu
from jax.sharding import PartitionSpec as P

HEADS = 16
HEAD_DIM = 64
FRAME_LEN = 196
LEN = 588
D = 384
FF = 2048
INNER = HEADS * HEAD_DIM
KEYS = 592
ROWS = 640
GROUP = 4
WIDE = GROUP * HEAD_DIM
GROUPS = HEADS // GROUP
QKV = 3 * WIDE
SMALL = 128
BLOCK = INNER + SMALL

epsilon = 1e-06
f32 = jnp.float32
bf16 = jnp.bfloat16

NN = (((1,), (0,)), ((), ()))
NT = (((1,), (1,)), ((), ()))
TN = (((0,), (0,)), ((), ()))

QUERY_BLOCKS = ((0, 128, 208), (128, 256, 400), (384, 256, 592))
KEY_RANGES = ((0, 208, 0), (208, 400, 128), (400, 592, 384))

VMEM = 56 * 1024 * 1024

BIAS_OUT, GAIN_TWO, SHIFT_TWO, BIAS_TWO, GAIN_ONE, SHIFT_ONE = (slice(k, k + 1) for k in range(6))


def dot(left, right, dims):
    return lax.dot_general(left, right, dims, preferred_element_type=f32)


def normalize(values):
    center = values - jnp.mean(values, axis=-1, keepdims=True)
    inverse = lax.rsqrt(jnp.mean(center * center, axis=-1, keepdims=True) + epsilon)
    return center * inverse, inverse


def normalize_back(grad_rows, norm_gain, scaled, inverse):
    scaled_grad = grad_rows * norm_gain
    return inverse * (
        scaled_grad
        - jnp.mean(scaled_grad, axis=-1, keepdims=True)
        - scaled * jnp.mean(scaled_grad * scaled, axis=-1, keepdims=True)
    )


def cost(micros):
    return pl.CostEstimate(flops=int(micros * 1.1e9), bytes_accessed=1024, transcendentals=0)


MASKS = (0, 2, 4, 6, 1, 3, 5, 7)


def owners(me, count):
    return [me ^ mask for mask in MASKS[:count]]


def staged_owners(me, count):
    if count == 1:
        return [0]
    first = 2 + 2 * (me & 1)
    second = 6 - first
    other = me ^ 1
    return [me, me ^ first, me ^ second, me ^ 6, other, other ^ second, other ^ first, other ^ 6]


def whole(shape):
    return pl.BlockSpec(
        shape, lambda *step: (0,) * len(shape), pipeline_mode=pl.Buffered(buffer_count=1)
    )


def prepare_kernel(one_ref, two_ref, hidden_bias_ref, out_ref, bias_ref, *refs):
    row_refs, (pack_ref, block_ref, rows_ref, columns_ref, wide_bias_ref) = refs[:6], refs[6:]
    rows, slot = one_ref.shape
    pack_ref[:rows, :slot] = one_ref[...]
    pack_ref[:rows, slot:] = two_ref[...]
    pack_ref[rows:] = jnp.zeros_like(pack_ref[rows:])
    pack_ref[rows : rows + 1, :slot] = hidden_bias_ref[...].reshape(1, slot)
    turned = out_ref[...].T
    width = turned.shape[1]
    for r in range(D // rows):
        block_ref[:, r * width : (r + 1) * width] = turned[r * rows : (r + 1) * rows]
    rows_ref[...] = jnp.zeros_like(rows_ref)
    for k, ref in enumerate(row_refs):
        rows_ref[k : k + 1] = ref[...].astype(f32).reshape(1, D)
    columns_ref[...] = rows_ref[...].T
    wide_bias_ref[...] = bias_ref[...].astype(f32).reshape(1, 2 * INNER)


def prepare(w_fc1, w_fc2, bias_fc1, w_out, bias_qv, vectors):
    rows, slot = w_fc1.shape
    return pl.pallas_call(
        prepare_kernel,
        out_shape=[
            jax.ShapeDtypeStruct((rows + 16, 2 * slot), bf16),
            jax.ShapeDtypeStruct((rows, INNER), bf16),
            jax.ShapeDtypeStruct((8, D), f32),
            jax.ShapeDtypeStruct((D, 8), f32),
            jax.ShapeDtypeStruct((1, 2 * INNER), f32),
        ],
        cost_estimate=cost(2),
        name="prepare",
    )(w_fc1, w_fc2.T, bias_fc1, w_out, bias_qv, *vectors)


def norm_kernel(tokens_ref, rows_ref, out_ref, scaled_ref):
    for s in range(out_ref.shape[0]):
        values = tokens_ref[s * LEN : (s + 1) * LEN].astype(f32)
        scaled, _ = normalize(values)
        normed = scaled * rows_ref[GAIN_ONE] + rows_ref[SHIFT_ONE]
        for ref, rows in ((scaled_ref, scaled), (out_ref, normed)):
            ref[s, :LEN] = rows.astype(bf16)
            ref[s, LEN:] = jnp.zeros((ROWS - LEN, D), bf16)


def first_norm(tokens, rows_in):
    seqs = tokens.shape[0] // LEN
    shape = jax.ShapeDtypeStruct((seqs, ROWS, D), bf16)
    return pl.pallas_call(
        norm_kernel,
        out_shape=[shape, shape],
        compiler_params=pltpu.CompilerParams(vmem_limit_bytes=10 * 1024 * 1024),
        cost_estimate=cost(2.5),
        name="first_norm",
    )(tokens, rows_in)


def attend_kernel(pieces, me_ref, normed_ref, bias_ref, mask_ref, *refs):
    parts, refs = refs[:pieces], refs[pieces:]
    projected_ref, mixed_ref, exp_ref, inverse_ref, wide_ref = refs[:5]
    hide_scr, score_scr, mixed_scr, total_scr, mask_scr = refs[5:]
    group, seq = pl.program_id(0), pl.program_id(1)

    @pl.when((group == 0) & (seq == 0))
    def _():
        rows = D // pieces
        for j, owner in enumerate(staged_owners(me_ref[0], pieces)):
            to = pl.ds(pl.multiple_of(owner * rows, 16), rows)
            for g in range(GROUPS):
                for k in range(3):
                    left = k * INNER + g * WIDE
                    at = g * QKV + k * WIDE
                    wide_ref[to, at : at + WIDE] = parts[j][:, left : left + WIDE]
        total_scr[...] = jnp.ones_like(total_scr)
        mask_scr[...] = jnp.zeros_like(mask_scr)
        count = hide_scr.shape[0]
        mask_scr[:count, :LEN] = mask_ref[...].astype(f32)
        turned = mask_scr[...].T
        key = lax.broadcasted_iota(jnp.int32, (KEYS, ROWS), 0)
        query = lax.broadcasted_iota(jnp.int32, (KEYS, ROWS), 1)
        later = ((query < FRAME_LEN) & (key >= FRAME_LEN)) | (
            (query < 2 * FRAME_LEN) & (key >= 2 * FRAME_LEN)
        )
        for s in range(count):
            usable = jnp.logical_not(later) & (turned[:KEYS, s : s + 1] > 0.5)
            hide_scr[s] = jnp.where(usable | (key == query), 0.0, -1e30)

    columns = pl.ds(pl.multiple_of(group * QKV, 128), QKV)
    projected = dot(normed_ref[seq, :KEYS], wide_ref[:, columns], NN)
    at = pl.multiple_of(group * WIDE, 128)
    queries = (projected[:, :WIDE] + bias_ref[:, pl.ds(at, WIDE)]).astype(bf16)
    projected_ref[0, :KEYS, :WIDE] = queries * bf16(HEAD_DIM**-0.5)
    projected_ref[0, :KEYS, WIDE : 2 * WIDE] = projected[:, WIDE : 2 * WIDE].astype(bf16)
    values = projected[:, 2 * WIDE :] + bias_ref[:, pl.ds(at + INNER, WIDE)]
    projected_ref[0, :KEYS, 2 * WIDE :] = values.astype(bf16)
    projected_ref[0, KEYS:] = jnp.zeros((ROWS - KEYS, QKV), bf16)
    from_ref = projected_ref.at[0]

    lane = lax.broadcasted_iota(jnp.int32, (1, 128), 1)
    units = [(h, b) for h in range(GROUP) for b in QUERY_BLOCKS]

    largest = {}
    flipped = {}

    def scores(unit):
        head, (start, width, keys) = units[unit]
        pair = head // 2 * 128
        mine = (lane < 64) if head % 2 == 0 else (lane >= 64)
        own_keys = from_ref[:keys, WIDE + pair : WIDE + pair + 128]
        own_keys = jnp.where(mine, own_keys, bf16(0))
        score = dot(own_keys, from_ref[start : start + width, pair : pair + 128], NT)
        score = score + hide_scr[seq, :keys, start : start + width]
        score_scr[unit % 3, :keys, :width] = score
        top = jnp.max(score.reshape(-1, 8, width), axis=0)
        largest[unit] = jnp.max(top, axis=0, keepdims=True)

    def exponents(unit):
        head, (start, width, keys) = units[unit]
        exponent = jnp.exp(score_scr[unit % 3, :keys, :width] - largest[unit])
        exp_ref[0, head, :keys, start : start + width] = exponent.astype(bf16)

    def mix(unit):
        head, (start, width, keys) = units[unit]
        pair = head // 2 * 128
        if head not in flipped:
            turned = from_ref[:KEYS, 2 * WIDE + pair : 2 * WIDE + pair + 128].T
            side = head % 2 * 64
            ones = jnp.ones((16, KEYS), bf16)
            flipped[head] = jnp.concatenate([turned[side : side + 64], ones])
        exponent = exp_ref[0, head, :keys, start : start + width]
        summed = dot(flipped[head][:, :keys], exponent, NN)
        values, total = summed[:64], summed[64:65]
        inverse = 1.0 / total
        mixed_scr[head * 64 : (head + 1) * 64, start : start + width] = values * inverse
        total_scr[head : head + 1, start : start + width] = inverse

    count = len(units)
    scores(0)
    scores(1)
    for unit in range(count + 2):
        if unit + 2 < count:
            scores(unit + 2)
        if unit < count:
            exponents(unit)
        if unit > 1:
            mix(unit - 2)
    mixed_ref[0] = mixed_scr[...].T.astype(bf16)
    inverse_ref[0, 0] = total_scr[...]


def attend(me, normed, parts, bias, mask):
    seqs = normed.shape[0]
    return pl.pallas_call(
        functools.partial(attend_kernel, len(parts)),
        grid=(GROUPS, seqs),
        in_specs=[
            pl.BlockSpec(memory_space=pltpu.SMEM),
            whole(normed.shape),
            whole(bias.shape),
            whole(mask.shape),
        ]
        + [whole(part.shape) for part in parts],
        out_specs=[
            pl.BlockSpec((1, ROWS, QKV), lambda g, s: (s, 0, g)),
            pl.BlockSpec((1, ROWS, WIDE), lambda g, s: (s, 0, g)),
            pl.BlockSpec((1, GROUP, KEYS, ROWS), lambda g, s: (s, g, 0, 0)),
            pl.BlockSpec((1, 1, 8, ROWS), lambda g, s: (s, g, 0, 0)),
            whole((D, GROUPS * QKV)),
        ],
        out_shape=[
            pltpu.HBM((seqs, ROWS, GROUPS * QKV), bf16),
            pltpu.HBM((seqs, ROWS, INNER), bf16),
            pltpu.HBM((seqs, HEADS, KEYS, ROWS), bf16),
            pltpu.HBM((seqs, GROUPS, 8, ROWS), f32),
            pltpu.HBM((D, GROUPS * QKV), bf16),
        ],
        scratch_shapes=[
            pltpu.VMEM((seqs, KEYS, ROWS), f32),
            pltpu.VMEM((3, KEYS, 256), f32),
            pltpu.VMEM((WIDE, ROWS), f32),
            pltpu.VMEM((8, ROWS), f32),
            pltpu.VMEM((8, ROWS), f32),
        ],
        compiler_params=pltpu.CompilerParams(vmem_limit_bytes=24 * 1024 * 1024),
        cost_estimate=cost(22),
        name="attend",
    )(me, normed, bias, mask, *parts)


def forward_kernel(pieces, n_bias, chunk, me_ref, tokens_ref, grad_ref, rows_ref, *refs):
    bias_refs, refs = refs[:n_bias], refs[n_bias:]
    mixed_ref, refs = refs[0], refs[1:]
    parts, refs = refs[:pieces], refs[pieces:]
    out_ref, middle_grad_ref, branch_ref, out_wide_ref = refs[:4]
    n_out = 2 if pieces > 1 else 1
    send_refs, refs = refs[4 : 4 + n_out], refs[4 + n_out :]
    one_scr, two_scr, middle_scr, scaled_scr, inverse_scr, second_scr, second_t, grad_scr = refs[:8]
    grad_t, total_scr, back_scr, weight_scr, small_scr, bias_scr = refs[8:14]
    stage_scrs = (refs[14:16], refs[16:18])
    seqs = branch_ref.shape[0]
    step = pl.program_id(0)
    rows = D // pieces
    per_slot = FF // 4
    ones = jnp.ones((16, seqs * KEYS), bf16)

    def send(value_ref, at, width, left):
        if pieces == 1:
            send_refs[0][0, :, left : left + width] = value_ref[:, at : at + width].astype(bf16)
            return
        for j, owner in enumerate(owners(me_ref[0], pieces)):
            first = pl.multiple_of(owner * rows, 16)
            send_refs[j // 4][j % 4, 0, :, left : left + width] = value_ref[
                pl.ds(first, rows), at : at + width
            ].astype(bf16)

    def send_vectors():
        vectors = small_scr[...].astype(bf16)
        if pieces == 1:
            send_refs[0][0, :48, INNER:] = vectors
        else:
            for j in range(pieces):
                send_refs[j // 4][j % 4, 0, :, INNER:] = vectors

    def produce(index, stage):
        act_scr, pre_scr = stage_scrs[stage]
        hidden = pl.ds(pl.multiple_of(index * chunk, 128), chunk)
        pre = dot(second_scr[...], one_scr[:, hidden], NN) + bias_scr[:, hidden]
        half = 0.5 + 0.5 * lax.erf(pre * (0.5**0.5))
        act_scr[...] = (pre * half).astype(bf16)
        slope = half + pre * (jnp.exp2(pre * pre * -0.7213475204444817) * 0.3989422804014327)
        grad_act = dot(grad_scr[...], two_scr[:, hidden], NN)
        pre_scr[...] = (grad_act * slope).astype(bf16)

    def consume(index, stage):
        act_scr, pre_scr = stage_scrs[stage]
        hidden = pl.ds(pl.multiple_of(index * chunk, 128), chunk)
        total_scr[...] += dot(act_scr[...], two_scr[:, hidden], NT)
        back_scr[...] += dot(pre_scr[...], one_scr[:, hidden], NT)
        left = stage * chunk
        weight_scr[:, :chunk] = dot(second_t[...], pre_scr[...], NN)
        send(weight_scr, 0, chunk, left)
        weight_scr[:, chunk : 2 * chunk] = dot(grad_t[...], act_scr[...], NN)
        send(weight_scr, chunk, chunk, left + per_slot)
        hidden_sum = dot(ones, pre_scr[...], NN)[0:1]
        for r in range(chunk // 128):
            at = stage * (chunk // 128) + r
            small_scr[at : at + 1] = hidden_sum[:, r * 128 : (r + 1) * 128]

    @pl.when(step == 0)
    def _():
        for j, owner in enumerate(owners(me_ref[0], pieces)):
            first = pl.multiple_of(owner * rows, 16)
            if pieces == 1:
                out_wide_ref[...] = parts[0][:, :INNER]
            else:
                to = pl.ds(pl.multiple_of(owner * 128, 128), 128)
                for r in range(pieces):
                    out_wide_ref[r * rows : (r + 1) * rows, to] = parts[j][
                        :, r * 128 : (r + 1) * 128
                    ]
            for z in range(4):
                left = INNER + 2 * per_slot * z
                slot = slice(z * per_slot, (z + 1) * per_slot)
                one_scr[pl.ds(first, rows), slot] = parts[j][:, left : left + per_slot]
                two_scr[pl.ds(first, rows), slot] = parts[j][
                    :, left + per_slot : left + 2 * per_slot
                ]
        if n_bias == 1:
            bias_scr[...] = bias_refs[0][...].astype(f32)
        else:
            for z in range(4):
                row = bias_refs[z][rows : rows + 1, :per_slot]
                bias_scr[:, z * per_slot : (z + 1) * per_slot] = row.astype(f32)
        for s in range(seqs):
            block = slice(s * KEYS, (s + 1) * KEYS)
            real = slice(s * KEYS, s * KEYS + LEN)
            spare = slice(s * KEYS + LEN, (s + 1) * KEYS)
            given = slice(s * LEN, (s + 1) * LEN)
            grad_scr[real] = grad_ref[given]
            grad_scr[spare] = jnp.zeros((KEYS - LEN, D), bf16)
            middle_scr[real] = tokens_ref[given].astype(f32) + rows_ref[BIAS_OUT]
            middle_scr[spare] = jnp.zeros((KEYS - LEN, D), f32)
            middle = middle_scr[block] + dot(mixed_ref[s, :KEYS], out_wide_ref[...], NT)
            middle_scr[block] = middle
            scaled, inverse = normalize(middle)
            scaled_scr[block] = scaled
            inverse_scr[block] = inverse
            second_scr[block] = (scaled * rows_ref[GAIN_TWO] + rows_ref[SHIFT_TWO]).astype(bf16)
        second_t[...] = second_scr[...].T
        grad_t[...] = grad_scr[...].T
        total_scr[...] = jnp.zeros_like(total_scr)
        back_scr[...] = jnp.zeros_like(back_scr)
        small_scr[...] = jnp.zeros_like(small_scr)
        produce(0, 0)

    @pl.when(step < 4)
    def _():
        produce(2 * step + 1, 1)
        consume(2 * step, 0)
        produce(jnp.minimum(2 * step + 2, FF // chunk - 1), 0)
        consume(2 * step + 1, 1)
        send_vectors()

    @pl.when(step == 4)
    def _():
        sums = [jnp.zeros((1, D), f32) for _ in range(2)]
        for s in range(seqs):
            block = slice(s * KEYS, (s + 1) * KEYS)
            given = slice(s * LEN, (s + 1) * LEN)
            output = (middle_scr[block] + total_scr[block] + rows_ref[BIAS_TWO]).astype(bf16)
            out_ref[given] = output[:LEN]
            scaled, inverse = scaled_scr[block], inverse_scr[block]
            grad_second = back_scr[block]
            grad_middle = grad_scr[block].astype(f32) + normalize_back(
                grad_second, rows_ref[GAIN_TWO], scaled, inverse
            )
            middle_grad_ref[s, :KEYS] = grad_middle
            branch_ref[s, :KEYS] = grad_middle.astype(bf16)
            branch_ref[s, KEYS:] = jnp.zeros((ROWS - KEYS, D), bf16)
            for k, term in enumerate((grad_second * scaled, grad_second)):
                sums[k] = sums[k] + jnp.sum(term, axis=0, keepdims=True)
        branch = jnp.concatenate([branch_ref[s, :KEYS] for s in range(seqs)], axis=0)
        sums.append(dot(ones, branch, NN)[0:1])
        sums.append(dot(ones, grad_scr[...], NN)[0:1])
        for k in range(4):
            for r in range(D // 128):
                at = 3 * k + r
                small_scr[at : at + 1] = sums[k][:, r * 128 : (r + 1) * 128]
        mixed = jnp.concatenate([mixed_ref[s, :KEYS] for s in range(seqs)], axis=0)
        weight_scr[...] = dot(branch, mixed, TN)
        if pieces == 1:
            send_refs[0][0, :, :INNER] = weight_scr[...].astype(bf16)
        else:
            for j, owner in enumerate(owners(me_ref[0], pieces)):
                to = pl.ds(pl.multiple_of(owner * 128, 128), 128)
                for r in range(pieces):
                    send_refs[j // 4][j % 4, 0, :, r * 128 : (r + 1) * 128] = weight_scr[
                        r * rows : (r + 1) * rows, to
                    ].astype(bf16)
        send_vectors()


def forward(me, tokens, cotangent, rows_in, biases, mixed, parts):
    seqs = tokens.shape[0] // LEN
    pieces = len(parts)
    chunk = 256
    if pieces > 1:
        send_shapes = [(pieces // 2, 5, D // pieces, BLOCK)] * 2
        send_specs = [pl.BlockSpec((pieces // 2, 1, D // pieces, BLOCK), lambda c: (0, c, 0, 0))] * 2
    else:
        send_shapes = [(5, D, BLOCK)]
        send_specs = [pl.BlockSpec((1, D, BLOCK), lambda c: (c, 0, 0))]
    rows3 = (seqs, ROWS, D)
    rows2 = (seqs * KEYS, D)
    mixed = pltpu.with_memory_space_constraint(mixed, pltpu.HBM)
    return pl.pallas_call(
        functools.partial(forward_kernel, pieces, len(biases), chunk),
        grid=(5,),
        in_specs=[
            pl.BlockSpec(memory_space=pltpu.SMEM),
            whole(tokens.shape),
            whole(tokens.shape),
            whole((8, D)),
        ]
        + [whole(b.shape) for b in biases]
        + [whole(mixed.shape)]
        + [whole(p.shape) for p in parts],
        out_specs=[whole(tokens.shape), whole(rows3), whole(rows3), whole((D, INNER))]
        + send_specs,
        out_shape=[
            jax.ShapeDtypeStruct(tokens.shape, bf16),
            jax.ShapeDtypeStruct(rows3, f32),
            jax.ShapeDtypeStruct(rows3, bf16),
            jax.ShapeDtypeStruct((D, INNER), bf16),
        ]
        + [jax.ShapeDtypeStruct(s, bf16) for s in send_shapes],
        scratch_shapes=[
            pltpu.VMEM((D, FF), bf16),
            pltpu.VMEM((D, FF), bf16),
            pltpu.VMEM(rows2, f32),
            pltpu.VMEM(rows2, f32),
            pltpu.VMEM((seqs * KEYS, 1), f32),
            pltpu.VMEM(rows2, bf16),
            pltpu.VMEM((D, seqs * KEYS), bf16),
            pltpu.VMEM(rows2, bf16),
            pltpu.VMEM((D, seqs * KEYS), bf16),
            pltpu.VMEM(rows2, f32),
            pltpu.VMEM(rows2, f32),
            pltpu.VMEM((D, INNER), f32),
            pltpu.VMEM((48, 128), f32),
            pltpu.VMEM((1, FF), f32),
        ]
        + [pltpu.VMEM((seqs * KEYS, chunk), bf16)] * 4,
        compiler_params=pltpu.CompilerParams(vmem_limit_bytes=36 * 1024 * 1024),
        cost_estimate=cost(30),
        name="forward",
    )(me, tokens, cotangent, rows_in, *biases, mixed, *parts)


def mixed_gradient_kernel(branch_ref, out_wide_ref, mixed_ref, grad_ref, delta_ref):
    lane = lax.broadcasted_iota(jnp.int32, (8, WIDE), 1)
    gather = (lane >> 6 == lax.broadcasted_iota(jnp.int32, (8, WIDE), 0)).astype(bf16)
    for g in range(delta_ref.shape[1]):
        columns = slice(g * WIDE, (g + 1) * WIDE)
        grad = dot(branch_ref[0], out_wide_ref[:, columns], NN).astype(bf16)
        grad_ref[0, :, columns] = grad
        product = grad.astype(f32) * mixed_ref[0, :, columns].astype(f32)
        first = product.astype(bf16)
        second = (product - first.astype(f32)).astype(bf16)
        delta_ref[0, g] = dot(gather, first, NT) + dot(gather, second, NT)


def mixed_gradient(branch, out_wide, mixed):
    seqs = branch.shape[0]
    each = 2
    columns = pl.BlockSpec((1, ROWS, each * WIDE), lambda s, g: (s, 0, g))
    return pl.pallas_call(
        mixed_gradient_kernel,
        grid=(seqs, GROUPS // each),
        in_specs=[
            pl.BlockSpec((1, ROWS, D), lambda s, g: (s, 0, 0)),
            pl.BlockSpec((D, each * WIDE), lambda s, g: (0, g)),
            columns,
        ],
        out_specs=[columns, pl.BlockSpec((1, each, 8, ROWS), lambda s, g: (s, g, 0, 0))],
        out_shape=[
            pltpu.HBM((seqs, ROWS, INNER), bf16),
            pltpu.HBM((seqs, GROUPS, 8, ROWS), f32),
        ],
        compiler_params=pltpu.CompilerParams(vmem_limit_bytes=16 * 1024 * 1024),
        cost_estimate=cost(5),
        name="mixed_gradient",
    )(branch, out_wide, mixed)


def backward_kernel(pieces, me_ref, *refs):
    grad_ref, delta_ref, scaled_ref, projected_ref, exp_ref, inverse_ref = refs[:6]
    wide_ref, norm_ref = refs[6:8]
    refs = refs[8:]
    n_out = 2 if pieces > 1 else 1
    back_ref = refs[0]
    send_refs = refs[1 : 1 + n_out]
    grad_scr, prob_scr, turned_scr, weight_scr, small_scr, sum_scr, norm_scr = refs[1 + n_out :]
    group, seq = pl.program_id(0), pl.program_id(1)
    groups, seqs = pl.num_programs(0), pl.num_programs(1)
    rows = D // pieces

    @pl.when((group == 0) & (seq == 0))
    def _():
        small_scr[...] = jnp.zeros_like(small_scr)
        norm_scr[...] = jnp.zeros_like(norm_scr)

    lane = lax.broadcasted_iota(jnp.int32, (1, 128), 1)
    low = lane < 64
    kept = {}
    for pair in range(GROUP // 2):
        columns = slice(pair * 128, pair * 128 + 128)
        grad = grad_ref[0, :, columns]
        query = projected_ref[0, :, columns]
        value = projected_ref[0, :KEYS, 2 * WIDE + pair * 128 : 2 * WIDE + pair * 128 + 128]
        turned = projected_ref[0, :KEYS, WIDE + pair * 128 : WIDE + pair * 128 + 128].T
        for half in range(2):
            head = 2 * pair + half
            mine = low if half == 0 else jnp.logical_not(low)
            own_value = jnp.where(mine, value, bf16(0))
            inverse = inverse_ref[0, 0, head : head + 1].astype(bf16)
            delta = delta_ref[0, 0, head : head + 1]
            side = slice(64 * half, 64 * half + 64)
            for start, width, keys in QUERY_BLOCKS:
                block = slice(start, start + width)
                change = dot(own_value[:keys], grad[block], NT) - delta[:, block]
                probability = exp_ref[0, head, :keys, block] * inverse[:, block]
                prob_scr[half, :keys, block] = probability
                grad_scr[half, :keys, block] = probability * change.astype(bf16)
            for start, width, keys in QUERY_BLOCKS:
                block = slice(start, start + width)
                turned_scr[head * 64 : (head + 1) * 64, block] = dot(
                    turned[side, :keys], grad_scr[half, :keys, block], NN
                ) * (HEAD_DIM**-0.5)
            for start, stop, seen in KEY_RANGES:
                value_grad = dot(prob_scr[half, start:stop, seen:], grad[seen:], NN)
                key_grad = dot(grad_scr[half, start:stop, seen:], query[seen:], NN)
                if half == 0:
                    kept[start] = (value_grad, key_grad)
                else:
                    at = slice(WIDE + pair * 128, WIDE + pair * 128 + 128)
                    back_ref[0, start:stop, at] = jnp.where(low, kept[start][1], key_grad).astype(
                        bf16
                    )
                    at = slice(2 * WIDE + pair * 128, 2 * WIDE + pair * 128 + 128)
                    back_ref[0, start:stop, at] = jnp.where(low, kept[start][0], value_grad).astype(
                        bf16
                    )
    back_ref[0, :KEYS, :WIDE] = turned_scr[...].T[:KEYS].astype(bf16)

    back = back_ref[0, :KEYS]
    weight = dot(scaled_ref[0, :KEYS], back, TN)
    total = dot(jnp.ones((16, KEYS), bf16), back, NN)[0:1]

    @pl.when(seq == 0)
    def _():
        weight_scr[...] = weight
        sum_scr[0:1] = total

    @pl.when(seq > 0)
    def _():
        weight_scr[...] += weight
        sum_scr[0:1] += total

    @pl.when(seq == seqs - 1)
    def _():
        sums = sum_scr[0:1]
        for r in range(WIDE // 128):
            at = group * (2 * WIDE // 128) + r
            small_scr[pl.ds(at, 1)] = sums[:, r * 128 : r * 128 + 128]
            at = at + WIDE // 128
            small_scr[pl.ds(at, 1)] = sums[:, 2 * WIDE + r * 128 : 2 * WIDE + r * 128 + 128]
        wide = wide_ref[...].astype(f32)
        scaled_weight = weight_scr[...]
        norm_scr[:, 0:1] += jnp.sum(scaled_weight * wide, axis=1, keepdims=True)
        norm_scr[:, 1:2] += jnp.sum(sums * wide, axis=1, keepdims=True)
        weight_scr[...] = scaled_weight * norm_ref[:, GAIN_ONE] + sums * norm_ref[:, SHIFT_ONE]
        start = pl.multiple_of(group * QKV, 128)
        if pieces == 1:
            send_refs[0][:, pl.ds(start, QKV)] = weight_scr[...].astype(bf16)
        else:
            for j, owner in enumerate(owners(me_ref[0], pieces)):
                first = pl.multiple_of(owner * rows, 16)
                send_refs[j // 4][j % 4, :, pl.ds(start, QKV)] = weight_scr[
                    pl.ds(first, rows)
                ].astype(bf16)

    @pl.when((group == groups - 1) & (seq == seqs - 1))
    def _():
        turned = norm_scr[...].T
        for k in range(2):
            for r in range(D // 128):
                small_scr[40 + 3 * k + r : 41 + 3 * k + r] = turned[
                    k : k + 1, r * 128 : (r + 1) * 128
                ]
        small = small_scr[...].astype(bf16)
        if pieces == 1:
            send_refs[0][:48, send_refs[0].shape[1] - SMALL :] = small
        else:
            for j in range(pieces):
                edge = send_refs[0].shape[2] - SMALL
                send_refs[j // 4][j % 4, :, edge:] = small


def backward(me, pieces, first_group, groups, grads, scaled, norm, saved):
    operands = [
        pltpu.with_memory_space_constraint(x, pltpu.HBM)
        for x in (*grads, scaled, saved[0], saved[2], saved[3], saved[4])
    ]
    seqs = scaled.shape[0]
    width = groups * QKV + SMALL
    if pieces > 1:
        send_shapes = [(pieces // 2, D // pieces, width)] * 2
    else:
        send_shapes = [(D, width)]
    columns = pl.BlockSpec((1, ROWS, WIDE), lambda g, s: (s, 0, g + first_group))
    heads = pl.BlockSpec((1, 1, 8, ROWS), lambda g, s: (s, g + first_group, 0, 0))
    rows_block = pl.BlockSpec((1, ROWS, D), lambda g, s: (s, 0, 0))
    return pl.pallas_call(
        functools.partial(backward_kernel, pieces),
        grid=(groups, seqs),
        in_specs=[
            pl.BlockSpec(memory_space=pltpu.SMEM),
            columns,
            heads,
            rows_block,
            pl.BlockSpec((1, ROWS, QKV), lambda g, s: (s, 0, g + first_group)),
            pl.BlockSpec((1, GROUP, KEYS, ROWS), lambda g, s: (s, g + first_group, 0, 0)),
            heads,
            pl.BlockSpec((D, QKV), lambda g, s: (0, g + first_group)),
            whole((D, 8)),
        ],
        out_specs=[pl.BlockSpec((1, ROWS, QKV), lambda g, s: (s, 0, g))]
        + [whole(s) for s in send_shapes],
        out_shape=[jax.ShapeDtypeStruct((seqs, ROWS, groups * QKV), bf16)]
        + [jax.ShapeDtypeStruct(s, bf16) for s in send_shapes],
        scratch_shapes=[
            pltpu.VMEM((2, KEYS, ROWS), bf16),
            pltpu.VMEM((2, KEYS, ROWS), bf16),
            pltpu.VMEM((WIDE, ROWS), f32),
            pltpu.VMEM((D, QKV), f32),
            pltpu.VMEM((48, 128), f32),
            pltpu.VMEM((8, QKV), f32),
            pltpu.VMEM((D, 128), f32),
        ],
        compiler_params=pltpu.CompilerParams(vmem_limit_bytes=23 * 1024 * 1024),
        cost_estimate=cost(11 * groups),
        name="backward",
    )(me, *operands, norm)


def early_kernel(back_ref, wide_ref, out_ref):
    for s in range(out_ref.shape[0]):
        grad = dot(back_ref[s, :KEYS], wide_ref[...], NT)
        before = jnp.where(pl.program_id(0) == 0, 0.0, out_ref[s])
        out_ref[s] = before + grad


def early_gradient(back, weights):
    seqs, groups = back.shape[0], back.shape[2] // QKV
    return pl.pallas_call(
        early_kernel,
        grid=(groups,),
        in_specs=[
            pl.BlockSpec((seqs, ROWS, QKV), lambda g: (0, 0, g)),
            pl.BlockSpec((D, QKV), lambda g: (0, g)),
        ],
        out_specs=whole((seqs, KEYS, D)),
        out_shape=jax.ShapeDtypeStruct((seqs, KEYS, D), f32),
        compiler_params=pltpu.CompilerParams(vmem_limit_bytes=14 * 1024 * 1024),
        cost_estimate=cost(5),
        name="early_gradient",
    )(back, weights)


def input_kernel(tokens_ref, middle_grad_ref, rows_ref, early_ref, back_ref, wide_ref, out_ref):
    for s in range(middle_grad_ref.shape[0]):
        grad_first = early_ref[s] + dot(back_ref[s, :KEYS], wide_ref[...], NT)
        given = slice(s * LEN, (s + 1) * LEN)
        scaled, inverse = normalize(tokens_ref[given].astype(f32))
        out_ref[given] = middle_grad_ref[s, :LEN] + normalize_back(
            grad_first[:LEN], rows_ref[GAIN_ONE], scaled, inverse
        )


def input_gradient(tokens, middle_grad, rows_in, early, back, weights):
    return pl.pallas_call(
        input_kernel,
        grid=(1,),
        in_specs=[
            whole(tokens.shape),
            whole(middle_grad.shape),
            whole(rows_in.shape),
            whole(early.shape),
            whole(back.shape),
            pl.BlockSpec((D, QKV), lambda g: (0, GROUPS - 1)),
        ],
        out_specs=whole(tokens.shape),
        out_shape=jax.ShapeDtypeStruct(tokens.shape, f32),
        compiler_params=pltpu.CompilerParams(vmem_limit_bytes=16 * 1024 * 1024),
        cost_estimate=cost(4),
        name="input_gradient",
    )(tokens, middle_grad, rows_in, early, back, weights)


def join_lines(values):
    return jnp.concatenate([values[k : k + 1] for k in range(values.shape[0])], axis=1)


def hidden_end_kernel(block_ref, rest_ref, arrived_ref, one_ref, two_ref, bias_ref, out_ref, *refs):
    rows, slot = one_ref.shape
    block = block_ref[...] + arrived_ref[:, :BLOCK].astype(f32)
    rest = rest_ref[...] + arrived_ref[:, BLOCK:].astype(f32)
    one_ref[...] = block[:, :slot]
    two_ref[...] = block[:, slot : 2 * slot]
    bias_ref[...] = join_lines(block[: slot // 128, INNER:]).reshape(slot)
    width = out_ref.shape[0]
    parts = [rest[:, r * width : (r + 1) * width] for r in range(INNER // width)]
    out_ref[...] = jnp.concatenate(parts, axis=0).T
    for k, ref in enumerate(refs):
        ref[...] = join_lines(rest[3 * k : 3 * k + 3, INNER:]).reshape(D)


def hidden_end(block, rest, arrived, slot):
    rows = block.shape[0]
    width = INNER // (D // rows)
    vector = jax.ShapeDtypeStruct((D,), f32)
    return pl.pallas_call(
        hidden_end_kernel,
        out_shape=[
            jax.ShapeDtypeStruct((rows, slot), f32),
            jax.ShapeDtypeStruct((rows, slot), f32),
            jax.ShapeDtypeStruct((slot,), f32),
            jax.ShapeDtypeStruct((width, D), f32),
        ]
        + [vector] * 4,
        compiler_params=pltpu.CompilerParams(vmem_limit_bytes=8 * 1024 * 1024),
        cost_estimate=cost(2),
        name="hidden_end",
    )(block, rest, arrived)


def heads_end_kernel(early_ref, early_line_ref, late_ref, late_line_ref, weight_ref, bias_ref, *refs):
    early = early_ref[...] + early_line_ref[...].astype(f32)
    late = late_ref[...] + late_line_ref[...].astype(f32)
    lines = WIDE // 128
    norms, group = 0.0, 0
    for part in (early, late):
        edge = part.shape[1] - SMALL
        for g in range(edge // QKV):
            for k in range(3):
                left = g * QKV + k * WIDE
                to = k * INNER + group * WIDE
                weight_ref[:, to : to + WIDE] = part[:, left : left + WIDE]
            for k in range(2):
                first = (2 * g + k) * lines
                values = join_lines(part[first : first + lines, edge:])
                at = k * INNER + group * WIDE
                bias_ref[at : at + WIDE] = values.reshape(WIDE)
            group += 1
        norms = norms + part[40:48, edge:]
    for k, ref in enumerate(refs):
        ref[...] = join_lines(norms[3 * k : 3 * k + 3]).reshape(D)


def heads_end(early, early_line, late, late_line):
    vector = jax.ShapeDtypeStruct((D,), f32)
    return pl.pallas_call(
        heads_end_kernel,
        out_shape=[
            jax.ShapeDtypeStruct((early.shape[0], 3 * INNER), f32),
            jax.ShapeDtypeStruct((2 * INNER,), f32),
            vector,
            vector,
        ],
        compiler_params=pltpu.CompilerParams(vmem_limit_bytes=8 * 1024 * 1024),
        cost_estimate=cost(2),
        name="heads_end",
    )(early, early_line, late, late_line)


def swap(values, mask):
    size = lax.axis_size("tok")
    return lax.ppermute(values, "tok", [(i, i ^ mask) for i in range(size)])


def swap_half_plane(values, stage):
    size = lax.axis_size("tok")
    pairs = [(t, t ^ (2 if (t % 2 == 0) == (stage == 0) else 4)) for t in range(size)]
    return lax.ppermute(values, "tok", pairs)


def swap_half_line(values, stage):
    tok, mlp = lax.axis_size("tok"), lax.axis_size("mlp")
    pairs = []
    for t in range(tok):
        for z in range(mlp):
            far = (t % 2 == 0) == (stage == 0)
            pairs.append((t * mlp + z, t * mlp + (z ^ (2 if far else 1))))
    return lax.ppermute(values.astype(bf16), ("tok", "mlp"), pairs)


def after(values, *earlier):
    return lax.optimization_barrier((values,) + earlier)


def wide(values):
    return values.astype(f32)


def join(kept, arrived):
    return (wide(kept) + wide(arrived)).astype(bf16)


def body(
    tokens,
    action_mask,
    ln1_gain,
    ln1_bias,
    w_qkv,
    bias_qv,
    w_out,
    bias_out,
    ln2_gain,
    ln2_bias,
    w_fc1,
    bias_fc1,
    w_fc2,
    bias_fc2,
    out_grad,
):
    rows = w_qkv.shape[0]
    tok = lax.axis_size("tok")
    mlp = lax.axis_size("mlp")
    slot = w_fc1.shape[1]
    fast = tok == 8 and mlp == 4
    pieces = tok if fast else 1
    me = lax.axis_index("tok").astype(jnp.int32).reshape(1)
    chips = (2, 4, 6)
    odd = (me[0] & 1) == 1

    def pick(if_odd, if_even):
        return jnp.where(odd, if_odd, if_even)


    vectors = (bias_out, ln2_gain, ln2_bias, bias_fc2, ln1_gain, ln1_bias)
    me_a = me
    if fast:
        first_near = [swap_half_plane(w_qkv, stage) for stage in (0, 1)]
        first_near.append(swap_half_plane(first_near[0], 1))
        first_other = swap(w_qkv, 1)
        hidden_pack, out_block, rows_in, columns_in, bias_pair = prepare(
            w_fc1, w_fc2, bias_fc1, w_out, bias_qv, vectors
        )
        line = jnp.stack([hidden_pack, swap_half_line(hidden_pack, 0)])
        line = jnp.concatenate([line, swap_half_line(line, 1)])
        line = [line[0], pick(line[1], line[2]), pick(line[2], line[1]), line[3]]
        norm_tokens, first_near[0] = after(tokens, first_near[0])
        normed, scaled = first_norm(norm_tokens, rows_in)
        first_parts = [w_qkv] + first_near + [first_other] + [swap(p, 1) for p in first_near]
        hidden_own = jnp.concatenate([out_block] + [part[:rows] for part in line], axis=1)
        me_a, hidden_own = after(me, hidden_own)
        hidden_near = [swap(hidden_own, mask) for mask in chips + (1,)]
        biases = line
    else:
        rows_in = jnp.pad(wide(jnp.stack(vectors)), ((0, 2), (0, 0)))
        columns_in = rows_in.T
        bias_pair = wide(bias_qv).reshape(1, -1)
        normed, scaled = first_norm(tokens, rows_in)
        first_parts = [lax.all_gather(w_qkv, "tok", axis=0, tiled=True)]
        line = lax.all_gather(jnp.concatenate([w_fc1, w_fc2.T], axis=1), "mlp", axis=1, tiled=True)
        line = lax.all_gather(line, "tok", axis=0, tiled=True)
        biases = [lax.all_gather(bias_fc1, "mlp", axis=0, tiled=True).reshape(1, -1)]
        out_all = lax.all_gather(w_out, "tok", axis=0, tiled=True).T
        hidden_parts = [jnp.concatenate([out_all, line], axis=1)]

    saved = list(attend(me_a, normed, first_parts, bias_pair, action_mask))
    weights = saved[4]
    if fast:
        saved[1], *hidden_near = after(saved[1], *hidden_near)
        hidden_other = hidden_near.pop()
        hidden_parts = [hidden_own] + hidden_near + [hidden_other]
        hidden_parts = hidden_parts + [swap(part, 1) for part in hidden_near]

    output, middle_grad, branch, out_wide, *hidden_sends = forward(
        me, tokens, out_grad, rows_in, biases, saved[1], hidden_parts
    )

    grads = list(mixed_gradient(branch, out_wide, saved[1]))

    def back(me, group, count):
        return backward(me, pieces, group, count, grads, scaled, columns_in, saved)

    if not fast:
        back_a, sends_a = back(me, 0, 3)
        back_b, sends_b = back(me, 3, 1)
        early = early_gradient(back_a, weights)
        input_grad = input_gradient(tokens, middle_grad, rows_in, early, back_b, weights)
        return slow_end(output, input_grad, hidden_sends[0], (sends_a, sends_b), slot)

    arrived = swap(hidden_sends[1], 1)
    grads[0], arrived = after(grads[0], arrived)
    hidden = join(hidden_sends[0], arrived)
    me_1, hidden = after(me, hidden)
    near = [swap(hidden[k], chips[k - 1]) for k in (1, 2, 3)]
    back_a, *sends_a = back(me_1, 0, 3)

    back_a, *near = after(back_a, *near)
    hidden = wide(hidden[0]) + wide(near[0]) + wide(near[1]) + wide(near[2])
    sent = jnp.stack([pick(hidden[1], hidden[2]), hidden[3], hidden[4]]).astype(bf16)
    group_a = join(sends_a[0], swap(sends_a[1], 1))
    me_2, group_a, sent = after(me, group_a, sent)
    line_1 = swap_half_line(sent, 0)
    near_a = [swap(group_a[k], chips[k - 1]) for k in (1, 2, 3)]
    back_b, *sends_b = back(me_2, 3, 1)

    back_b, line_1, *near_a = after(back_b, line_1, *near_a)
    total_a = wide(group_a[0]) + wide(near_a[0]) + wide(near_a[1]) + wide(near_a[2])
    sent, kept_b, sent_b = after(total_a.astype(bf16), *sends_b)
    line_a = swap_half_line(sent, 1)
    group_b = join(kept_b, swap(sent_b, 1))
    line_1, group_b = after(line_1, group_b)
    block = hidden[0] + wide(line_1[0])
    middle_block = pick(hidden[2], hidden[1]) + wide(line_1[1])
    rest = hidden[4] + wide(line_1[2])
    sent = jnp.concatenate([middle_block, rest], axis=1).astype(bf16)
    group_b, sent = after(group_b, sent)
    line_2 = swap_half_line(sent, 1)
    near_b = [swap(group_b[k], chips[k - 1]) for k in (1, 2, 3)]
    line_a, *near_b = after(line_a, *near_b)
    total_b = wide(group_b[0]) + wide(near_b[0]) + wide(near_b[1]) + wide(near_b[2])
    total_a = total_a + wide(line_a)
    back_a, sent_b, sent_a = after(back_a, total_b.astype(bf16), total_a.astype(bf16))
    line_b = swap_half_line(sent_b, 0)
    line_a = swap_half_line(sent_a, 0)
    early = early_gradient(back_a, weights)

    early, line_b = after(early, line_b)
    total_b = total_b + wide(line_b)
    early, sent = after(early, total_b.astype(bf16))
    line_b = swap_half_line(sent, 1)
    input_grad = input_gradient(tokens, middle_grad, rows_in, early, back_b, weights)

    input_grad, line_a, line_b, line_2 = after(input_grad, line_a, line_b, line_2)
    hidden_grads = hidden_end(block, rest, line_2, slot)
    one_grad = hidden_grads[0]
    qkv_grad, bias_grad, gain_grad, shift_grad = heads_end(total_a, line_a, total_b, line_b)
    _, two_grad, hidden_bias_grad, out_rows, *vector_grads = hidden_grads
    return (
        output,
        input_grad,
        gain_grad,
        shift_grad,
        qkv_grad,
        bias_grad,
        out_rows,
        vector_grads[2],
        vector_grads[0],
        vector_grads[1],
        one_grad,
        hidden_bias_grad,
        two_grad.T,
        vector_grads[3],
    )


def slow_end(output, input_grad, hidden, sends, slot):
    def scatter(values):
        values = lax.psum_scatter(wide(values), "tok", scatter_dimension=0, tiled=True)
        return lax.psum(values, "mlp")

    hidden = wide(hidden)
    blocks = jnp.concatenate([hidden[k, :, :INNER] for k in range(4)], axis=1)
    blocks = lax.psum_scatter(blocks, "tok", scatter_dimension=0, tiled=True)
    hidden_sum = lax.psum_scatter(blocks, "mlp", scatter_dimension=1, tiled=True)
    out_rows = scatter(hidden[4, :, :INNER].T)
    lines = slot // 128
    small = lax.psum(hidden[:, :48, INNER:], ("tok", "mlp"))
    bias_sum = lax.dynamic_index_in_dim(small[:4, :lines], lax.axis_index("mlp"), 0, False)
    small = small[4]
    weights = [scatter(s[:, :-SMALL]) for s in sends]
    smalls = [lax.psum(wide(s[:48, -SMALL:]), ("tok", "mlp")) for s in sends]
    return results(output, input_grad, weights, smalls, out_rows, small, hidden_sum, bias_sum)


def results(output, input_grad, weights, smalls, out_rows, small, hidden_sum, bias_sum):
    blocks = []
    for part in weights:
        blocks += [part[:, at : at + WIDE] for at in range(0, part.shape[1], WIDE)]
    qkv_grad = jnp.concatenate([block for k in range(3) for block in blocks[k::3]], axis=1)
    lines = WIDE // 128
    biases = []
    for part, weight in zip(smalls, weights):
        count = 2 * (weight.shape[1] // QKV)
        biases += [part[k * lines : (k + 1) * lines] for k in range(count)]
    bias_grad = jnp.concatenate(biases[0::2] + biases[1::2], axis=0).reshape(-1)
    norm_grad = smalls[0][40:46] + smalls[1][40:46]
    vectors = [small[3 * k : 3 * k + 3].reshape(-1) for k in range(4)]
    slot = hidden_sum.shape[1] // 2
    return (
        output,
        input_grad,
        norm_grad[:3].reshape(-1),
        norm_grad[3:].reshape(-1),
        qkv_grad,
        bias_grad,
        out_rows,
        vectors[2],
        vectors[0],
        vectors[1],
        hidden_sum[:, :slot],
        bias_sum.reshape(-1),
        hidden_sum[:, slot:].T,
        vectors[3],
    )


def solution(mesh):
    placed = (
        P(("tok", "mlp"), None),
        P(("tok", "mlp"), None),
        P(),
        P(),
        P("tok", None),
        P(),
        P("tok", None),
        P(),
        P(),
        P(),
        P("tok", "mlp"),
        P("mlp"),
        P("mlp", "tok"),
        P(),
        P(("tok", "mlp"), None),
    )
    return jax.shard_map(
        body,
        mesh=mesh,
        in_specs=placed,
        out_specs=(
            P(("tok", "mlp"), None),
            P(("tok", "mlp"), None),
            P(),
            P(),
            P("tok", None),
            P(),
            P("tok", None),
            P(),
            P(),
            P(),
            P("tok", "mlp"),
            P("mlp"),
            P("mlp", "tok"),
            P(),
        ),
        check_vma=False,
    )
```

```python
import functools

import jax
import jax.numpy as jnp
from jax import lax
from jax.experimental import pallas as pl
from jax.experimental.pallas import tpu as pltpu
from jax.sharding import PartitionSpec as P

HEADS = 16
HEAD_DIM = 64
FRAME_LEN = 196
LEN = 588
D = 384
FF = 2048
INNER = HEADS * HEAD_DIM
KEYS = 592
ROWS = 640
GROUP = 4
WIDE = GROUP * HEAD_DIM
GROUPS = HEADS // GROUP
QKV = 3 * WIDE
SMALL = 128
BLOCK = INNER + SMALL

epsilon = 1e-06
f32 = jnp.float32
bf16 = jnp.bfloat16

NN = (((1,), (0,)), ((), ()))
NT = (((1,), (1,)), ((), ()))
TN = (((0,), (0,)), ((), ()))

QUERY_BLOCKS = ((0, 128, 208), (128, 256, 400), (384, 256, 592))
KEY_RANGES = ((0, 208, 0), (208, 400, 128), (400, 592, 384))

VMEM = 56 * 1024 * 1024

BIAS_OUT, GAIN_TWO, SHIFT_TWO, BIAS_TWO, GAIN_ONE, SHIFT_ONE = (slice(k, k + 1) for k in range(6))


def dot(left, right, dims):
    return lax.dot_general(left, right, dims, preferred_element_type=f32)


def normalize(values):
    center = values - jnp.mean(values, axis=-1, keepdims=True)
    inverse = lax.rsqrt(jnp.mean(center * center, axis=-1, keepdims=True) + epsilon)
    return center * inverse, inverse


def normalize_back(grad_rows, norm_gain, scaled, inverse):
    scaled_grad = grad_rows * norm_gain
    return inverse * (
        scaled_grad
        - jnp.mean(scaled_grad, axis=-1, keepdims=True)
        - scaled * jnp.mean(scaled_grad * scaled, axis=-1, keepdims=True)
    )


def cost(micros):
    return pl.CostEstimate(flops=int(micros * 1.1e9), bytes_accessed=1024, transcendentals=0)


MASKS = (0, 2, 4, 6, 1, 3, 5, 7)


def owners(me, count):
    return [me ^ mask for mask in MASKS[:count]]


def staged_owners(me, count):
    if count == 1:
        return [0]
    first = 2 + 2 * (me & 1)
    second = 6 - first
    other = me ^ 1
    return [me, me ^ first, me ^ second, me ^ 6, other, other ^ second, other ^ first, other ^ 6]


def whole(shape):
    return pl.BlockSpec(
        shape, lambda *step: (0,) * len(shape), pipeline_mode=pl.Buffered(buffer_count=1)
    )


def prepare_kernel(one_ref, two_ref, hidden_bias_ref, out_ref, bias_ref, *refs):
    row_refs, (pack_ref, block_ref, rows_ref, columns_ref, wide_bias_ref) = refs[:6], refs[6:]
    rows, slot = one_ref.shape
    pack_ref[:rows, :slot] = one_ref[...]
    pack_ref[:rows, slot:] = two_ref[...]
    pack_ref[rows:] = jnp.zeros_like(pack_ref[rows:])
    pack_ref[rows : rows + 1, :slot] = hidden_bias_ref[...].reshape(1, slot)
    turned = out_ref[...].T
    width = turned.shape[1]
    for r in range(D // rows):
        block_ref[:, r * width : (r + 1) * width] = turned[r * rows : (r + 1) * rows]
    rows_ref[...] = jnp.zeros_like(rows_ref)
    for k, ref in enumerate(row_refs):
        rows_ref[k : k + 1] = ref[...].astype(f32).reshape(1, D)
    columns_ref[...] = rows_ref[...].T
    wide_bias_ref[...] = bias_ref[...].astype(f32).reshape(1, 2 * INNER)


def prepare(w_fc1, w_fc2, bias_fc1, w_out, bias_qv, vectors):
    rows, slot = w_fc1.shape
    return pl.pallas_call(
        prepare_kernel,
        out_shape=[
            jax.ShapeDtypeStruct((rows + 16, 2 * slot), bf16),
            jax.ShapeDtypeStruct((rows, INNER), bf16),
            jax.ShapeDtypeStruct((8, D), f32),
            jax.ShapeDtypeStruct((D, 8), f32),
            jax.ShapeDtypeStruct((1, 2 * INNER), f32),
        ],
        cost_estimate=cost(2),
        name="prepare",
    )(w_fc1, w_fc2.T, bias_fc1, w_out, bias_qv, *vectors)


def norm_kernel(tokens_ref, rows_ref, out_ref, scaled_ref):
    for s in range(out_ref.shape[0]):
        values = tokens_ref[s * LEN : (s + 1) * LEN].astype(f32)
        scaled, _ = normalize(values)
        normed = scaled * rows_ref[GAIN_ONE] + rows_ref[SHIFT_ONE]
        for ref, rows in ((scaled_ref, scaled), (out_ref, normed)):
            ref[s, :LEN] = rows.astype(bf16)
            ref[s, LEN:] = jnp.zeros((ROWS - LEN, D), bf16)


def first_norm(tokens, rows_in):
    seqs = tokens.shape[0] // LEN
    shape = jax.ShapeDtypeStruct((seqs, ROWS, D), bf16)
    return pl.pallas_call(
        norm_kernel,
        out_shape=[shape, shape],
        compiler_params=pltpu.CompilerParams(vmem_limit_bytes=10 * 1024 * 1024),
        cost_estimate=cost(2.5),
        name="first_norm",
    )(tokens, rows_in)


def attend_kernel(pieces, me_ref, normed_ref, bias_ref, mask_ref, *refs):
    parts, refs = refs[:pieces], refs[pieces:]
    projected_ref, mixed_ref, exp_ref, inverse_ref, wide_ref = refs[:5]
    hide_scr, score_scr, mixed_scr, total_scr, mask_scr = refs[5:]
    group, seq = pl.program_id(0), pl.program_id(1)

    @pl.when((group == 0) & (seq == 0))
    def _():
        rows = D // pieces
        for j, owner in enumerate(staged_owners(me_ref[0], pieces)):
            to = pl.ds(pl.multiple_of(owner * rows, 16), rows)
            for g in range(GROUPS):
                for k in range(3):
                    left = k * INNER + g * WIDE
                    at = g * QKV + k * WIDE
                    wide_ref[to, at : at + WIDE] = parts[j][:, left : left + WIDE]
        total_scr[...] = jnp.ones_like(total_scr)
        mask_scr[...] = jnp.zeros_like(mask_scr)
        count = hide_scr.shape[0]
        mask_scr[:count, :LEN] = mask_ref[...].astype(f32)
        turned = mask_scr[...].T
        key = lax.broadcasted_iota(jnp.int32, (KEYS, ROWS), 0)
        query = lax.broadcasted_iota(jnp.int32, (KEYS, ROWS), 1)
        later = ((query < FRAME_LEN) & (key >= FRAME_LEN)) | (
            (query < 2 * FRAME_LEN) & (key >= 2 * FRAME_LEN)
        )
        for s in range(count):
            usable = jnp.logical_not(later) & (turned[:KEYS, s : s + 1] > 0.5)
            hide_scr[s] = jnp.where(usable | (key == query), 0.0, -1e30)

    columns = pl.ds(pl.multiple_of(group * QKV, 128), QKV)
    projected = dot(normed_ref[seq, :KEYS], wide_ref[:, columns], NN)
    at = pl.multiple_of(group * WIDE, 128)
    queries = (projected[:, :WIDE] + bias_ref[:, pl.ds(at, WIDE)]).astype(bf16)
    projected_ref[0, :KEYS, :WIDE] = queries * bf16(HEAD_DIM**-0.5)
    projected_ref[0, :KEYS, WIDE : 2 * WIDE] = projected[:, WIDE : 2 * WIDE].astype(bf16)
    values = projected[:, 2 * WIDE :] + bias_ref[:, pl.ds(at + INNER, WIDE)]
    projected_ref[0, :KEYS, 2 * WIDE :] = values.astype(bf16)
    projected_ref[0, KEYS:] = jnp.zeros((ROWS - KEYS, QKV), bf16)
    from_ref = projected_ref.at[0]

    lane = lax.broadcasted_iota(jnp.int32, (1, 128), 1)
    units = [(h, b) for h in range(GROUP) for b in QUERY_BLOCKS]

    largest = {}
    flipped = {}

    def scores(unit):
        head, (start, width, keys) = units[unit]
        pair = head // 2 * 128
        mine = (lane < 64) if head % 2 == 0 else (lane >= 64)
        own_keys = from_ref[:keys, WIDE + pair : WIDE + pair + 128]
        own_keys = jnp.where(mine, own_keys, bf16(0))
        score = dot(own_keys, from_ref[start : start + width, pair : pair + 128], NT)
        score = score + hide_scr[seq, :keys, start : start + width]
        score_scr[unit % 3, :keys, :width] = score
        top = jnp.max(score.reshape(-1, 8, width), axis=0)
        largest[unit] = jnp.max(top, axis=0, keepdims=True)

    def exponents(unit):
        head, (start, width, keys) = units[unit]
        exponent = jnp.exp(score_scr[unit % 3, :keys, :width] - largest[unit])
        exp_ref[0, head, :keys, start : start + width] = exponent.astype(bf16)

    def mix(unit):
        head, (start, width, keys) = units[unit]
        pair = head // 2 * 128
        if head not in flipped:
            turned = from_ref[:KEYS, 2 * WIDE + pair : 2 * WIDE + pair + 128].T
            side = head % 2 * 64
            ones = jnp.ones((16, KEYS), bf16)
            flipped[head] = jnp.concatenate([turned[side : side + 64], ones])
        exponent = exp_ref[0, head, :keys, start : start + width]
        summed = dot(flipped[head][:, :keys], exponent, NN)
        values, total = summed[:64], summed[64:65]
        inverse = 1.0 / total
        mixed_scr[head * 64 : (head + 1) * 64, start : start + width] = values * inverse
        total_scr[head : head + 1, start : start + width] = inverse

    count = len(units)
    scores(0)
    scores(1)
    for unit in range(count + 2):
        if unit + 2 < count:
            scores(unit + 2)
        if unit < count:
            exponents(unit)
        if unit > 1:
            mix(unit - 2)
    mixed_ref[0] = mixed_scr[...].T.astype(bf16)
    inverse_ref[0, 0] = total_scr[...]


def attend(me, normed, parts, bias, mask):
    seqs = normed.shape[0]
    return pl.pallas_call(
        functools.partial(attend_kernel, len(parts)),
        grid=(GROUPS, seqs),
        in_specs=[
            pl.BlockSpec(memory_space=pltpu.SMEM),
            whole(normed.shape),
            whole(bias.shape),
            whole(mask.shape),
        ]
        + [whole(part.shape) for part in parts],
        out_specs=[
            pl.BlockSpec((1, ROWS, QKV), lambda g, s: (s, 0, g)),
            pl.BlockSpec((1, ROWS, WIDE), lambda g, s: (s, 0, g)),
            pl.BlockSpec((1, GROUP, KEYS, ROWS), lambda g, s: (s, g, 0, 0)),
            pl.BlockSpec((1, 1, 8, ROWS), lambda g, s: (s, g, 0, 0)),
            whole((D, GROUPS * QKV)),
        ],
        out_shape=[
            pltpu.HBM((seqs, ROWS, GROUPS * QKV), bf16),
            pltpu.VMEM((seqs, ROWS, INNER), bf16),
            pltpu.HBM((seqs, HEADS, KEYS, ROWS), bf16),
            pltpu.HBM((seqs, GROUPS, 8, ROWS), f32),
            pltpu.HBM((D, GROUPS * QKV), bf16),
        ],
        scratch_shapes=[
            pltpu.VMEM((seqs, KEYS, ROWS), f32),
            pltpu.VMEM((3, KEYS, 256), f32),
            pltpu.VMEM((WIDE, ROWS), f32),
            pltpu.VMEM((8, ROWS), f32),
            pltpu.VMEM((8, ROWS), f32),
        ],
        compiler_params=pltpu.CompilerParams(vmem_limit_bytes=24 * 1024 * 1024),
        cost_estimate=cost(22),
        name="attend",
    )(me, normed, bias, mask, *parts)


def forward_kernel(pieces, n_bias, chunk, me_ref, tokens_ref, grad_ref, rows_ref, *refs):
    bias_refs, refs = refs[:n_bias], refs[n_bias:]
    mixed_ref, refs = refs[0], refs[1:]
    parts, refs = refs[:pieces], refs[pieces:]
    out_ref, middle_grad_ref, branch_ref, out_wide_ref = refs[:4]
    n_out = 2 if pieces > 1 else 1
    send_refs, refs = refs[4 : 4 + n_out], refs[4 + n_out :]
    one_scr, two_scr, middle_scr, scaled_scr, inverse_scr, second_scr, second_t, grad_scr = refs[:8]
    grad_t, total_scr, back_scr, weight_scr, small_scr, bias_scr = refs[8:14]
    stage_scrs = (refs[14:16], refs[16:18])
    seqs = branch_ref.shape[0]
    step = pl.program_id(0)
    rows = D // pieces
    per_slot = FF // 4
    ones = jnp.ones((16, seqs * KEYS), bf16)

    def send(value_ref, at, width, left):
        if pieces == 1:
            send_refs[0][0, :, left : left + width] = value_ref[:, at : at + width].astype(bf16)
            return
        for j, owner in enumerate(owners(me_ref[0], pieces)):
            first = pl.multiple_of(owner * rows, 16)
            send_refs[j // 4][j % 4, 0, :, left : left + width] = value_ref[
                pl.ds(first, rows), at : at + width
            ].astype(bf16)

    def send_vectors():
        vectors = small_scr[...].astype(bf16)
        if pieces == 1:
            send_refs[0][0, :48, INNER:] = vectors
        else:
            for j in range(pieces):
                send_refs[j // 4][j % 4, 0, :, INNER:] = vectors

    def produce(index, stage):
        act_scr, pre_scr = stage_scrs[stage]
        hidden = pl.ds(pl.multiple_of(index * chunk, 128), chunk)
        pre = dot(second_scr[...], one_scr[:, hidden], NN) + bias_scr[:, hidden]
        half = 0.5 + 0.5 * lax.erf(pre * (0.5**0.5))
        act_scr[...] = (pre * half).astype(bf16)
        slope = half + pre * (jnp.exp2(pre * pre * -0.7213475204444817) * 0.3989422804014327)
        grad_act = dot(grad_scr[...], two_scr[:, hidden], NN)
        pre_scr[...] = (grad_act * slope).astype(bf16)

    def consume(index, stage):
        act_scr, pre_scr = stage_scrs[stage]
        hidden = pl.ds(pl.multiple_of(index * chunk, 128), chunk)
        total_scr[...] += dot(act_scr[...], two_scr[:, hidden], NT)
        back_scr[...] += dot(pre_scr[...], one_scr[:, hidden], NT)
        left = stage * chunk
        weight_scr[:, :chunk] = dot(second_t[...], pre_scr[...], NN)
        send(weight_scr, 0, chunk, left)
        weight_scr[:, chunk : 2 * chunk] = dot(grad_t[...], act_scr[...], NN)
        send(weight_scr, chunk, chunk, left + per_slot)
        hidden_sum = dot(ones, pre_scr[...], NN)[0:1]
        for r in range(chunk // 128):
            at = stage * (chunk // 128) + r
            small_scr[at : at + 1] = hidden_sum[:, r * 128 : (r + 1) * 128]

    @pl.when(step == 0)
    def _():
        for j, owner in enumerate(owners(me_ref[0], pieces)):
            first = pl.multiple_of(owner * rows, 16)
            if pieces == 1:
                out_wide_ref[...] = parts[0][:, :INNER]
            else:
                to = pl.ds(pl.multiple_of(owner * 128, 128), 128)
                for r in range(pieces):
                    out_wide_ref[r * rows : (r + 1) * rows, to] = parts[j][
                        :, r * 128 : (r + 1) * 128
                    ]
            for z in range(4):
                left = INNER + 2 * per_slot * z
                slot = slice(z * per_slot, (z + 1) * per_slot)
                one_scr[pl.ds(first, rows), slot] = parts[j][:, left : left + per_slot]
                two_scr[pl.ds(first, rows), slot] = parts[j][
                    :, left + per_slot : left + 2 * per_slot
                ]
        if n_bias == 1:
            bias_scr[...] = bias_refs[0][...].astype(f32)
        else:
            for z in range(4):
                row = bias_refs[z][rows : rows + 1, :per_slot]
                bias_scr[:, z * per_slot : (z + 1) * per_slot] = row.astype(f32)
        for s in range(seqs):
            block = slice(s * KEYS, (s + 1) * KEYS)
            real = slice(s * KEYS, s * KEYS + LEN)
            spare = slice(s * KEYS + LEN, (s + 1) * KEYS)
            given = slice(s * LEN, (s + 1) * LEN)
            grad_scr[real] = grad_ref[given]
            grad_scr[spare] = jnp.zeros((KEYS - LEN, D), bf16)
            middle_scr[real] = tokens_ref[given].astype(f32) + rows_ref[BIAS_OUT]
            middle_scr[spare] = jnp.zeros((KEYS - LEN, D), f32)
            middle = middle_scr[block] + dot(mixed_ref[s, :KEYS], out_wide_ref[...], NT)
            middle_scr[block] = middle
            scaled, inverse = normalize(middle)
            scaled_scr[block] = scaled
            inverse_scr[block] = inverse
            second_scr[block] = (scaled * rows_ref[GAIN_TWO] + rows_ref[SHIFT_TWO]).astype(bf16)
        second_t[...] = second_scr[...].T
        grad_t[...] = grad_scr[...].T
        total_scr[...] = jnp.zeros_like(total_scr)
        back_scr[...] = jnp.zeros_like(back_scr)
        small_scr[...] = jnp.zeros_like(small_scr)
        produce(0, 0)

    @pl.when(step < 4)
    def _():
        produce(2 * step + 1, 1)
        consume(2 * step, 0)
        produce(jnp.minimum(2 * step + 2, FF // chunk - 1), 0)
        consume(2 * step + 1, 1)
        send_vectors()

    @pl.when(step == 4)
    def _():
        sums = [jnp.zeros((1, D), f32) for _ in range(2)]
        for s in range(seqs):
            block = slice(s * KEYS, (s + 1) * KEYS)
            given = slice(s * LEN, (s + 1) * LEN)
            output = (middle_scr[block] + total_scr[block] + rows_ref[BIAS_TWO]).astype(bf16)
            out_ref[given] = output[:LEN]
            scaled, inverse = scaled_scr[block], inverse_scr[block]
            grad_second = back_scr[block]
            grad_middle = grad_scr[block].astype(f32) + normalize_back(
                grad_second, rows_ref[GAIN_TWO], scaled, inverse
            )
            middle_grad_ref[s, :KEYS] = grad_middle
            branch_ref[s, :KEYS] = grad_middle.astype(bf16)
            branch_ref[s, KEYS:] = jnp.zeros((ROWS - KEYS, D), bf16)
            for k, term in enumerate((grad_second * scaled, grad_second)):
                sums[k] = sums[k] + jnp.sum(term, axis=0, keepdims=True)
        branch = jnp.concatenate([branch_ref[s, :KEYS] for s in range(seqs)], axis=0)
        sums.append(dot(ones, branch, NN)[0:1])
        sums.append(dot(ones, grad_scr[...], NN)[0:1])
        for k in range(4):
            for r in range(D // 128):
                at = 3 * k + r
                small_scr[at : at + 1] = sums[k][:, r * 128 : (r + 1) * 128]
        mixed = jnp.concatenate([mixed_ref[s, :KEYS] for s in range(seqs)], axis=0)
        weight_scr[...] = dot(branch, mixed, TN)
        if pieces == 1:
            send_refs[0][0, :, :INNER] = weight_scr[...].astype(bf16)
        else:
            for j, owner in enumerate(owners(me_ref[0], pieces)):
                to = pl.ds(pl.multiple_of(owner * 128, 128), 128)
                for r in range(pieces):
                    send_refs[j // 4][j % 4, 0, :, r * 128 : (r + 1) * 128] = weight_scr[
                        r * rows : (r + 1) * rows, to
                    ].astype(bf16)
        send_vectors()


def forward(me, tokens, cotangent, rows_in, biases, mixed, parts):
    seqs = tokens.shape[0] // LEN
    pieces = len(parts)
    chunk = 256
    if pieces > 1:
        send_shapes = [(pieces // 2, 5, D // pieces, BLOCK)] * 2
        send_specs = [pl.BlockSpec((pieces // 2, 1, D // pieces, BLOCK), lambda c: (0, c, 0, 0))] * 2
    else:
        send_shapes = [(5, D, BLOCK)]
        send_specs = [pl.BlockSpec((1, D, BLOCK), lambda c: (c, 0, 0))]
    rows3 = (seqs, ROWS, D)
    rows2 = (seqs * KEYS, D)
    return pl.pallas_call(
        functools.partial(forward_kernel, pieces, len(biases), chunk),
        grid=(5,),
        in_specs=[
            pl.BlockSpec(memory_space=pltpu.SMEM),
            whole(tokens.shape),
            whole(tokens.shape),
            whole((8, D)),
        ]
        + [whole(b.shape) for b in biases]
        + [whole(mixed.shape)]
        + [whole(p.shape) for p in parts],
        out_specs=[whole(tokens.shape), whole(rows3), whole(rows3), whole((D, INNER))]
        + send_specs,
        out_shape=[
            jax.ShapeDtypeStruct(tokens.shape, bf16),
            jax.ShapeDtypeStruct(rows3, f32),
            pltpu.VMEM(rows3, bf16),
            pltpu.VMEM((D, INNER), bf16),
        ]
        + [pltpu.VMEM(s, bf16) for s in send_shapes],
        scratch_shapes=[
            pltpu.VMEM((D, FF), bf16),
            pltpu.VMEM((D, FF), bf16),
            pltpu.VMEM(rows2, f32),
            pltpu.VMEM(rows2, f32),
            pltpu.VMEM((seqs * KEYS, 1), f32),
            pltpu.VMEM(rows2, bf16),
            pltpu.VMEM((D, seqs * KEYS), bf16),
            pltpu.VMEM(rows2, bf16),
            pltpu.VMEM((D, seqs * KEYS), bf16),
            pltpu.VMEM(rows2, f32),
            pltpu.VMEM(rows2, f32),
            pltpu.VMEM((D, INNER), f32),
            pltpu.VMEM((48, 128), f32),
            pltpu.VMEM((1, FF), f32),
        ]
        + [pltpu.VMEM((seqs * KEYS, chunk), bf16)] * 4,
        compiler_params=pltpu.CompilerParams(vmem_limit_bytes=36 * 1024 * 1024),
        cost_estimate=cost(30),
        name="forward",
    )(me, tokens, cotangent, rows_in, *biases, mixed, *parts)


def mixed_gradient_kernel(branch_ref, out_wide_ref, mixed_ref, grad_ref, delta_ref):
    lane = lax.broadcasted_iota(jnp.int32, (8, WIDE), 1)
    gather = (lane >> 6 == lax.broadcasted_iota(jnp.int32, (8, WIDE), 0)).astype(bf16)
    for g in range(delta_ref.shape[1]):
        columns = slice(g * WIDE, (g + 1) * WIDE)
        grad = dot(branch_ref[0], out_wide_ref[:, columns], NN).astype(bf16)
        grad_ref[0, :, columns] = grad
        product = grad.astype(f32) * mixed_ref[0, :, columns].astype(f32)
        first = product.astype(bf16)
        second = (product - first.astype(f32)).astype(bf16)
        delta_ref[0, g] = dot(gather, first, NT) + dot(gather, second, NT)


def mixed_gradient(branch, out_wide, mixed):
    seqs = branch.shape[0]
    each = 2
    columns = pl.BlockSpec((1, ROWS, each * WIDE), lambda s, g: (s, 0, g))
    return pl.pallas_call(
        mixed_gradient_kernel,
        grid=(seqs, GROUPS // each),
        in_specs=[
            pl.BlockSpec((1, ROWS, D), lambda s, g: (s, 0, 0)),
            pl.BlockSpec((D, each * WIDE), lambda s, g: (0, g)),
            columns,
        ],
        out_specs=[columns, pl.BlockSpec((1, each, 8, ROWS), lambda s, g: (s, g, 0, 0))],
        out_shape=[
            pltpu.HBM((seqs, ROWS, INNER), bf16),
            pltpu.HBM((seqs, GROUPS, 8, ROWS), f32),
        ],
        compiler_params=pltpu.CompilerParams(vmem_limit_bytes=16 * 1024 * 1024),
        cost_estimate=cost(5),
        name="mixed_gradient",
    )(branch, out_wide, mixed)


def backward_kernel(pieces, me_ref, *refs):
    grad_ref, delta_ref, scaled_ref, projected_ref, exp_ref, inverse_ref = refs[:6]
    wide_ref, norm_ref = refs[6:8]
    refs = refs[8:]
    n_out = 2 if pieces > 1 else 1
    back_ref = refs[0]
    send_refs = refs[1 : 1 + n_out]
    grad_scr, prob_scr, turned_scr, weight_scr, small_scr, sum_scr, norm_scr = refs[1 + n_out :]
    group, seq = pl.program_id(0), pl.program_id(1)
    groups, seqs = pl.num_programs(0), pl.num_programs(1)
    rows = D // pieces

    @pl.when((group == 0) & (seq == 0))
    def _():
        small_scr[...] = jnp.zeros_like(small_scr)
        norm_scr[...] = jnp.zeros_like(norm_scr)

    lane = lax.broadcasted_iota(jnp.int32, (1, 128), 1)
    low = lane < 64
    kept = {}
    for pair in range(GROUP // 2):
        columns = slice(pair * 128, pair * 128 + 128)
        grad = grad_ref[0, :, columns]
        query = projected_ref[0, :, columns]
        value = projected_ref[0, :KEYS, 2 * WIDE + pair * 128 : 2 * WIDE + pair * 128 + 128]
        turned = projected_ref[0, :KEYS, WIDE + pair * 128 : WIDE + pair * 128 + 128].T
        for half in range(2):
            head = 2 * pair + half
            mine = low if half == 0 else jnp.logical_not(low)
            own_value = jnp.where(mine, value, bf16(0))
            inverse = inverse_ref[0, 0, head : head + 1].astype(bf16)
            delta = delta_ref[0, 0, head : head + 1]
            side = slice(64 * half, 64 * half + 64)
            for start, width, keys in QUERY_BLOCKS:
                block = slice(start, start + width)
                change = dot(own_value[:keys], grad[block], NT) - delta[:, block]
                probability = exp_ref[0, head, :keys, block] * inverse[:, block]
                prob_scr[half, :keys, block] = probability
                grad_scr[half, :keys, block] = probability * change.astype(bf16)
            for start, width, keys in QUERY_BLOCKS:
                block = slice(start, start + width)
                turned_scr[head * 64 : (head + 1) * 64, block] = dot(
                    turned[side, :keys], grad_scr[half, :keys, block], NN
                ) * (HEAD_DIM**-0.5)
            for start, stop, seen in KEY_RANGES:
                value_grad = dot(prob_scr[half, start:stop, seen:], grad[seen:], NN)
                key_grad = dot(grad_scr[half, start:stop, seen:], query[seen:], NN)
                if half == 0:
                    kept[start] = (value_grad, key_grad)
                else:
                    at = slice(WIDE + pair * 128, WIDE + pair * 128 + 128)
                    back_ref[0, start:stop, at] = jnp.where(low, kept[start][1], key_grad).astype(
                        bf16
                    )
                    at = slice(2 * WIDE + pair * 128, 2 * WIDE + pair * 128 + 128)
                    back_ref[0, start:stop, at] = jnp.where(low, kept[start][0], value_grad).astype(
                        bf16
                    )
    back_ref[0, :KEYS, :WIDE] = turned_scr[...].T[:KEYS].astype(bf16)

    back = back_ref[0, :KEYS]
    weight = dot(scaled_ref[0, :KEYS], back, TN)
    total = dot(jnp.ones((16, KEYS), bf16), back, NN)[0:1]

    @pl.when(seq == 0)
    def _():
        weight_scr[...] = weight
        sum_scr[0:1] = total

    @pl.when(seq > 0)
    def _():
        weight_scr[...] += weight
        sum_scr[0:1] += total

    @pl.when(seq == seqs - 1)
    def _():
        sums = sum_scr[0:1]
        for r in range(WIDE // 128):
            at = group * (2 * WIDE // 128) + r
            small_scr[pl.ds(at, 1)] = sums[:, r * 128 : r * 128 + 128]
            at = at + WIDE // 128
            small_scr[pl.ds(at, 1)] = sums[:, 2 * WIDE + r * 128 : 2 * WIDE + r * 128 + 128]
        wide = wide_ref[...].astype(f32)
        scaled_weight = weight_scr[...]
        norm_scr[:, 0:1] += jnp.sum(scaled_weight * wide, axis=1, keepdims=True)
        norm_scr[:, 1:2] += jnp.sum(sums * wide, axis=1, keepdims=True)
        weight_scr[...] = scaled_weight * norm_ref[:, GAIN_ONE] + sums * norm_ref[:, SHIFT_ONE]
        start = pl.multiple_of(group * QKV, 128)
        if pieces == 1:
            send_refs[0][:, pl.ds(start, QKV)] = weight_scr[...].astype(bf16)
        else:
            for j, owner in enumerate(owners(me_ref[0], pieces)):
                first = pl.multiple_of(owner * rows, 16)
                send_refs[j // 4][j % 4, :, pl.ds(start, QKV)] = weight_scr[
                    pl.ds(first, rows)
                ].astype(bf16)

    @pl.when((group == groups - 1) & (seq == seqs - 1))
    def _():
        turned = norm_scr[...].T
        for k in range(2):
            for r in range(D // 128):
                small_scr[40 + 3 * k + r : 41 + 3 * k + r] = turned[
                    k : k + 1, r * 128 : (r + 1) * 128
                ]
        small = small_scr[...].astype(bf16)
        if pieces == 1:
            send_refs[0][:48, send_refs[0].shape[1] - SMALL :] = small
        else:
            for j in range(pieces):
                edge = send_refs[0].shape[2] - SMALL
                send_refs[j // 4][j % 4, :, edge:] = small


def backward(me, pieces, first_group, groups, grads, scaled, norm, saved):
    operands = [
        pltpu.with_memory_space_constraint(x, pltpu.HBM)
        for x in (*grads, scaled, saved[0], saved[2], saved[3], saved[4])
    ]
    seqs = scaled.shape[0]
    width = groups * QKV + SMALL
    if pieces > 1:
        send_shapes = [(pieces // 2, D // pieces, width)] * 2
    else:
        send_shapes = [(D, width)]
    columns = pl.BlockSpec((1, ROWS, WIDE), lambda g, s: (s, 0, g + first_group))
    heads = pl.BlockSpec((1, 1, 8, ROWS), lambda g, s: (s, g + first_group, 0, 0))
    rows_block = pl.BlockSpec((1, ROWS, D), lambda g, s: (s, 0, 0))
    return pl.pallas_call(
        functools.partial(backward_kernel, pieces),
        grid=(groups, seqs),
        in_specs=[
            pl.BlockSpec(memory_space=pltpu.SMEM),
            columns,
            heads,
            rows_block,
            pl.BlockSpec((1, ROWS, QKV), lambda g, s: (s, 0, g + first_group)),
            pl.BlockSpec((1, GROUP, KEYS, ROWS), lambda g, s: (s, g + first_group, 0, 0)),
            heads,
            pl.BlockSpec((D, QKV), lambda g, s: (0, g + first_group)),
            whole((D, 8)),
        ],
        out_specs=[pl.BlockSpec((1, ROWS, QKV), lambda g, s: (s, 0, g))]
        + [whole(s) for s in send_shapes],
        out_shape=[jax.ShapeDtypeStruct((seqs, ROWS, groups * QKV), bf16)]
        + [jax.ShapeDtypeStruct(s, bf16) for s in send_shapes],
        scratch_shapes=[
            pltpu.VMEM((2, KEYS, ROWS), bf16),
            pltpu.VMEM((2, KEYS, ROWS), bf16),
            pltpu.VMEM((WIDE, ROWS), f32),
            pltpu.VMEM((D, QKV), f32),
            pltpu.VMEM((48, 128), f32),
            pltpu.VMEM((8, QKV), f32),
            pltpu.VMEM((D, 128), f32),
        ],
        compiler_params=pltpu.CompilerParams(vmem_limit_bytes=23 * 1024 * 1024),
        cost_estimate=cost(11 * groups),
        name="backward",
    )(me, *operands, norm)


def early_kernel(back_ref, wide_ref, out_ref):
    for s in range(out_ref.shape[0]):
        grad = dot(back_ref[s, :KEYS], wide_ref[...], NT)
        before = jnp.where(pl.program_id(0) == 0, 0.0, out_ref[s])
        out_ref[s] = before + grad


def early_gradient(back, weights):
    seqs, groups = back.shape[0], back.shape[2] // QKV
    return pl.pallas_call(
        early_kernel,
        grid=(groups,),
        in_specs=[
            pl.BlockSpec((seqs, ROWS, QKV), lambda g: (0, 0, g)),
            pl.BlockSpec((D, QKV), lambda g: (0, g)),
        ],
        out_specs=whole((seqs, KEYS, D)),
        out_shape=jax.ShapeDtypeStruct((seqs, KEYS, D), f32),
        compiler_params=pltpu.CompilerParams(vmem_limit_bytes=14 * 1024 * 1024),
        cost_estimate=cost(5),
        name="early_gradient",
    )(back, weights)


def input_kernel(tokens_ref, middle_grad_ref, rows_ref, early_ref, back_ref, wide_ref, out_ref):
    for s in range(middle_grad_ref.shape[0]):
        grad_first = early_ref[s] + dot(back_ref[s, :KEYS], wide_ref[...], NT)
        given = slice(s * LEN, (s + 1) * LEN)
        scaled, inverse = normalize(tokens_ref[given].astype(f32))
        out_ref[given] = middle_grad_ref[s, :LEN] + normalize_back(
            grad_first[:LEN], rows_ref[GAIN_ONE], scaled, inverse
        )


def input_gradient(tokens, middle_grad, rows_in, early, back, weights):
    return pl.pallas_call(
        input_kernel,
        grid=(1,),
        in_specs=[
            whole(tokens.shape),
            whole(middle_grad.shape),
            whole(rows_in.shape),
            whole(early.shape),
            whole(back.shape),
            pl.BlockSpec((D, QKV), lambda g: (0, GROUPS - 1)),
        ],
        out_specs=whole(tokens.shape),
        out_shape=jax.ShapeDtypeStruct(tokens.shape, f32),
        compiler_params=pltpu.CompilerParams(vmem_limit_bytes=16 * 1024 * 1024),
        cost_estimate=cost(4),
        name="input_gradient",
    )(tokens, middle_grad, rows_in, early, back, weights)


def join_lines(values):
    return jnp.concatenate([values[k : k + 1] for k in range(values.shape[0])], axis=1)


def hidden_end_kernel(block_ref, rest_ref, arrived_ref, one_ref, two_ref, bias_ref, out_ref, *refs):
    rows, slot = one_ref.shape
    block = block_ref[...] + arrived_ref[:, :BLOCK].astype(f32)
    rest = rest_ref[...] + arrived_ref[:, BLOCK:].astype(f32)
    one_ref[...] = block[:, :slot]
    two_ref[...] = block[:, slot : 2 * slot]
    bias_ref[...] = join_lines(block[: slot // 128, INNER:]).reshape(slot)
    width = out_ref.shape[0]
    parts = [rest[:, r * width : (r + 1) * width] for r in range(INNER // width)]
    out_ref[...] = jnp.concatenate(parts, axis=0).T
    for k, ref in enumerate(refs):
        ref[...] = join_lines(rest[3 * k : 3 * k + 3, INNER:]).reshape(D)


def hidden_end(block, rest, arrived, slot):
    rows = block.shape[0]
    width = INNER // (D // rows)
    vector = jax.ShapeDtypeStruct((D,), f32)
    return pl.pallas_call(
        hidden_end_kernel,
        out_shape=[
            jax.ShapeDtypeStruct((rows, slot), f32),
            jax.ShapeDtypeStruct((rows, slot), f32),
            jax.ShapeDtypeStruct((slot,), f32),
            jax.ShapeDtypeStruct((width, D), f32),
        ]
        + [vector] * 4,
        compiler_params=pltpu.CompilerParams(vmem_limit_bytes=8 * 1024 * 1024),
        cost_estimate=cost(2),
        name="hidden_end",
    )(block, rest, arrived)


def heads_end_kernel(early_ref, early_line_ref, late_ref, late_line_ref, weight_ref, bias_ref, *refs):
    early = early_ref[...] + early_line_ref[...].astype(f32)
    late = late_ref[...] + late_line_ref[...].astype(f32)
    lines = WIDE // 128
    norms, group = 0.0, 0
    for part in (early, late):
        edge = part.shape[1] - SMALL
        for g in range(edge // QKV):
            for k in range(3):
                left = g * QKV + k * WIDE
                to = k * INNER + group * WIDE
                weight_ref[:, to : to + WIDE] = part[:, left : left + WIDE]
            for k in range(2):
                first = (2 * g + k) * lines
                values = join_lines(part[first : first + lines, edge:])
                at = k * INNER + group * WIDE
                bias_ref[at : at + WIDE] = values.reshape(WIDE)
            group += 1
        norms = norms + part[40:48, edge:]
    for k, ref in enumerate(refs):
        ref[...] = join_lines(norms[3 * k : 3 * k + 3]).reshape(D)


def heads_end(early, early_line, late, late_line):
    vector = jax.ShapeDtypeStruct((D,), f32)
    return pl.pallas_call(
        heads_end_kernel,
        out_shape=[
            jax.ShapeDtypeStruct((early.shape[0], 3 * INNER), f32),
            jax.ShapeDtypeStruct((2 * INNER,), f32),
            vector,
            vector,
        ],
        compiler_params=pltpu.CompilerParams(vmem_limit_bytes=8 * 1024 * 1024),
        cost_estimate=cost(2),
        name="heads_end",
    )(early, early_line, late, late_line)


def swap(values, mask):
    size = lax.axis_size("tok")
    return lax.ppermute(values, "tok", [(i, i ^ mask) for i in range(size)])


def swap_half_plane(values, stage):
    size = lax.axis_size("tok")
    pairs = [(t, t ^ (2 if (t % 2 == 0) == (stage == 0) else 4)) for t in range(size)]
    return lax.ppermute(values, "tok", pairs)


def swap_half_line(values, stage):
    tok, mlp = lax.axis_size("tok"), lax.axis_size("mlp")
    pairs = []
    for t in range(tok):
        for z in range(mlp):
            far = (t % 2 == 0) == (stage == 0)
            pairs.append((t * mlp + z, t * mlp + (z ^ (2 if far else 1))))
    return lax.ppermute(values.astype(bf16), ("tok", "mlp"), pairs)


def after(values, *earlier):
    return lax.optimization_barrier((values,) + earlier)


def wide(values):
    return values.astype(f32)


def join(kept, arrived):
    return (wide(kept) + wide(arrived)).astype(bf16)


def body(
    tokens,
    action_mask,
    ln1_gain,
    ln1_bias,
    w_qkv,
    bias_qv,
    w_out,
    bias_out,
    ln2_gain,
    ln2_bias,
    w_fc1,
    bias_fc1,
    w_fc2,
    bias_fc2,
    out_grad,
):
    rows = w_qkv.shape[0]
    tok = lax.axis_size("tok")
    mlp = lax.axis_size("mlp")
    slot = w_fc1.shape[1]
    fast = tok == 8 and mlp == 4
    pieces = tok if fast else 1
    me = lax.axis_index("tok").astype(jnp.int32).reshape(1)
    chips = (2, 4, 6)
    odd = (me[0] & 1) == 1

    def pick(if_odd, if_even):
        return jnp.where(odd, if_odd, if_even)


    vectors = (bias_out, ln2_gain, ln2_bias, bias_fc2, ln1_gain, ln1_bias)
    me_a = me
    if fast:
        first_near = [swap_half_plane(w_qkv, stage) for stage in (0, 1)]
        first_near.append(swap_half_plane(first_near[0], 1))
        first_other = swap(w_qkv, 1)
        hidden_pack, out_block, rows_in, columns_in, bias_pair = prepare(
            w_fc1, w_fc2, bias_fc1, w_out, bias_qv, vectors
        )
        line = jnp.stack([hidden_pack, swap_half_line(hidden_pack, 0)])
        line = jnp.concatenate([line, swap_half_line(line, 1)])
        line = [line[0], pick(line[1], line[2]), pick(line[2], line[1]), line[3]]
        norm_tokens, first_near[0] = after(tokens, first_near[0])
        normed, scaled = first_norm(norm_tokens, rows_in)
        first_parts = [w_qkv] + first_near + [first_other] + [swap(p, 1) for p in first_near]
        hidden_own = jnp.concatenate([out_block] + [part[:rows] for part in line], axis=1)
        me_a, hidden_own = after(me, hidden_own)
        hidden_near = [swap(hidden_own, mask) for mask in chips + (1,)]
        biases = line
    else:
        rows_in = jnp.pad(wide(jnp.stack(vectors)), ((0, 2), (0, 0)))
        columns_in = rows_in.T
        bias_pair = wide(bias_qv).reshape(1, -1)
        normed, scaled = first_norm(tokens, rows_in)
        first_parts = [lax.all_gather(w_qkv, "tok", axis=0, tiled=True)]
        line = lax.all_gather(jnp.concatenate([w_fc1, w_fc2.T], axis=1), "mlp", axis=1, tiled=True)
        line = lax.all_gather(line, "tok", axis=0, tiled=True)
        biases = [lax.all_gather(bias_fc1, "mlp", axis=0, tiled=True).reshape(1, -1)]
        out_all = lax.all_gather(w_out, "tok", axis=0, tiled=True).T
        hidden_parts = [jnp.concatenate([out_all, line], axis=1)]

    saved = list(attend(me_a, normed, first_parts, bias_pair, action_mask))
    weights = saved[4]
    if fast:
        saved[1], *hidden_near = after(saved[1], *hidden_near)
        hidden_other = hidden_near.pop()
        hidden_parts = [hidden_own] + hidden_near + [hidden_other]
        hidden_parts = hidden_parts + [swap(part, 1) for part in hidden_near]

    output, middle_grad, branch, out_wide, *hidden_sends = forward(
        me, tokens, out_grad, rows_in, biases, saved[1], hidden_parts
    )

    grads = list(mixed_gradient(branch, out_wide, saved[1]))

    def back(me, group, count):
        return backward(me, pieces, group, count, grads, scaled, columns_in, saved)

    if not fast:
        back_a, sends_a = back(me, 0, 3)
        back_b, sends_b = back(me, 3, 1)
        early = early_gradient(back_a, weights)
        input_grad = input_gradient(tokens, middle_grad, rows_in, early, back_b, weights)
        return slow_end(output, input_grad, hidden_sends[0], (sends_a, sends_b), slot)

    arrived = swap(hidden_sends[1], 1)
    grads[0], arrived = after(grads[0], arrived)
    hidden = join(hidden_sends[0], arrived)
    me_1, hidden = after(me, hidden)
    near = [swap(hidden[k], chips[k - 1]) for k in (1, 2, 3)]
    back_a, *sends_a = back(me_1, 0, 3)

    back_a, *near = after(back_a, *near)
    hidden = wide(hidden[0]) + wide(near[0]) + wide(near[1]) + wide(near[2])
    sent = jnp.stack([pick(hidden[1], hidden[2]), hidden[3], hidden[4]]).astype(bf16)
    group_a = join(sends_a[0], swap(sends_a[1], 1))
    me_2, group_a, sent = after(me, group_a, sent)
    line_1 = swap_half_line(sent, 0)
    near_a = [swap(group_a[k], chips[k - 1]) for k in (1, 2, 3)]
    back_b, *sends_b = back(me_2, 3, 1)

    back_b, line_1, *near_a = after(back_b, line_1, *near_a)
    total_a = wide(group_a[0]) + wide(near_a[0]) + wide(near_a[1]) + wide(near_a[2])
    sent, kept_b, sent_b = after(total_a.astype(bf16), *sends_b)
    line_a = swap_half_line(sent, 1)
    group_b = join(kept_b, swap(sent_b, 1))
    line_1, group_b = after(line_1, group_b)
    block = hidden[0] + wide(line_1[0])
    middle_block = pick(hidden[2], hidden[1]) + wide(line_1[1])
    rest = hidden[4] + wide(line_1[2])
    sent = jnp.concatenate([middle_block, rest], axis=1).astype(bf16)
    group_b, sent = after(group_b, sent)
    line_2 = swap_half_line(sent, 1)
    near_b = [swap(group_b[k], chips[k - 1]) for k in (1, 2, 3)]
    line_a, *near_b = after(line_a, *near_b)
    total_b = wide(group_b[0]) + wide(near_b[0]) + wide(near_b[1]) + wide(near_b[2])
    total_a = total_a + wide(line_a)
    back_a, sent_b, sent_a = after(back_a, total_b.astype(bf16), total_a.astype(bf16))
    line_b = swap_half_line(sent_b, 0)
    line_a = swap_half_line(sent_a, 0)
    early = early_gradient(back_a, weights)

    early, line_b = after(early, line_b)
    total_b = total_b + wide(line_b)
    early, sent = after(early, total_b.astype(bf16))
    line_b = swap_half_line(sent, 1)
    input_grad = input_gradient(tokens, middle_grad, rows_in, early, back_b, weights)

    input_grad, line_a, line_b, line_2 = after(input_grad, line_a, line_b, line_2)
    hidden_grads = hidden_end(block, rest, line_2, slot)
    one_grad = hidden_grads[0]
    qkv_grad, bias_grad, gain_grad, shift_grad = heads_end(total_a, line_a, total_b, line_b)
    _, two_grad, hidden_bias_grad, out_rows, *vector_grads = hidden_grads
    return (
        output,
        input_grad,
        gain_grad,
        shift_grad,
        qkv_grad,
        bias_grad,
        out_rows,
        vector_grads[2],
        vector_grads[0],
        vector_grads[1],
        one_grad,
        hidden_bias_grad,
        two_grad.T,
        vector_grads[3],
    )


def slow_end(output, input_grad, hidden, sends, slot):
    def scatter(values):
        values = lax.psum_scatter(wide(values), "tok", scatter_dimension=0, tiled=True)
        return lax.psum(values, "mlp")

    hidden = wide(hidden)
    blocks = jnp.concatenate([hidden[k, :, :INNER] for k in range(4)], axis=1)
    blocks = lax.psum_scatter(blocks, "tok", scatter_dimension=0, tiled=True)
    hidden_sum = lax.psum_scatter(blocks, "mlp", scatter_dimension=1, tiled=True)
    out_rows = scatter(hidden[4, :, :INNER].T)
    lines = slot // 128
    small = lax.psum(hidden[:, :48, INNER:], ("tok", "mlp"))
    bias_sum = lax.dynamic_index_in_dim(small[:4, :lines], lax.axis_index("mlp"), 0, False)
    small = small[4]
    weights = [scatter(s[:, :-SMALL]) for s in sends]
    smalls = [lax.psum(wide(s[:48, -SMALL:]), ("tok", "mlp")) for s in sends]
    return results(output, input_grad, weights, smalls, out_rows, small, hidden_sum, bias_sum)


def results(output, input_grad, weights, smalls, out_rows, small, hidden_sum, bias_sum):
    blocks = []
    for part in weights:
        blocks += [part[:, at : at + WIDE] for at in range(0, part.shape[1], WIDE)]
    qkv_grad = jnp.concatenate([block for k in range(3) for block in blocks[k::3]], axis=1)
    lines = WIDE // 128
    biases = []
    for part, weight in zip(smalls, weights):
        count = 2 * (weight.shape[1] // QKV)
        biases += [part[k * lines : (k + 1) * lines] for k in range(count)]
    bias_grad = jnp.concatenate(biases[0::2] + biases[1::2], axis=0).reshape(-1)
    norm_grad = smalls[0][40:46] + smalls[1][40:46]
    vectors = [small[3 * k : 3 * k + 3].reshape(-1) for k in range(4)]
    slot = hidden_sum.shape[1] // 2
    return (
        output,
        input_grad,
        norm_grad[:3].reshape(-1),
        norm_grad[3:].reshape(-1),
        qkv_grad,
        bias_grad,
        out_rows,
        vectors[2],
        vectors[0],
        vectors[1],
        hidden_sum[:, :slot],
        bias_sum.reshape(-1),
        hidden_sum[:, slot:].T,
        vectors[3],
    )


def solution(mesh):
    placed = (
        P(("tok", "mlp"), None),
        P(("tok", "mlp"), None),
        P(),
        P(),
        P("tok", None),
        P(),
        P("tok", None),
        P(),
        P(),
        P(),
        P("tok", "mlp"),
        P("mlp"),
        P("mlp", "tok"),
        P(),
        P(("tok", "mlp"), None),
    )
    return jax.shard_map(
        body,
        mesh=mesh,
        in_specs=placed,
        out_specs=(
            P(("tok", "mlp"), None),
            P(("tok", "mlp"), None),
            P(),
            P(),
            P("tok", None),
            P(),
            P("tok", None),
            P(),
            P(),
            P(),
            P("tok", "mlp"),
            P("mlp"),
            P("mlp", "tok"),
            P(),
        ),
        check_vma=False,
    )
```

```python
import functools

import jax
import jax.numpy as jnp
from jax import lax
from jax.experimental import pallas as pl
from jax.experimental.pallas import tpu as pltpu
from jax.sharding import PartitionSpec as P

HEADS = 16
HEAD_DIM = 64
FRAME_LEN = 196
LEN = 588
D = 384
FF = 2048
INNER = HEADS * HEAD_DIM
KEYS = 592
ROWS = 640
GROUP = 4
WIDE = GROUP * HEAD_DIM
GROUPS = HEADS // GROUP
QKV = 3 * WIDE
SMALL = 128
BLOCK = INNER + SMALL

epsilon = 1e-06
f32 = jnp.float32
bf16 = jnp.bfloat16

NN = (((1,), (0,)), ((), ()))
NT = (((1,), (1,)), ((), ()))
TN = (((0,), (0,)), ((), ()))

QUERY_BLOCKS = ((0, 128, 208), (128, 256, 400), (384, 256, 592))
KEY_RANGES = ((0, 208, 0), (208, 400, 128), (400, 592, 384))

VMEM = 56 * 1024 * 1024

BIAS_OUT, GAIN_TWO, SHIFT_TWO, BIAS_TWO, GAIN_ONE, SHIFT_ONE = (slice(k, k + 1) for k in range(6))


def dot(left, right, dims):
    return lax.dot_general(left, right, dims, preferred_element_type=f32)


def normalize(values):
    center = values - jnp.mean(values, axis=-1, keepdims=True)
    inverse = lax.rsqrt(jnp.mean(center * center, axis=-1, keepdims=True) + epsilon)
    return center * inverse, inverse


def normalize_back(grad_rows, norm_gain, scaled, inverse):
    scaled_grad = grad_rows * norm_gain
    return inverse * (
        scaled_grad
        - jnp.mean(scaled_grad, axis=-1, keepdims=True)
        - scaled * jnp.mean(scaled_grad * scaled, axis=-1, keepdims=True)
    )


def cost(micros):
    return pl.CostEstimate(flops=int(micros * 1.1e9), bytes_accessed=1024, transcendentals=0)


MASKS = (0, 2, 4, 6, 1, 3, 5, 7)


def owners(me, count):
    return [me ^ mask for mask in MASKS[:count]]


def staged_owners(me, count):
    if count == 1:
        return [0]
    first = 2 + 2 * (me & 1)
    second = 6 - first
    other = me ^ 1
    return [me, me ^ first, me ^ second, me ^ 6, other, other ^ second, other ^ first, other ^ 6]


def whole(shape):
    return pl.BlockSpec(
        shape, lambda *step: (0,) * len(shape), pipeline_mode=pl.Buffered(buffer_count=1)
    )


def prepare_kernel(one_ref, two_ref, hidden_bias_ref, out_ref, bias_ref, *refs):
    row_refs, (pack_ref, block_ref, rows_ref, columns_ref, wide_bias_ref) = refs[:6], refs[6:]
    rows, slot = one_ref.shape
    pack_ref[:rows, :slot] = one_ref[...]
    pack_ref[:rows, slot:] = two_ref[...]
    pack_ref[rows:] = jnp.zeros_like(pack_ref[rows:])
    pack_ref[rows : rows + 1, :slot] = hidden_bias_ref[...].reshape(1, slot)
    turned = out_ref[...].T
    width = turned.shape[1]
    for r in range(D // rows):
        block_ref[:, r * width : (r + 1) * width] = turned[r * rows : (r + 1) * rows]
    rows_ref[...] = jnp.zeros_like(rows_ref)
    for k, ref in enumerate(row_refs):
        rows_ref[k : k + 1] = ref[...].astype(f32).reshape(1, D)
    columns_ref[...] = rows_ref[...].T
    wide_bias_ref[...] = bias_ref[...].astype(f32).reshape(1, 2 * INNER)


def prepare(w_fc1, w_fc2, bias_fc1, w_out, bias_qv, vectors):
    rows, slot = w_fc1.shape
    return pl.pallas_call(
        prepare_kernel,
        out_shape=[
            jax.ShapeDtypeStruct((rows + 16, 2 * slot), bf16),
            jax.ShapeDtypeStruct((rows, INNER), bf16),
            jax.ShapeDtypeStruct((8, D), f32),
            jax.ShapeDtypeStruct((D, 8), f32),
            jax.ShapeDtypeStruct((1, 2 * INNER), f32),
        ],
        cost_estimate=cost(2),
        name="prepare",
    )(w_fc1, w_fc2.T, bias_fc1, w_out, bias_qv, *vectors)


def norm_kernel(tokens_ref, rows_ref, out_ref, scaled_ref):
    for s in range(out_ref.shape[0]):
        values = tokens_ref[s * LEN : (s + 1) * LEN].astype(f32)
        scaled, _ = normalize(values)
        normed = scaled * rows_ref[GAIN_ONE] + rows_ref[SHIFT_ONE]
        for ref, rows in ((scaled_ref, scaled), (out_ref, normed)):
            ref[s, :LEN] = rows.astype(bf16)
            ref[s, LEN:] = jnp.zeros((ROWS - LEN, D), bf16)


def first_norm(tokens, rows_in):
    seqs = tokens.shape[0] // LEN
    shape = jax.ShapeDtypeStruct((seqs, ROWS, D), bf16)
    return pl.pallas_call(
        norm_kernel,
        out_shape=[shape, shape],
        compiler_params=pltpu.CompilerParams(vmem_limit_bytes=10 * 1024 * 1024),
        cost_estimate=cost(2.5),
        name="first_norm",
    )(tokens, rows_in)


def attend_kernel(pieces, me_ref, normed_ref, bias_ref, mask_ref, *refs):
    parts, refs = refs[:pieces], refs[pieces:]
    projected_ref, mixed_ref, exp_ref, inverse_ref, wide_ref = refs[:5]
    hide_scr, score_scr, mixed_scr, total_scr, mask_scr = refs[5:]
    group, seq = pl.program_id(0), pl.program_id(1)

    @pl.when((group == 0) & (seq == 0))
    def _():
        rows = D // pieces
        for j, owner in enumerate(staged_owners(me_ref[0], pieces)):
            to = pl.ds(pl.multiple_of(owner * rows, 16), rows)
            for g in range(GROUPS):
                for k in range(3):
                    left = k * INNER + g * WIDE
                    at = g * QKV + k * WIDE
                    wide_ref[to, at : at + WIDE] = parts[j][:, left : left + WIDE]
        total_scr[...] = jnp.ones_like(total_scr)
        mask_scr[...] = jnp.zeros_like(mask_scr)
        count = hide_scr.shape[0]
        mask_scr[:count, :LEN] = mask_ref[...].astype(f32)
        turned = mask_scr[...].T
        key = lax.broadcasted_iota(jnp.int32, (KEYS, ROWS), 0)
        query = lax.broadcasted_iota(jnp.int32, (KEYS, ROWS), 1)
        later = ((query < FRAME_LEN) & (key >= FRAME_LEN)) | (
            (query < 2 * FRAME_LEN) & (key >= 2 * FRAME_LEN)
        )
        for s in range(count):
            usable = jnp.logical_not(later) & (turned[:KEYS, s : s + 1] > 0.5)
            hide_scr[s] = jnp.where(usable | (key == query), 0.0, -1e30)

    columns = pl.ds(pl.multiple_of(group * QKV, 128), QKV)
    projected = dot(normed_ref[seq, :KEYS], wide_ref[:, columns], NN)
    at = pl.multiple_of(group * WIDE, 128)
    queries = (projected[:, :WIDE] + bias_ref[:, pl.ds(at, WIDE)]).astype(bf16)
    projected_ref[0, :KEYS, :WIDE] = queries * bf16(HEAD_DIM**-0.5)
    projected_ref[0, :KEYS, WIDE : 2 * WIDE] = projected[:, WIDE : 2 * WIDE].astype(bf16)
    values = projected[:, 2 * WIDE :] + bias_ref[:, pl.ds(at + INNER, WIDE)]
    projected_ref[0, :KEYS, 2 * WIDE :] = values.astype(bf16)
    projected_ref[0, KEYS:] = jnp.zeros((ROWS - KEYS, QKV), bf16)
    from_ref = projected_ref.at[0]

    lane = lax.broadcasted_iota(jnp.int32, (1, 128), 1)
    units = [(h, b) for h in range(GROUP) for b in QUERY_BLOCKS]

    largest = {}
    flipped = {}

    def scores(unit):
        head, (start, width, keys) = units[unit]
        pair = head // 2 * 128
        mine = (lane < 64) if head % 2 == 0 else (lane >= 64)
        own_keys = from_ref[:keys, WIDE + pair : WIDE + pair + 128]
        own_keys = jnp.where(mine, own_keys, bf16(0))
        score = dot(own_keys, from_ref[start : start + width, pair : pair + 128], NT)
        score = score + hide_scr[seq, :keys, start : start + width]
        score_scr[unit % 3, :keys, :width] = score
        top = jnp.max(score.reshape(-1, 8, width), axis=0)
        largest[unit] = jnp.max(top, axis=0, keepdims=True)

    def exponents(unit):
        head, (start, width, keys) = units[unit]
        exponent = jnp.exp(score_scr[unit % 3, :keys, :width] - largest[unit])
        exp_ref[0, head, :keys, start : start + width] = exponent.astype(bf16)

    def mix(unit):
        head, (start, width, keys) = units[unit]
        pair = head // 2 * 128
        if head not in flipped:
            turned = from_ref[:KEYS, 2 * WIDE + pair : 2 * WIDE + pair + 128].T
            side = head % 2 * 64
            ones = jnp.ones((16, KEYS), bf16)
            flipped[head] = jnp.concatenate([turned[side : side + 64], ones])
        exponent = exp_ref[0, head, :keys, start : start + width]
        summed = dot(flipped[head][:, :keys], exponent, NN)
        values, total = summed[:64], summed[64:65]
        inverse = 1.0 / total
        mixed_scr[head * 64 : (head + 1) * 64, start : start + width] = values * inverse
        total_scr[head : head + 1, start : start + width] = inverse

    count = len(units)
    scores(0)
    scores(1)
    for unit in range(count + 2):
        if unit + 2 < count:
            scores(unit + 2)
        if unit < count:
            exponents(unit)
        if unit > 1:
            mix(unit - 2)
    mixed_ref[0] = mixed_scr[...].T.astype(bf16)
    inverse_ref[0, 0] = total_scr[...]


def attend(me, normed, parts, bias, mask):
    seqs = normed.shape[0]
    return pl.pallas_call(
        functools.partial(attend_kernel, len(parts)),
        grid=(GROUPS, seqs),
        in_specs=[
            pl.BlockSpec(memory_space=pltpu.SMEM),
            whole(normed.shape),
            whole(bias.shape),
            whole(mask.shape),
        ]
        + [whole(part.shape) for part in parts],
        out_specs=[
            pl.BlockSpec((1, ROWS, QKV), lambda g, s: (s, 0, g)),
            pl.BlockSpec((1, ROWS, WIDE), lambda g, s: (s, 0, g)),
            pl.BlockSpec((1, GROUP, KEYS, ROWS), lambda g, s: (s, g, 0, 0)),
            pl.BlockSpec((1, 1, 8, ROWS), lambda g, s: (s, g, 0, 0)),
            whole((D, GROUPS * QKV)),
        ],
        out_shape=[
            pltpu.HBM((seqs, ROWS, GROUPS * QKV), bf16),
            pltpu.VMEM((seqs, ROWS, INNER), bf16),
            pltpu.HBM((seqs, HEADS, KEYS, ROWS), bf16),
            pltpu.HBM((seqs, GROUPS, 8, ROWS), f32),
            pltpu.HBM((D, GROUPS * QKV), bf16),
        ],
        scratch_shapes=[
            pltpu.VMEM((seqs, KEYS, ROWS), f32),
            pltpu.VMEM((3, KEYS, 256), f32),
            pltpu.VMEM((WIDE, ROWS), f32),
            pltpu.VMEM((8, ROWS), f32),
            pltpu.VMEM((8, ROWS), f32),
        ],
        compiler_params=pltpu.CompilerParams(vmem_limit_bytes=24 * 1024 * 1024),
        cost_estimate=cost(22),
        name="attend",
    )(me, normed, bias, mask, *parts)


def forward_kernel(pieces, n_bias, chunk, me_ref, tokens_ref, grad_ref, rows_ref, *refs):
    bias_refs, refs = refs[:n_bias], refs[n_bias:]
    mixed_ref, refs = refs[0], refs[1:]
    parts, refs = refs[:pieces], refs[pieces:]
    out_ref, middle_grad_ref, branch_ref, out_wide_ref = refs[:4]
    n_out = 2 if pieces > 1 else 1
    send_refs, refs = refs[4 : 4 + n_out], refs[4 + n_out :]
    one_scr, two_scr, middle_scr, scaled_scr, inverse_scr, second_scr, second_t, grad_scr = refs[:8]
    grad_t, total_scr, back_scr, weight_scr, small_scr, bias_scr = refs[8:14]
    stage_scrs = (refs[14:16], refs[16:18])
    seqs = branch_ref.shape[0]
    step = pl.program_id(0)
    rows = D // pieces
    per_slot = FF // 4
    ones = jnp.ones((16, seqs * KEYS), bf16)

    def send(value_ref, at, width, left):
        if pieces == 1:
            send_refs[0][0, :, left : left + width] = value_ref[:, at : at + width].astype(bf16)
            return
        for j, owner in enumerate(owners(me_ref[0], pieces)):
            first = pl.multiple_of(owner * rows, 16)
            send_refs[j // 4][j % 4, 0, :, left : left + width] = value_ref[
                pl.ds(first, rows), at : at + width
            ].astype(bf16)

    def send_vectors():
        vectors = small_scr[...].astype(bf16)
        if pieces == 1:
            send_refs[0][0, :48, INNER:] = vectors
        else:
            for j in range(pieces):
                send_refs[j // 4][j % 4, 0, :, INNER:] = vectors

    def produce(index, stage):
        act_scr, pre_scr = stage_scrs[stage]
        hidden = pl.ds(pl.multiple_of(index * chunk, 128), chunk)
        pre = dot(second_scr[...], one_scr[:, hidden], NN) + bias_scr[:, hidden]
        half = 0.5 + 0.5 * lax.erf(pre * (0.5**0.5))
        act_scr[...] = (pre * half).astype(bf16)
        slope = half + pre * (jnp.exp2(pre * pre * -0.7213475204444817) * 0.3989422804014327)
        grad_act = dot(grad_scr[...], two_scr[:, hidden], NN)
        pre_scr[...] = (grad_act * slope).astype(bf16)

    def consume(index, stage):
        act_scr, pre_scr = stage_scrs[stage]
        hidden = pl.ds(pl.multiple_of(index * chunk, 128), chunk)
        total_scr[...] += dot(act_scr[...], two_scr[:, hidden], NT)
        back_scr[...] += dot(pre_scr[...], one_scr[:, hidden], NT)
        left = stage * chunk
        weight_scr[:, :chunk] = dot(second_t[...], pre_scr[...], NN)
        send(weight_scr, 0, chunk, left)
        weight_scr[:, chunk : 2 * chunk] = dot(grad_t[...], act_scr[...], NN)
        send(weight_scr, chunk, chunk, left + per_slot)
        hidden_sum = dot(ones, pre_scr[...], NN)[0:1]
        for r in range(chunk // 128):
            at = stage * (chunk // 128) + r
            small_scr[at : at + 1] = hidden_sum[:, r * 128 : (r + 1) * 128]

    @pl.when(step == 0)
    def _():
        for j, owner in enumerate(owners(me_ref[0], pieces)):
            first = pl.multiple_of(owner * rows, 16)
            if pieces == 1:
                out_wide_ref[...] = parts[0][:, :INNER]
            else:
                to = pl.ds(pl.multiple_of(owner * 128, 128), 128)
                for r in range(pieces):
                    out_wide_ref[r * rows : (r + 1) * rows, to] = parts[j][
                        :, r * 128 : (r + 1) * 128
                    ]
            for z in range(4):
                left = INNER + 2 * per_slot * z
                slot = slice(z * per_slot, (z + 1) * per_slot)
                one_scr[pl.ds(first, rows), slot] = parts[j][:, left : left + per_slot]
                two_scr[pl.ds(first, rows), slot] = parts[j][
                    :, left + per_slot : left + 2 * per_slot
                ]
        if n_bias == 1:
            bias_scr[...] = bias_refs[0][...].astype(f32)
        else:
            for z in range(4):
                row = bias_refs[z][rows : rows + 1, :per_slot]
                bias_scr[:, z * per_slot : (z + 1) * per_slot] = row.astype(f32)
        for s in range(seqs):
            block = slice(s * KEYS, (s + 1) * KEYS)
            real = slice(s * KEYS, s * KEYS + LEN)
            spare = slice(s * KEYS + LEN, (s + 1) * KEYS)
            given = slice(s * LEN, (s + 1) * LEN)
            grad_scr[real] = grad_ref[given]
            grad_scr[spare] = jnp.zeros((KEYS - LEN, D), bf16)
            middle_scr[real] = tokens_ref[given].astype(f32) + rows_ref[BIAS_OUT]
            middle_scr[spare] = jnp.zeros((KEYS - LEN, D), f32)
            middle = middle_scr[block] + dot(mixed_ref[s, :KEYS], out_wide_ref[...], NT)
            middle_scr[block] = middle
            scaled, inverse = normalize(middle)
            scaled_scr[block] = scaled
            inverse_scr[block] = inverse
            second_scr[block] = (scaled * rows_ref[GAIN_TWO] + rows_ref[SHIFT_TWO]).astype(bf16)
        second_t[...] = second_scr[...].T
        grad_t[...] = grad_scr[...].T
        total_scr[...] = jnp.zeros_like(total_scr)
        back_scr[...] = jnp.zeros_like(back_scr)
        small_scr[...] = jnp.zeros_like(small_scr)
        produce(0, 0)

    @pl.when(step < 4)
    def _():
        produce(2 * step + 1, 1)
        consume(2 * step, 0)
        produce(jnp.minimum(2 * step + 2, FF // chunk - 1), 0)
        consume(2 * step + 1, 1)
        send_vectors()

    @pl.when(step == 4)
    def _():
        sums = [jnp.zeros((1, D), f32) for _ in range(2)]
        for s in range(seqs):
            block = slice(s * KEYS, (s + 1) * KEYS)
            given = slice(s * LEN, (s + 1) * LEN)
            output = (middle_scr[block] + total_scr[block] + rows_ref[BIAS_TWO]).astype(bf16)
            out_ref[given] = output[:LEN]
            scaled, inverse = scaled_scr[block], inverse_scr[block]
            grad_second = back_scr[block]
            grad_middle = grad_scr[block].astype(f32) + normalize_back(
                grad_second, rows_ref[GAIN_TWO], scaled, inverse
            )
            middle_grad_ref[s, :KEYS] = grad_middle
            branch_ref[s, :KEYS] = grad_middle.astype(bf16)
            branch_ref[s, KEYS:] = jnp.zeros((ROWS - KEYS, D), bf16)
            for k, term in enumerate((grad_second * scaled, grad_second)):
                sums[k] = sums[k] + jnp.sum(term, axis=0, keepdims=True)
        branch = jnp.concatenate([branch_ref[s, :KEYS] for s in range(seqs)], axis=0)
        sums.append(dot(ones, branch, NN)[0:1])
        sums.append(dot(ones, grad_scr[...], NN)[0:1])
        for k in range(4):
            for r in range(D // 128):
                at = 3 * k + r
                small_scr[at : at + 1] = sums[k][:, r * 128 : (r + 1) * 128]
        mixed = jnp.concatenate([mixed_ref[s, :KEYS] for s in range(seqs)], axis=0)
        weight_scr[...] = dot(branch, mixed, TN)
        if pieces == 1:
            send_refs[0][0, :, :INNER] = weight_scr[...].astype(bf16)
        else:
            for j, owner in enumerate(owners(me_ref[0], pieces)):
                to = pl.ds(pl.multiple_of(owner * 128, 128), 128)
                for r in range(pieces):
                    send_refs[j // 4][j % 4, 0, :, r * 128 : (r + 1) * 128] = weight_scr[
                        r * rows : (r + 1) * rows, to
                    ].astype(bf16)
        send_vectors()


def forward(me, tokens, cotangent, rows_in, biases, mixed, parts):
    seqs = tokens.shape[0] // LEN
    pieces = len(parts)
    chunk = 256
    if pieces > 1:
        send_shapes = [(pieces // 2, 5, D // pieces, BLOCK)] * 2
        send_specs = [pl.BlockSpec((pieces // 2, 1, D // pieces, BLOCK), lambda c: (0, c, 0, 0))] * 2
    else:
        send_shapes = [(5, D, BLOCK)]
        send_specs = [pl.BlockSpec((1, D, BLOCK), lambda c: (c, 0, 0))]
    rows3 = (seqs, ROWS, D)
    rows2 = (seqs * KEYS, D)
    return pl.pallas_call(
        functools.partial(forward_kernel, pieces, len(biases), chunk),
        grid=(5,),
        in_specs=[
            pl.BlockSpec(memory_space=pltpu.SMEM),
            whole(tokens.shape),
            whole(tokens.shape),
            whole((8, D)),
        ]
        + [whole(b.shape) for b in biases]
        + [whole(mixed.shape)]
        + [whole(p.shape) for p in parts],
        out_specs=[whole(tokens.shape), whole(rows3), whole(rows3), whole((D, INNER))]
        + send_specs,
        out_shape=[
            jax.ShapeDtypeStruct(tokens.shape, bf16),
            jax.ShapeDtypeStruct(rows3, f32),
            pltpu.VMEM(rows3, bf16),
            pltpu.VMEM((D, INNER), bf16),
        ]
        + [pltpu.VMEM(s, bf16) for s in send_shapes],
        scratch_shapes=[
            pltpu.VMEM((D, FF), bf16),
            pltpu.VMEM((D, FF), bf16),
            pltpu.VMEM(rows2, f32),
            pltpu.VMEM(rows2, f32),
            pltpu.VMEM((seqs * KEYS, 1), f32),
            pltpu.VMEM(rows2, bf16),
            pltpu.VMEM((D, seqs * KEYS), bf16),
            pltpu.VMEM(rows2, bf16),
            pltpu.VMEM((D, seqs * KEYS), bf16),
            pltpu.VMEM(rows2, f32),
            pltpu.VMEM(rows2, f32),
            pltpu.VMEM((D, INNER), f32),
            pltpu.VMEM((48, 128), f32),
            pltpu.VMEM((1, FF), f32),
        ]
        + [pltpu.VMEM((seqs * KEYS, chunk), bf16)] * 4,
        compiler_params=pltpu.CompilerParams(vmem_limit_bytes=36 * 1024 * 1024),
        cost_estimate=cost(30),
        name="forward",
    )(me, tokens, cotangent, rows_in, *biases, mixed, *parts)


def mixed_gradient_kernel(branch_ref, out_wide_ref, mixed_ref, grad_ref, delta_ref):
    lane = lax.broadcasted_iota(jnp.int32, (8, WIDE), 1)
    gather = (lane >> 6 == lax.broadcasted_iota(jnp.int32, (8, WIDE), 0)).astype(bf16)
    for g in range(delta_ref.shape[1]):
        columns = slice(g * WIDE, (g + 1) * WIDE)
        grad = dot(branch_ref[0], out_wide_ref[:, columns], NN).astype(bf16)
        grad_ref[0, :, columns] = grad
        product = grad.astype(f32) * mixed_ref[0, :, columns].astype(f32)
        first = product.astype(bf16)
        second = (product - first.astype(f32)).astype(bf16)
        delta_ref[0, g] = dot(gather, first, NT) + dot(gather, second, NT)


def mixed_gradient(branch, out_wide, mixed):
    seqs = branch.shape[0]
    each = 2
    columns = pl.BlockSpec((1, ROWS, each * WIDE), lambda s, g: (s, 0, g))
    return pl.pallas_call(
        mixed_gradient_kernel,
        grid=(seqs, GROUPS // each),
        in_specs=[
            pl.BlockSpec((1, ROWS, D), lambda s, g: (s, 0, 0)),
            pl.BlockSpec((D, each * WIDE), lambda s, g: (0, g)),
            columns,
        ],
        out_specs=[columns, pl.BlockSpec((1, each, 8, ROWS), lambda s, g: (s, g, 0, 0))],
        out_shape=[
            pltpu.HBM((seqs, ROWS, INNER), bf16),
            pltpu.HBM((seqs, GROUPS, 8, ROWS), f32),
        ],
        compiler_params=pltpu.CompilerParams(vmem_limit_bytes=16 * 1024 * 1024),
        cost_estimate=cost(5),
        name="mixed_gradient",
    )(branch, out_wide, mixed)


def backward_kernel(pieces, me_ref, *refs):
    grad_ref, delta_ref, scaled_ref, projected_ref, exp_ref, inverse_ref = refs[:6]
    wide_ref, norm_ref = refs[6:8]
    refs = refs[8:]
    n_out = 2 if pieces > 1 else 1
    back_ref = refs[0]
    send_refs = refs[1 : 1 + n_out]
    grad_scr, prob_scr, turned_scr, weight_scr, small_scr, sum_scr, norm_scr = refs[1 + n_out :]
    group, seq = pl.program_id(0), pl.program_id(1)
    groups, seqs = pl.num_programs(0), pl.num_programs(1)
    rows = D // pieces

    @pl.when((group == 0) & (seq == 0))
    def _():
        small_scr[...] = jnp.zeros_like(small_scr)
        norm_scr[...] = jnp.zeros_like(norm_scr)

    lane = lax.broadcasted_iota(jnp.int32, (1, 128), 1)
    low = lane < 64
    kept = {}
    turned_keys = {}

    def parts(head):
        columns = slice(head // 2 * 128, head // 2 * 128 + 128)
        return columns, head % 2, grad_ref[0, :, columns]

    def score_gradients(head):
        columns, half, grad = parts(head)
        mine = low if half == 0 else jnp.logical_not(low)
        value = projected_ref[0, :KEYS, 2 * WIDE + columns.start : 2 * WIDE + columns.stop]
        own_value = jnp.where(mine, value, bf16(0))
        inverse = inverse_ref[0, 0, head : head + 1].astype(bf16)
        delta = delta_ref[0, 0, head : head + 1]
        for start, width, keys in QUERY_BLOCKS:
            block = slice(start, start + width)
            change = dot(own_value[:keys], grad[block], NT) - delta[:, block]
            probability = exp_ref[0, head, :keys, block] * inverse[:, block]
            prob_scr[half, :keys, block] = probability
            grad_scr[half, :keys, block] = probability * change.astype(bf16)

    def input_gradients(head):
        columns, half, grad = parts(head)
        pair = head // 2
        query = projected_ref[0, :, columns]
        if half == 0:
            turned_keys[pair] = projected_ref[0, :KEYS, WIDE + columns.start : WIDE + columns.stop].T
        turned = turned_keys[pair]
        side = slice(64 * half, 64 * half + 64)
        for start, width, keys in QUERY_BLOCKS:
            block = slice(start, start + width)
            turned_scr[head * 64 : (head + 1) * 64, block] = dot(
                turned[side, :keys], grad_scr[half, :keys, block], NN
            ) * (HEAD_DIM**-0.5)
        for start, stop, seen in KEY_RANGES:
            value_grad = dot(prob_scr[half, start:stop, seen:], grad[seen:], NN)
            key_grad = dot(grad_scr[half, start:stop, seen:], query[seen:], NN)
            if half == 0:
                kept[start] = (value_grad, key_grad)
            else:
                at = slice(WIDE + columns.start, WIDE + columns.stop)
                back_ref[0, start:stop, at] = jnp.where(low, kept[start][1], key_grad).astype(bf16)
                at = slice(2 * WIDE + columns.start, 2 * WIDE + columns.stop)
                back_ref[0, start:stop, at] = jnp.where(low, kept[start][0], value_grad).astype(bf16)

    score_gradients(0)
    for head in range(GROUP):
        if head + 1 < GROUP:
            score_gradients(head + 1)
        input_gradients(head)
    back_ref[0, :KEYS, :WIDE] = turned_scr[...].T[:KEYS].astype(bf16)

    back = back_ref[0, :KEYS]
    weight = dot(scaled_ref[0, :KEYS], back, TN)
    total = dot(jnp.ones((16, KEYS), bf16), back, NN)[0:1]

    @pl.when(seq == 0)
    def _():
        weight_scr[...] = weight
        sum_scr[0:1] = total

    @pl.when(seq > 0)
    def _():
        weight_scr[...] += weight
        sum_scr[0:1] += total

    @pl.when(seq == seqs - 1)
    def _():
        sums = sum_scr[0:1]
        for r in range(WIDE // 128):
            at = group * (2 * WIDE // 128) + r
            small_scr[pl.ds(at, 1)] = sums[:, r * 128 : r * 128 + 128]
            at = at + WIDE // 128
            small_scr[pl.ds(at, 1)] = sums[:, 2 * WIDE + r * 128 : 2 * WIDE + r * 128 + 128]
        wide = wide_ref[...].astype(f32)
        scaled_weight = weight_scr[...]
        norm_scr[:, 0:1] += jnp.sum(scaled_weight * wide, axis=1, keepdims=True)
        norm_scr[:, 1:2] += jnp.sum(sums * wide, axis=1, keepdims=True)
        weight_scr[...] = scaled_weight * norm_ref[:, GAIN_ONE] + sums * norm_ref[:, SHIFT_ONE]
        start = pl.multiple_of(group * QKV, 128)
        if pieces == 1:
            send_refs[0][:, pl.ds(start, QKV)] = weight_scr[...].astype(bf16)
        else:
            for j, owner in enumerate(owners(me_ref[0], pieces)):
                first = pl.multiple_of(owner * rows, 16)
                send_refs[j // 4][j % 4, :, pl.ds(start, QKV)] = weight_scr[
                    pl.ds(first, rows)
                ].astype(bf16)

    @pl.when((group == groups - 1) & (seq == seqs - 1))
    def _():
        turned = norm_scr[...].T
        for k in range(2):
            for r in range(D // 128):
                small_scr[40 + 3 * k + r : 41 + 3 * k + r] = turned[
                    k : k + 1, r * 128 : (r + 1) * 128
                ]
        small = small_scr[...].astype(bf16)
        if pieces == 1:
            send_refs[0][:48, send_refs[0].shape[1] - SMALL :] = small
        else:
            for j in range(pieces):
                edge = send_refs[0].shape[2] - SMALL
                send_refs[j // 4][j % 4, :, edge:] = small


def backward(me, pieces, first_group, groups, grads, scaled, norm, saved):
    operands = [
        pltpu.with_memory_space_constraint(x, pltpu.HBM)
        for x in (*grads, scaled, saved[0], saved[2], saved[3], saved[4])
    ]
    seqs = scaled.shape[0]
    width = groups * QKV + SMALL
    if pieces > 1:
        send_shapes = [(pieces // 2, D // pieces, width)] * 2
    else:
        send_shapes = [(D, width)]
    columns = pl.BlockSpec((1, ROWS, WIDE), lambda g, s: (s, 0, g + first_group))
    heads = pl.BlockSpec((1, 1, 8, ROWS), lambda g, s: (s, g + first_group, 0, 0))
    rows_block = pl.BlockSpec((1, ROWS, D), lambda g, s: (s, 0, 0))
    return pl.pallas_call(
        functools.partial(backward_kernel, pieces),
        grid=(groups, seqs),
        in_specs=[
            pl.BlockSpec(memory_space=pltpu.SMEM),
            columns,
            heads,
            rows_block,
            pl.BlockSpec((1, ROWS, QKV), lambda g, s: (s, 0, g + first_group)),
            pl.BlockSpec((1, GROUP, KEYS, ROWS), lambda g, s: (s, g + first_group, 0, 0)),
            heads,
            pl.BlockSpec((D, QKV), lambda g, s: (0, g + first_group)),
            whole((D, 8)),
        ],
        out_specs=[pl.BlockSpec((1, ROWS, QKV), lambda g, s: (s, 0, g))]
        + [whole(s) for s in send_shapes],
        out_shape=[jax.ShapeDtypeStruct((seqs, ROWS, groups * QKV), bf16)]
        + [jax.ShapeDtypeStruct(s, bf16) for s in send_shapes],
        scratch_shapes=[
            pltpu.VMEM((2, KEYS, ROWS), bf16),
            pltpu.VMEM((2, KEYS, ROWS), bf16),
            pltpu.VMEM((WIDE, ROWS), f32),
            pltpu.VMEM((D, QKV), f32),
            pltpu.VMEM((48, 128), f32),
            pltpu.VMEM((8, QKV), f32),
            pltpu.VMEM((D, 128), f32),
        ],
        compiler_params=pltpu.CompilerParams(vmem_limit_bytes=23 * 1024 * 1024),
        cost_estimate=cost(11 * groups),
        name="backward",
    )(me, *operands, norm)


def early_kernel(back_ref, wide_ref, out_ref):
    for s in range(out_ref.shape[0]):
        grad = dot(back_ref[s, :KEYS], wide_ref[...], NT)
        before = jnp.where(pl.program_id(0) == 0, 0.0, out_ref[s])
        out_ref[s] = before + grad


def early_gradient(back, weights):
    seqs, groups = back.shape[0], back.shape[2] // QKV
    return pl.pallas_call(
        early_kernel,
        grid=(groups,),
        in_specs=[
            pl.BlockSpec((seqs, ROWS, QKV), lambda g: (0, 0, g)),
            pl.BlockSpec((D, QKV), lambda g: (0, g)),
        ],
        out_specs=whole((seqs, KEYS, D)),
        out_shape=jax.ShapeDtypeStruct((seqs, KEYS, D), f32),
        compiler_params=pltpu.CompilerParams(vmem_limit_bytes=14 * 1024 * 1024),
        cost_estimate=cost(5),
        name="early_gradient",
    )(back, weights)


def input_kernel(tokens_ref, middle_grad_ref, rows_ref, early_ref, back_ref, wide_ref, out_ref):
    for s in range(middle_grad_ref.shape[0]):
        grad_first = early_ref[s] + dot(back_ref[s, :KEYS], wide_ref[...], NT)
        given = slice(s * LEN, (s + 1) * LEN)
        scaled, inverse = normalize(tokens_ref[given].astype(f32))
        out_ref[given] = middle_grad_ref[s, :LEN] + normalize_back(
            grad_first[:LEN], rows_ref[GAIN_ONE], scaled, inverse
        )


def input_gradient(tokens, middle_grad, rows_in, early, back, weights):
    return pl.pallas_call(
        input_kernel,
        grid=(1,),
        in_specs=[
            whole(tokens.shape),
            whole(middle_grad.shape),
            whole(rows_in.shape),
            whole(early.shape),
            whole(back.shape),
            pl.BlockSpec((D, QKV), lambda g: (0, GROUPS - 1)),
        ],
        out_specs=whole(tokens.shape),
        out_shape=jax.ShapeDtypeStruct(tokens.shape, f32),
        compiler_params=pltpu.CompilerParams(vmem_limit_bytes=16 * 1024 * 1024),
        cost_estimate=cost(4),
        name="input_gradient",
    )(tokens, middle_grad, rows_in, early, back, weights)


def join_lines(values):
    return jnp.concatenate([values[k : k + 1] for k in range(values.shape[0])], axis=1)


def hidden_end_kernel(block_ref, rest_ref, arrived_ref, one_ref, two_ref, bias_ref, out_ref, *refs):
    rows, slot = one_ref.shape
    block = block_ref[...] + arrived_ref[:, :BLOCK].astype(f32)
    rest = rest_ref[...] + arrived_ref[:, BLOCK:].astype(f32)
    one_ref[...] = block[:, :slot]
    two_ref[...] = block[:, slot : 2 * slot]
    bias_ref[...] = join_lines(block[: slot // 128, INNER:]).reshape(slot)
    width = out_ref.shape[0]
    parts = [rest[:, r * width : (r + 1) * width] for r in range(INNER // width)]
    out_ref[...] = jnp.concatenate(parts, axis=0).T
    for k, ref in enumerate(refs):
        ref[...] = join_lines(rest[3 * k : 3 * k + 3, INNER:]).reshape(D)


def hidden_end(block, rest, arrived, slot):
    rows = block.shape[0]
    width = INNER // (D // rows)
    vector = jax.ShapeDtypeStruct((D,), f32)
    return pl.pallas_call(
        hidden_end_kernel,
        out_shape=[
            jax.ShapeDtypeStruct((rows, slot), f32),
            jax.ShapeDtypeStruct((rows, slot), f32),
            jax.ShapeDtypeStruct((slot,), f32),
            jax.ShapeDtypeStruct((width, D), f32),
        ]
        + [vector] * 4,
        compiler_params=pltpu.CompilerParams(vmem_limit_bytes=8 * 1024 * 1024),
        cost_estimate=cost(2),
        name="hidden_end",
    )(block, rest, arrived)


def heads_end_kernel(early_ref, early_line_ref, late_ref, late_line_ref, weight_ref, bias_ref, *refs):
    early = early_ref[...] + early_line_ref[...].astype(f32)
    late = late_ref[...] + late_line_ref[...].astype(f32)
    lines = WIDE // 128
    norms, group = 0.0, 0
    for part in (early, late):
        edge = part.shape[1] - SMALL
        for g in range(edge // QKV):
            for k in range(3):
                left = g * QKV + k * WIDE
                to = k * INNER + group * WIDE
                weight_ref[:, to : to + WIDE] = part[:, left : left + WIDE]
            for k in range(2):
                first = (2 * g + k) * lines
                values = join_lines(part[first : first + lines, edge:])
                at = k * INNER + group * WIDE
                bias_ref[at : at + WIDE] = values.reshape(WIDE)
            group += 1
        norms = norms + part[40:48, edge:]
    for k, ref in enumerate(refs):
        ref[...] = join_lines(norms[3 * k : 3 * k + 3]).reshape(D)


def heads_end(early, early_line, late, late_line):
    vector = jax.ShapeDtypeStruct((D,), f32)
    return pl.pallas_call(
        heads_end_kernel,
        out_shape=[
            jax.ShapeDtypeStruct((early.shape[0], 3 * INNER), f32),
            jax.ShapeDtypeStruct((2 * INNER,), f32),
            vector,
            vector,
        ],
        compiler_params=pltpu.CompilerParams(vmem_limit_bytes=8 * 1024 * 1024),
        cost_estimate=cost(2),
        name="heads_end",
    )(early, early_line, late, late_line)


def swap(values, mask):
    size = lax.axis_size("tok")
    return lax.ppermute(values, "tok", [(i, i ^ mask) for i in range(size)])


def swap_half_plane(values, stage):
    size = lax.axis_size("tok")
    pairs = [(t, t ^ (2 if (t % 2 == 0) == (stage == 0) else 4)) for t in range(size)]
    return lax.ppermute(values, "tok", pairs)


def swap_half_line(values, stage):
    tok, mlp = lax.axis_size("tok"), lax.axis_size("mlp")
    pairs = []
    for t in range(tok):
        for z in range(mlp):
            far = (t % 2 == 0) == (stage == 0)
            pairs.append((t * mlp + z, t * mlp + (z ^ (2 if far else 1))))
    return lax.ppermute(values.astype(bf16), ("tok", "mlp"), pairs)


def after(values, *earlier):
    return lax.optimization_barrier((values,) + earlier)


def wide(values):
    return values.astype(f32)


def join(kept, arrived):
    return (wide(kept) + wide(arrived)).astype(bf16)


def body(
    tokens,
    action_mask,
    ln1_gain,
    ln1_bias,
    w_qkv,
    bias_qv,
    w_out,
    bias_out,
    ln2_gain,
    ln2_bias,
    w_fc1,
    bias_fc1,
    w_fc2,
    bias_fc2,
    out_grad,
):
    rows = w_qkv.shape[0]
    tok = lax.axis_size("tok")
    mlp = lax.axis_size("mlp")
    slot = w_fc1.shape[1]
    fast = tok == 8 and mlp == 4
    pieces = tok if fast else 1
    me = lax.axis_index("tok").astype(jnp.int32).reshape(1)
    chips = (2, 4, 6)
    odd = (me[0] & 1) == 1

    def pick(if_odd, if_even):
        return jnp.where(odd, if_odd, if_even)


    vectors = (bias_out, ln2_gain, ln2_bias, bias_fc2, ln1_gain, ln1_bias)
    me_a = me
    if fast:
        first_near = [swap_half_plane(w_qkv, stage) for stage in (0, 1)]
        first_near.append(swap_half_plane(first_near[0], 1))
        first_other = swap(w_qkv, 1)
        hidden_pack, out_block, rows_in, columns_in, bias_pair = prepare(
            w_fc1, w_fc2, bias_fc1, w_out, bias_qv, vectors
        )
        line = jnp.stack([hidden_pack, swap_half_line(hidden_pack, 0)])
        line = jnp.concatenate([line, swap_half_line(line, 1)])
        line = [line[0], pick(line[1], line[2]), pick(line[2], line[1]), line[3]]
        norm_tokens, first_near[0] = after(tokens, first_near[0])
        normed, scaled = first_norm(norm_tokens, rows_in)
        first_parts = [w_qkv] + first_near + [first_other] + [swap(p, 1) for p in first_near]
        hidden_own = jnp.concatenate([out_block] + [part[:rows] for part in line], axis=1)
        me_a, hidden_own = after(me, hidden_own)
        hidden_near = [swap(hidden_own, mask) for mask in chips + (1,)]
        biases = line
    else:
        rows_in = jnp.pad(wide(jnp.stack(vectors)), ((0, 2), (0, 0)))
        columns_in = rows_in.T
        bias_pair = wide(bias_qv).reshape(1, -1)
        normed, scaled = first_norm(tokens, rows_in)
        first_parts = [lax.all_gather(w_qkv, "tok", axis=0, tiled=True)]
        line = lax.all_gather(jnp.concatenate([w_fc1, w_fc2.T], axis=1), "mlp", axis=1, tiled=True)
        line = lax.all_gather(line, "tok", axis=0, tiled=True)
        biases = [lax.all_gather(bias_fc1, "mlp", axis=0, tiled=True).reshape(1, -1)]
        out_all = lax.all_gather(w_out, "tok", axis=0, tiled=True).T
        hidden_parts = [jnp.concatenate([out_all, line], axis=1)]

    saved = list(attend(me_a, normed, first_parts, bias_pair, action_mask))
    weights = saved[4]
    if fast:
        saved[1], *hidden_near = after(saved[1], *hidden_near)
        hidden_other = hidden_near.pop()
        hidden_parts = [hidden_own] + hidden_near + [hidden_other]
        hidden_parts = hidden_parts + [swap(part, 1) for part in hidden_near]

    output, middle_grad, branch, out_wide, *hidden_sends = forward(
        me, tokens, out_grad, rows_in, biases, saved[1], hidden_parts
    )

    grads = list(mixed_gradient(branch, out_wide, saved[1]))

    def back(me, group, count):
        return backward(me, pieces, group, count, grads, scaled, columns_in, saved)

    if not fast:
        back_a, sends_a = back(me, 0, 3)
        back_b, sends_b = back(me, 3, 1)
        early = early_gradient(back_a, weights)
        input_grad = input_gradient(tokens, middle_grad, rows_in, early, back_b, weights)
        return slow_end(output, input_grad, hidden_sends[0], (sends_a, sends_b), slot)

    arrived = swap(hidden_sends[1], 1)
    grads[0], arrived = after(grads[0], arrived)
    hidden = join(hidden_sends[0], arrived)
    me_1, hidden = after(me, hidden)
    near = [swap(hidden[k], chips[k - 1]) for k in (1, 2, 3)]
    back_a, *sends_a = back(me_1, 0, 3)

    back_a, *near = after(back_a, *near)
    hidden = wide(hidden[0]) + wide(near[0]) + wide(near[1]) + wide(near[2])
    sent = jnp.stack([pick(hidden[1], hidden[2]), hidden[3], hidden[4]]).astype(bf16)
    group_a = join(sends_a[0], swap(sends_a[1], 1))
    me_2, group_a, sent = after(me, group_a, sent)
    line_1 = swap_half_line(sent, 0)
    near_a = [swap(group_a[k], chips[k - 1]) for k in (1, 2, 3)]
    back_b, *sends_b = back(me_2, 3, 1)

    back_b, line_1, *near_a = after(back_b, line_1, *near_a)
    total_a = wide(group_a[0]) + wide(near_a[0]) + wide(near_a[1]) + wide(near_a[2])
    sent, kept_b, sent_b = after(total_a.astype(bf16), *sends_b)
    line_a = swap_half_line(sent, 1)
    group_b = join(kept_b, swap(sent_b, 1))
    line_1, group_b = after(line_1, group_b)
    block = hidden[0] + wide(line_1[0])
    middle_block = pick(hidden[2], hidden[1]) + wide(line_1[1])
    rest = hidden[4] + wide(line_1[2])
    sent = jnp.concatenate([middle_block, rest], axis=1).astype(bf16)
    group_b, sent = after(group_b, sent)
    line_2 = swap_half_line(sent, 1)
    near_b = [swap(group_b[k], chips[k - 1]) for k in (1, 2, 3)]
    line_a, *near_b = after(line_a, *near_b)
    total_b = wide(group_b[0]) + wide(near_b[0]) + wide(near_b[1]) + wide(near_b[2])
    total_a = total_a + wide(line_a)
    back_a, sent_b, sent_a = after(back_a, total_b.astype(bf16), total_a.astype(bf16))
    line_b = swap_half_line(sent_b, 0)
    line_a = swap_half_line(sent_a, 0)
    early = early_gradient(back_a, weights)

    early, line_b = after(early, line_b)
    total_b = total_b + wide(line_b)
    early, sent = after(early, total_b.astype(bf16))
    line_b = swap_half_line(sent, 1)
    input_grad = input_gradient(tokens, middle_grad, rows_in, early, back_b, weights)

    input_grad, line_a, line_b, line_2 = after(input_grad, line_a, line_b, line_2)
    hidden_grads = hidden_end(block, rest, line_2, slot)
    one_grad = hidden_grads[0]
    qkv_grad, bias_grad, gain_grad, shift_grad = heads_end(total_a, line_a, total_b, line_b)
    _, two_grad, hidden_bias_grad, out_rows, *vector_grads = hidden_grads
    return (
        output,
        input_grad,
        gain_grad,
        shift_grad,
        qkv_grad,
        bias_grad,
        out_rows,
        vector_grads[2],
        vector_grads[0],
        vector_grads[1],
        one_grad,
        hidden_bias_grad,
        two_grad.T,
        vector_grads[3],
    )


def slow_end(output, input_grad, hidden, sends, slot):
    def scatter(values):
        values = lax.psum_scatter(wide(values), "tok", scatter_dimension=0, tiled=True)
        return lax.psum(values, "mlp")

    hidden = wide(hidden)
    blocks = jnp.concatenate([hidden[k, :, :INNER] for k in range(4)], axis=1)
    blocks = lax.psum_scatter(blocks, "tok", scatter_dimension=0, tiled=True)
    hidden_sum = lax.psum_scatter(blocks, "mlp", scatter_dimension=1, tiled=True)
    out_rows = scatter(hidden[4, :, :INNER].T)
    lines = slot // 128
    small = lax.psum(hidden[:, :48, INNER:], ("tok", "mlp"))
    bias_sum = lax.dynamic_index_in_dim(small[:4, :lines], lax.axis_index("mlp"), 0, False)
    small = small[4]
    weights = [scatter(s[:, :-SMALL]) for s in sends]
    smalls = [lax.psum(wide(s[:48, -SMALL:]), ("tok", "mlp")) for s in sends]
    return results(output, input_grad, weights, smalls, out_rows, small, hidden_sum, bias_sum)


def results(output, input_grad, weights, smalls, out_rows, small, hidden_sum, bias_sum):
    blocks = []
    for part in weights:
        blocks += [part[:, at : at + WIDE] for at in range(0, part.shape[1], WIDE)]
    qkv_grad = jnp.concatenate([block for k in range(3) for block in blocks[k::3]], axis=1)
    lines = WIDE // 128
    biases = []
    for part, weight in zip(smalls, weights):
        count = 2 * (weight.shape[1] // QKV)
        biases += [part[k * lines : (k + 1) * lines] for k in range(count)]
    bias_grad = jnp.concatenate(biases[0::2] + biases[1::2], axis=0).reshape(-1)
    norm_grad = smalls[0][40:46] + smalls[1][40:46]
    vectors = [small[3 * k : 3 * k + 3].reshape(-1) for k in range(4)]
    slot = hidden_sum.shape[1] // 2
    return (
        output,
        input_grad,
        norm_grad[:3].reshape(-1),
        norm_grad[3:].reshape(-1),
        qkv_grad,
        bias_grad,
        out_rows,
        vectors[2],
        vectors[0],
        vectors[1],
        hidden_sum[:, :slot],
        bias_sum.reshape(-1),
        hidden_sum[:, slot:].T,
        vectors[3],
    )


def solution(mesh):
    placed = (
        P(("tok", "mlp"), None),
        P(("tok", "mlp"), None),
        P(),
        P(),
        P("tok", None),
        P(),
        P("tok", None),
        P(),
        P(),
        P(),
        P("tok", "mlp"),
        P("mlp"),
        P("mlp", "tok"),
        P(),
        P(("tok", "mlp"), None),
    )
    return jax.shard_map(
        body,
        mesh=mesh,
        in_specs=placed,
        out_specs=(
            P(("tok", "mlp"), None),
            P(("tok", "mlp"), None),
            P(),
            P(),
            P("tok", None),
            P(),
            P("tok", None),
            P(),
            P(),
            P(),
            P("tok", "mlp"),
            P("mlp"),
            P("mlp", "tok"),
            P(),
        ),
        check_vma=False,
    )
```

```python
import functools

import jax
import jax.numpy as jnp
from jax import lax
from jax.experimental import pallas as pl
from jax.experimental.pallas import tpu as pltpu
from jax.sharding import PartitionSpec as P

HEADS = 16
HEAD_DIM = 64
FRAME_LEN = 196
LEN = 588
D = 384
FF = 2048
INNER = HEADS * HEAD_DIM
KEYS = 592
ROWS = 640
GROUP = 4
WIDE = GROUP * HEAD_DIM
GROUPS = HEADS // GROUP
QKV = 3 * WIDE
SMALL = 128
BLOCK = INNER + SMALL

epsilon = 1e-06
f32 = jnp.float32
bf16 = jnp.bfloat16

NN = (((1,), (0,)), ((), ()))
NT = (((1,), (1,)), ((), ()))
TN = (((0,), (0,)), ((), ()))

QUERY_BLOCKS = ((0, 128, 208), (128, 256, 400), (384, 256, 592))
KEY_RANGES = ((0, 208, 0), (208, 400, 128), (400, 592, 384))

VMEM = 56 * 1024 * 1024

BIAS_OUT, GAIN_TWO, SHIFT_TWO, BIAS_TWO, GAIN_ONE, SHIFT_ONE = (slice(k, k + 1) for k in range(6))


def dot(left, right, dims):
    return lax.dot_general(left, right, dims, preferred_element_type=f32)


def normalize(values):
    center = values - jnp.mean(values, axis=-1, keepdims=True)
    inverse = lax.rsqrt(jnp.mean(center * center, axis=-1, keepdims=True) + epsilon)
    return center * inverse, inverse


def normalize_back(grad_rows, norm_gain, scaled, inverse):
    scaled_grad = grad_rows * norm_gain
    return inverse * (
        scaled_grad
        - jnp.mean(scaled_grad, axis=-1, keepdims=True)
        - scaled * jnp.mean(scaled_grad * scaled, axis=-1, keepdims=True)
    )


def cost(micros):
    return pl.CostEstimate(flops=int(micros * 1.1e9), bytes_accessed=1024, transcendentals=0)


MASKS = (0, 2, 4, 6, 1, 3, 5, 7)


def owners(me, count):
    return [me ^ mask for mask in MASKS[:count]]


def staged_owners(me, count):
    if count == 1:
        return [0]
    first = 2 + 2 * (me & 1)
    second = 6 - first
    other = me ^ 1
    return [me, me ^ first, me ^ second, me ^ 6, other, other ^ second, other ^ first, other ^ 6]


def whole(shape):
    return pl.BlockSpec(
        shape, lambda *step: (0,) * len(shape), pipeline_mode=pl.Buffered(buffer_count=1)
    )


def prepare_kernel(one_ref, two_ref, hidden_bias_ref, out_ref, bias_ref, *refs):
    row_refs, (pack_ref, block_ref, rows_ref, columns_ref, wide_bias_ref) = refs[:6], refs[6:]
    rows, slot = one_ref.shape
    pack_ref[:rows, :slot] = one_ref[...]
    pack_ref[:rows, slot:] = two_ref[...]
    first_row = lax.broadcasted_iota(jnp.int32, (16, 1), 0) == 0
    hidden_bias = hidden_bias_ref[...].astype(f32).reshape(1, slot)
    pack_ref[rows:, :slot] = jnp.where(first_row, hidden_bias, 0.0).astype(bf16)
    pack_ref[rows:, slot:] = jnp.zeros((16, slot), bf16)
    turned = out_ref[...].T
    width = turned.shape[1]
    for r in range(D // rows):
        block_ref[:, r * width : (r + 1) * width] = turned[r * rows : (r + 1) * rows]
    rows_ref[...] = jnp.zeros_like(rows_ref)
    for k, ref in enumerate(row_refs):
        rows_ref[k : k + 1] = ref[...].astype(f32).reshape(1, D)
    columns_ref[...] = rows_ref[...].T
    wide_bias_ref[...] = bias_ref[...].astype(f32).reshape(1, 2 * INNER)


def prepare(w_fc1, w_fc2, bias_fc1, w_out, bias_qv, vectors):
    rows, slot = w_fc1.shape
    return pl.pallas_call(
        prepare_kernel,
        out_shape=[
            jax.ShapeDtypeStruct((rows + 16, 2 * slot), bf16),
            jax.ShapeDtypeStruct((rows, INNER), bf16),
            jax.ShapeDtypeStruct((8, D), f32),
            jax.ShapeDtypeStruct((D, 8), f32),
            jax.ShapeDtypeStruct((1, 2 * INNER), f32),
        ],
        cost_estimate=cost(2),
        name="prepare",
    )(w_fc1, w_fc2.T, bias_fc1, w_out, bias_qv, *vectors)


def sequence_rows(scr_ref, s):
    values = scr_ref[s * LEN : s * LEN + KEYS]
    row = lax.broadcasted_iota(jnp.int32, (KEYS, 1), 0)
    return jnp.where(row < LEN, values, 0.0)


def norm_kernel(tokens_ref, rows_ref, out_ref, scaled_ref, rows_scr):
    count = tokens_ref.shape[0]
    rows_scr[:count] = tokens_ref[...].astype(f32)
    rows_scr[count:] = jnp.zeros_like(rows_scr[count:])
    row = lax.broadcasted_iota(jnp.int32, (KEYS, 1), 0)
    for s in range(out_ref.shape[0]):
        scaled, _ = normalize(sequence_rows(rows_scr, s))
        normed = scaled * rows_ref[GAIN_ONE] + rows_ref[SHIFT_ONE]
        for ref, rows in ((scaled_ref, scaled), (out_ref, normed)):
            ref[s, :KEYS] = jnp.where(row < LEN, rows, 0.0).astype(bf16)
            ref[s, KEYS:] = jnp.zeros((ROWS - KEYS, D), bf16)


def first_norm(tokens, rows_in):
    seqs = tokens.shape[0] // LEN
    shape = jax.ShapeDtypeStruct((seqs, ROWS, D), bf16)
    return pl.pallas_call(
        norm_kernel,
        out_shape=[shape, shape],
        scratch_shapes=[pltpu.VMEM((seqs * KEYS, D), f32)],
        compiler_params=pltpu.CompilerParams(vmem_limit_bytes=14 * 1024 * 1024),
        cost_estimate=cost(2.5),
        name="first_norm",
    )(tokens, rows_in)


def attend_kernel(pieces, me_ref, normed_ref, bias_ref, mask_ref, *refs):
    parts, refs = refs[:pieces], refs[pieces:]
    projected_ref, mixed_ref, exp_ref, inverse_ref, wide_ref = refs[:5]
    hide_scr, score_scr, mixed_scr, total_scr, mask_scr = refs[5:]
    group, seq = pl.program_id(0), pl.program_id(1)

    @pl.when((group == 0) & (seq == 0))
    def _():
        rows = D // pieces
        for j, owner in enumerate(staged_owners(me_ref[0], pieces)):
            to = pl.ds(pl.multiple_of(owner * rows, 16), rows)
            for g in range(GROUPS):
                for k in range(3):
                    left = k * INNER + g * WIDE
                    at = g * QKV + k * WIDE
                    wide_ref[to, at : at + WIDE] = parts[j][:, left : left + WIDE]
        total_scr[...] = jnp.ones_like(total_scr)
        mask_scr[...] = jnp.zeros_like(mask_scr)
        count = hide_scr.shape[0]
        mask_scr[:count, :LEN] = mask_ref[...].astype(f32)
        turned = mask_scr[...].T
        key = lax.broadcasted_iota(jnp.int32, (KEYS, ROWS), 0)
        query = lax.broadcasted_iota(jnp.int32, (KEYS, ROWS), 1)
        later = ((query < FRAME_LEN) & (key >= FRAME_LEN)) | (
            (query < 2 * FRAME_LEN) & (key >= 2 * FRAME_LEN)
        )
        for s in range(count):
            usable = jnp.logical_not(later) & (turned[:KEYS, s : s + 1] > 0.5)
            hide_scr[s] = jnp.where(usable | (key == query), 0.0, -1e30)

    columns = pl.ds(pl.multiple_of(group * QKV, 128), QKV)
    projected = dot(normed_ref[seq, :KEYS], wide_ref[:, columns], NN)
    at = pl.multiple_of(group * WIDE, 128)
    queries = (projected[:, :WIDE] + bias_ref[:, pl.ds(at, WIDE)]).astype(bf16)
    projected_ref[0, :KEYS, :WIDE] = queries * bf16(HEAD_DIM**-0.5)
    projected_ref[0, :KEYS, WIDE : 2 * WIDE] = projected[:, WIDE : 2 * WIDE].astype(bf16)
    values = projected[:, 2 * WIDE :] + bias_ref[:, pl.ds(at + INNER, WIDE)]
    projected_ref[0, :KEYS, 2 * WIDE :] = values.astype(bf16)
    projected_ref[0, KEYS:] = jnp.zeros((ROWS - KEYS, QKV), bf16)
    from_ref = projected_ref.at[0]

    lane = lax.broadcasted_iota(jnp.int32, (1, 128), 1)
    units = [(h, b) for h in range(GROUP) for b in QUERY_BLOCKS]

    largest = {}
    flipped = {}

    def scores(unit):
        head, (start, width, keys) = units[unit]
        pair = head // 2 * 128
        mine = (lane < 64) if head % 2 == 0 else (lane >= 64)
        own_keys = from_ref[:keys, WIDE + pair : WIDE + pair + 128]
        own_keys = jnp.where(mine, own_keys, bf16(0))
        score = dot(own_keys, from_ref[start : start + width, pair : pair + 128], NT)
        score = score + hide_scr[seq, :keys, start : start + width]
        score_scr[unit % 3, :keys, :width] = score
        top = jnp.max(score.reshape(-1, 8, width), axis=0)
        largest[unit] = jnp.max(top, axis=0, keepdims=True)

    def exponents(unit):
        head, (start, width, keys) = units[unit]
        exponent = jnp.exp(score_scr[unit % 3, :keys, :width] - largest[unit])
        exp_ref[0, head, :keys, start : start + width] = exponent.astype(bf16)

    def mix(unit):
        head, (start, width, keys) = units[unit]
        pair = head // 2 * 128
        if head not in flipped:
            turned = from_ref[:KEYS, 2 * WIDE + pair : 2 * WIDE + pair + 128].T
            side = head % 2 * 64
            ones = jnp.ones((16, KEYS), bf16)
            flipped[head] = jnp.concatenate([turned[side : side + 64], ones])
        exponent = exp_ref[0, head, :keys, start : start + width]
        summed = dot(flipped[head][:, :keys], exponent, NN)
        values, total = summed[:64], summed[64:65]
        inverse = 1.0 / total
        mixed_scr[head * 64 : (head + 1) * 64, start : start + width] = values * inverse
        total_scr[head : head + 1, start : start + width] = inverse

    count = len(units)
    scores(0)
    scores(1)
    for unit in range(count + 2):
        if unit + 2 < count:
            scores(unit + 2)
        if unit < count:
            exponents(unit)
        if unit > 1:
            mix(unit - 2)
    mixed_ref[0] = mixed_scr[...].T.astype(bf16)
    inverse_ref[0, 0] = total_scr[...]


def attend(me, normed, parts, bias, mask):
    seqs = normed.shape[0]
    return pl.pallas_call(
        functools.partial(attend_kernel, len(parts)),
        grid=(GROUPS, seqs),
        in_specs=[
            pl.BlockSpec(memory_space=pltpu.SMEM),
            whole(normed.shape),
            whole(bias.shape),
            whole(mask.shape),
        ]
        + [whole(part.shape) for part in parts],
        out_specs=[
            pl.BlockSpec((1, ROWS, QKV), lambda g, s: (s, 0, g)),
            pl.BlockSpec((1, ROWS, WIDE), lambda g, s: (s, 0, g)),
            pl.BlockSpec((1, GROUP, KEYS, ROWS), lambda g, s: (s, g, 0, 0)),
            pl.BlockSpec((1, 1, 8, ROWS), lambda g, s: (s, g, 0, 0)),
            whole((D, GROUPS * QKV)),
        ],
        out_shape=[
            pltpu.HBM((seqs, ROWS, GROUPS * QKV), bf16),
            pltpu.VMEM((seqs, ROWS, INNER), bf16),
            pltpu.HBM((seqs, HEADS, KEYS, ROWS), bf16),
            pltpu.HBM((seqs, GROUPS, 8, ROWS), f32),
            pltpu.HBM((D, GROUPS * QKV), bf16),
        ],
        scratch_shapes=[
            pltpu.VMEM((seqs, KEYS, ROWS), f32),
            pltpu.VMEM((3, KEYS, 256), f32),
            pltpu.VMEM((WIDE, ROWS), f32),
            pltpu.VMEM((8, ROWS), f32),
            pltpu.VMEM((8, ROWS), f32),
        ],
        compiler_params=pltpu.CompilerParams(vmem_limit_bytes=24 * 1024 * 1024),
        cost_estimate=cost(22),
        name="attend",
    )(me, normed, bias, mask, *parts)


def forward_kernel(pieces, n_bias, chunk, me_ref, tokens_ref, grad_ref, rows_ref, *refs):
    bias_refs, refs = refs[:n_bias], refs[n_bias:]
    mixed_ref, refs = refs[0], refs[1:]
    parts, refs = refs[:pieces], refs[pieces:]
    out_ref, middle_grad_ref, branch_ref, out_wide_ref = refs[:4]
    n_out = 2 if pieces > 1 else 1
    send_refs, refs = refs[4 : 4 + n_out], refs[4 + n_out :]
    one_scr, two_scr, middle_scr, scaled_scr, inverse_scr, second_scr, second_t, grad_scr = refs[:8]
    grad_t, total_scr, back_scr, weight_scr, small_scr, bias_scr = refs[8:14]
    stage_scrs = (refs[14:16], refs[16:18])
    seqs = branch_ref.shape[0]
    step = pl.program_id(0)
    rows = D // pieces
    per_slot = FF // 4
    ones = jnp.ones((16, seqs * KEYS), bf16)

    def send(value_ref, at, width, left):
        if pieces == 1:
            send_refs[0][0, :, left : left + width] = value_ref[:, at : at + width].astype(bf16)
            return
        for j, owner in enumerate(owners(me_ref[0], pieces)):
            first = pl.multiple_of(owner * rows, 16)
            send_refs[j // 4][j % 4, 0, :, left : left + width] = value_ref[
                pl.ds(first, rows), at : at + width
            ].astype(bf16)

    def send_vectors():
        vectors = small_scr[...].astype(bf16)
        if pieces == 1:
            send_refs[0][0, :48, INNER:] = vectors
        else:
            for j in range(pieces):
                send_refs[j // 4][j % 4, 0, :, INNER:] = vectors

    def produce(index, stage):
        act_scr, pre_scr = stage_scrs[stage]
        hidden = pl.ds(pl.multiple_of(index * chunk, 128), chunk)
        pre = dot(second_scr[...], one_scr[:, hidden], NN) + bias_scr[:, hidden]
        half = 0.5 + 0.5 * lax.erf(pre * (0.5**0.5))
        act_scr[...] = (pre * half).astype(bf16)
        slope = half + pre * (jnp.exp2(pre * pre * -0.7213475204444817) * 0.3989422804014327)
        grad_act = dot(grad_scr[...], two_scr[:, hidden], NN)
        pre_scr[...] = (grad_act * slope).astype(bf16)

    def consume(index, stage):
        act_scr, pre_scr = stage_scrs[stage]
        hidden = pl.ds(pl.multiple_of(index * chunk, 128), chunk)
        total_scr[...] += dot(act_scr[...], two_scr[:, hidden], NT)
        back_scr[...] += dot(pre_scr[...], one_scr[:, hidden], NT)
        left = stage * chunk
        weight_scr[:, :chunk] = dot(second_t[...], pre_scr[...], NN)
        send(weight_scr, 0, chunk, left)
        weight_scr[:, chunk : 2 * chunk] = dot(grad_t[...], act_scr[...], NN)
        send(weight_scr, chunk, chunk, left + per_slot)
        hidden_sum = dot(ones, pre_scr[...], NN)[0:1]
        for r in range(chunk // 128):
            at = stage * (chunk // 128) + r
            small_scr[at : at + 1] = hidden_sum[:, r * 128 : (r + 1) * 128]

    @pl.when(step == 0)
    def _():
        for j, owner in enumerate(owners(me_ref[0], pieces)):
            first = pl.multiple_of(owner * rows, 16)
            if pieces == 1:
                out_wide_ref[...] = parts[0][:, :INNER]
            else:
                to = pl.ds(pl.multiple_of(owner * 128, 128), 128)
                for r in range(pieces):
                    out_wide_ref[r * rows : (r + 1) * rows, to] = parts[j][
                        :, r * 128 : (r + 1) * 128
                    ]
            for z in range(4):
                left = INNER + 2 * per_slot * z
                slot = slice(z * per_slot, (z + 1) * per_slot)
                one_scr[pl.ds(first, rows), slot] = parts[j][:, left : left + per_slot]
                two_scr[pl.ds(first, rows), slot] = parts[j][
                    :, left + per_slot : left + 2 * per_slot
                ]
        if n_bias == 1:
            bias_scr[...] = bias_refs[0][...].astype(f32)
        else:
            for z in range(4):
                row = bias_refs[z][rows:, :per_slot].astype(f32)[0:1]
                bias_scr[:, z * per_slot : (z + 1) * per_slot] = row
        count = tokens_ref.shape[0]
        for scr, ref in ((total_scr, tokens_ref), (back_scr, grad_ref)):
            scr[:count] = ref[...].astype(f32)
            scr[count:] = jnp.zeros_like(scr[count:])
        for s in range(seqs):
            block = slice(s * KEYS, (s + 1) * KEYS)
            grad_scr[block] = sequence_rows(back_scr, s).astype(bf16)
            middle = sequence_rows(total_scr, s) + rows_ref[BIAS_OUT]
            middle = middle + dot(mixed_ref[s, :KEYS], out_wide_ref[...], NT)
            middle_scr[block] = middle
            scaled, inverse = normalize(middle)
            scaled_scr[block] = scaled
            inverse_scr[block] = inverse
            second_scr[block] = (scaled * rows_ref[GAIN_TWO] + rows_ref[SHIFT_TWO]).astype(bf16)
        second_t[...] = second_scr[...].T
        grad_t[...] = grad_scr[...].T
        total_scr[...] = jnp.zeros_like(total_scr)
        back_scr[...] = jnp.zeros_like(back_scr)
        small_scr[...] = jnp.zeros_like(small_scr)
        produce(0, 0)

    @pl.when(step < 4)
    def _():
        produce(2 * step + 1, 1)
        consume(2 * step, 0)
        produce(jnp.minimum(2 * step + 2, FF // chunk - 1), 0)
        consume(2 * step + 1, 1)
        send_vectors()

    @pl.when(step == 4)
    def _():
        sums = [jnp.zeros((1, D), f32) for _ in range(2)]
        for s in range(seqs):
            block = slice(s * KEYS, (s + 1) * KEYS)
            output = middle_scr[block] + total_scr[block] + rows_ref[BIAS_TWO]
            total_scr[s * LEN : (s + 1) * LEN] = output[:LEN]
        out_ref[...] = total_scr[: seqs * LEN].astype(bf16)
        for s in range(seqs):
            block = slice(s * KEYS, (s + 1) * KEYS)
            scaled, inverse = scaled_scr[block], inverse_scr[block]
            grad_second = back_scr[block]
            grad_middle = grad_scr[block].astype(f32) + normalize_back(
                grad_second, rows_ref[GAIN_TWO], scaled, inverse
            )
            middle_grad_ref[s, :KEYS] = grad_middle
            branch_ref[s, :KEYS] = grad_middle.astype(bf16)
            branch_ref[s, KEYS:] = jnp.zeros((ROWS - KEYS, D), bf16)
            for k, term in enumerate((grad_second * scaled, grad_second)):
                sums[k] = sums[k] + jnp.sum(term, axis=0, keepdims=True)
        branch = jnp.concatenate([branch_ref[s, :KEYS] for s in range(seqs)], axis=0)
        sums.append(dot(ones, branch, NN)[0:1])
        sums.append(dot(ones, grad_scr[...], NN)[0:1])
        for k in range(4):
            for r in range(D // 128):
                at = 3 * k + r
                small_scr[at : at + 1] = sums[k][:, r * 128 : (r + 1) * 128]
        mixed = jnp.concatenate([mixed_ref[s, :KEYS] for s in range(seqs)], axis=0)
        weight_scr[...] = dot(branch, mixed, TN)
        if pieces == 1:
            send_refs[0][0, :, :INNER] = weight_scr[...].astype(bf16)
        else:
            for j, owner in enumerate(owners(me_ref[0], pieces)):
                to = pl.ds(pl.multiple_of(owner * 128, 128), 128)
                for r in range(pieces):
                    send_refs[j // 4][j % 4, 0, :, r * 128 : (r + 1) * 128] = weight_scr[
                        r * rows : (r + 1) * rows, to
                    ].astype(bf16)
        send_vectors()


def forward(me, tokens, cotangent, rows_in, biases, mixed, parts):
    seqs = tokens.shape[0] // LEN
    pieces = len(parts)
    chunk = 256
    if pieces > 1:
        send_shapes = [(pieces // 2, 5, D // pieces, BLOCK)] * 2
        send_specs = [pl.BlockSpec((pieces // 2, 1, D // pieces, BLOCK), lambda c: (0, c, 0, 0))] * 2
    else:
        send_shapes = [(5, D, BLOCK)]
        send_specs = [pl.BlockSpec((1, D, BLOCK), lambda c: (c, 0, 0))]
    rows3 = (seqs, ROWS, D)
    rows2 = (seqs * KEYS, D)
    return pl.pallas_call(
        functools.partial(forward_kernel, pieces, len(biases), chunk),
        grid=(5,),
        in_specs=[
            pl.BlockSpec(memory_space=pltpu.SMEM),
            whole(tokens.shape),
            whole(tokens.shape),
            whole((8, D)),
        ]
        + [whole(b.shape) for b in biases]
        + [whole(mixed.shape)]
        + [whole(p.shape) for p in parts],
        out_specs=[whole(tokens.shape), whole(rows3), whole(rows3), whole((D, INNER))]
        + send_specs,
        out_shape=[
            jax.ShapeDtypeStruct(tokens.shape, bf16),
            jax.ShapeDtypeStruct(rows3, f32),
            pltpu.VMEM(rows3, bf16),
            pltpu.VMEM((D, INNER), bf16),
        ]
        + [pltpu.VMEM(s, bf16) for s in send_shapes],
        scratch_shapes=[
            pltpu.VMEM((D, FF), bf16),
            pltpu.VMEM((D, FF), bf16),
            pltpu.VMEM(rows2, f32),
            pltpu.VMEM(rows2, f32),
            pltpu.VMEM((seqs * KEYS, 1), f32),
            pltpu.VMEM(rows2, bf16),
            pltpu.VMEM((D, seqs * KEYS), bf16),
            pltpu.VMEM(rows2, bf16),
            pltpu.VMEM((D, seqs * KEYS), bf16),
            pltpu.VMEM(rows2, f32),
            pltpu.VMEM(rows2, f32),
            pltpu.VMEM((D, INNER), f32),
            pltpu.VMEM((48, 128), f32),
            pltpu.VMEM((1, FF), f32),
        ]
        + [pltpu.VMEM((seqs * KEYS, chunk), bf16)] * 4,
        compiler_params=pltpu.CompilerParams(vmem_limit_bytes=36 * 1024 * 1024),
        cost_estimate=cost(30),
        name="forward",
    )(me, tokens, cotangent, rows_in, *biases, mixed, *parts)


def mixed_gradient_kernel(branch_ref, out_wide_ref, mixed_ref, grad_ref, delta_ref):
    lane = lax.broadcasted_iota(jnp.int32, (8, WIDE), 1)
    gather = (lane >> 6 == lax.broadcasted_iota(jnp.int32, (8, WIDE), 0)).astype(bf16)
    for g in range(delta_ref.shape[1]):
        columns = slice(g * WIDE, (g + 1) * WIDE)
        grad = dot(branch_ref[0], out_wide_ref[:, columns], NN).astype(bf16)
        grad_ref[0, :, columns] = grad
        product = grad.astype(f32) * mixed_ref[0, :, columns].astype(f32)
        first = product.astype(bf16)
        second = (product - first.astype(f32)).astype(bf16)
        delta_ref[0, g] = dot(gather, first, NT) + dot(gather, second, NT)


def mixed_gradient(branch, out_wide, mixed):
    seqs = branch.shape[0]
    each = 2
    columns = pl.BlockSpec((1, ROWS, each * WIDE), lambda s, g: (s, 0, g))
    return pl.pallas_call(
        mixed_gradient_kernel,
        grid=(seqs, GROUPS // each),
        in_specs=[
            pl.BlockSpec((1, ROWS, D), lambda s, g: (s, 0, 0)),
            pl.BlockSpec((D, each * WIDE), lambda s, g: (0, g)),
            columns,
        ],
        out_specs=[columns, pl.BlockSpec((1, each, 8, ROWS), lambda s, g: (s, g, 0, 0))],
        out_shape=[
            pltpu.HBM((seqs, ROWS, INNER), bf16),
            pltpu.HBM((seqs, GROUPS, 8, ROWS), f32),
        ],
        compiler_params=pltpu.CompilerParams(vmem_limit_bytes=16 * 1024 * 1024),
        cost_estimate=cost(5),
        name="mixed_gradient",
    )(branch, out_wide, mixed)


def backward_kernel(pieces, me_ref, *refs):
    grad_ref, delta_ref, scaled_ref, projected_ref, exp_ref, inverse_ref = refs[:6]
    wide_ref, norm_ref = refs[6:8]
    refs = refs[8:]
    n_out = 2 if pieces > 1 else 1
    back_ref = refs[0]
    send_refs = refs[1 : 1 + n_out]
    grad_scr, prob_scr, turned_scr, weight_scr, small_scr, sum_scr, norm_scr = refs[1 + n_out :]
    group, seq = pl.program_id(0), pl.program_id(1)
    groups, seqs = pl.num_programs(0), pl.num_programs(1)
    rows = D // pieces

    @pl.when((group == 0) & (seq == 0))
    def _():
        small_scr[...] = jnp.zeros_like(small_scr)
        norm_scr[...] = jnp.zeros_like(norm_scr)

    lane = lax.broadcasted_iota(jnp.int32, (1, 128), 1)
    low = lane < 64
    kept = {}
    turned_keys = {}

    def parts(head):
        columns = slice(head // 2 * 128, head // 2 * 128 + 128)
        return columns, head % 2, grad_ref[0, :, columns]

    def score_gradients(head):
        columns, half, grad = parts(head)
        mine = low if half == 0 else jnp.logical_not(low)
        value = projected_ref[0, :KEYS, 2 * WIDE + columns.start : 2 * WIDE + columns.stop]
        own_value = jnp.where(mine, value, bf16(0))
        inverse = inverse_ref[0, 0, head : head + 1].astype(bf16)
        delta = delta_ref[0, 0, head : head + 1]
        for start, width, keys in QUERY_BLOCKS:
            block = slice(start, start + width)
            change = dot(own_value[:keys], grad[block], NT) - delta[:, block]
            probability = exp_ref[0, head, :keys, block] * inverse[:, block]
            prob_scr[half, :keys, block] = probability
            grad_scr[half, :keys, block] = probability * change.astype(bf16)

    def input_gradients(head):
        columns, half, grad = parts(head)
        pair = head // 2
        query = projected_ref[0, :, columns]
        if half == 0:
            turned_keys[pair] = projected_ref[0, :KEYS, WIDE + columns.start : WIDE + columns.stop].T
        turned = turned_keys[pair]
        side = slice(64 * half, 64 * half + 64)
        for start, width, keys in QUERY_BLOCKS:
            block = slice(start, start + width)
            turned_scr[head * 64 : (head + 1) * 64, block] = dot(
                turned[side, :keys], grad_scr[half, :keys, block], NN
            ) * (HEAD_DIM**-0.5)
        for start, stop, seen in KEY_RANGES:
            value_grad = dot(prob_scr[half, start:stop, seen:], grad[seen:], NN)
            key_grad = dot(grad_scr[half, start:stop, seen:], query[seen:], NN)
            if half == 0:
                kept[start] = (value_grad, key_grad)
            else:
                at = slice(WIDE + columns.start, WIDE + columns.stop)
                back_ref[0, start:stop, at] = jnp.where(low, kept[start][1], key_grad).astype(bf16)
                at = slice(2 * WIDE + columns.start, 2 * WIDE + columns.stop)
                back_ref[0, start:stop, at] = jnp.where(low, kept[start][0], value_grad).astype(bf16)

    score_gradients(0)
    for head in range(GROUP):
        if head + 1 < GROUP:
            score_gradients(head + 1)
        input_gradients(head)
    back_ref[0, :KEYS, :WIDE] = turned_scr[...].T[:KEYS].astype(bf16)

    back = back_ref[0, :KEYS]
    weight = dot(scaled_ref[0, :KEYS], back, TN)
    total = dot(jnp.ones((16, KEYS), bf16), back, NN)[0:1]

    @pl.when(seq == 0)
    def _():
        weight_scr[...] = weight
        sum_scr[0:1] = total

    @pl.when(seq > 0)
    def _():
        weight_scr[...] += weight
        sum_scr[0:1] += total

    @pl.when(seq == seqs - 1)
    def _():
        sums = sum_scr[0:1]
        for r in range(WIDE // 128):
            at = group * (2 * WIDE // 128) + r
            small_scr[pl.ds(at, 1)] = sums[:, r * 128 : r * 128 + 128]
            at = at + WIDE // 128
            small_scr[pl.ds(at, 1)] = sums[:, 2 * WIDE + r * 128 : 2 * WIDE + r * 128 + 128]
        wide = wide_ref[...].astype(f32)
        scaled_weight = weight_scr[...]
        norm_scr[:, 0:1] += jnp.sum(scaled_weight * wide, axis=1, keepdims=True)
        norm_scr[:, 1:2] += jnp.sum(sums * wide, axis=1, keepdims=True)
        weight_scr[...] = scaled_weight * norm_ref[:, GAIN_ONE] + sums * norm_ref[:, SHIFT_ONE]
        start = pl.multiple_of(group * QKV, 128)
        if pieces == 1:
            send_refs[0][:, pl.ds(start, QKV)] = weight_scr[...].astype(bf16)
        else:
            for j, owner in enumerate(owners(me_ref[0], pieces)):
                first = pl.multiple_of(owner * rows, 16)
                send_refs[j // 4][j % 4, :, pl.ds(start, QKV)] = weight_scr[
                    pl.ds(first, rows)
                ].astype(bf16)

    @pl.when((group == groups - 1) & (seq == seqs - 1))
    def _():
        turned = norm_scr[...].T
        for k in range(2):
            for r in range(D // 128):
                small_scr[40 + 3 * k + r : 41 + 3 * k + r] = turned[
                    k : k + 1, r * 128 : (r + 1) * 128
                ]
        small = small_scr[...].astype(bf16)
        if pieces == 1:
            send_refs[0][:48, send_refs[0].shape[1] - SMALL :] = small
        else:
            for j in range(pieces):
                edge = send_refs[0].shape[2] - SMALL
                send_refs[j // 4][j % 4, :, edge:] = small


def backward(me, pieces, first_group, groups, grads, scaled, norm, saved):
    operands = [
        pltpu.with_memory_space_constraint(x, pltpu.HBM)
        for x in (*grads, scaled, saved[0], saved[2], saved[3], saved[4])
    ]
    seqs = scaled.shape[0]
    width = groups * QKV + SMALL
    if pieces > 1:
        send_shapes = [(pieces // 2, D // pieces, width)] * 2
    else:
        send_shapes = [(D, width)]
    columns = pl.BlockSpec((1, ROWS, WIDE), lambda g, s: (s, 0, g + first_group))
    heads = pl.BlockSpec((1, 1, 8, ROWS), lambda g, s: (s, g + first_group, 0, 0))
    rows_block = pl.BlockSpec((1, ROWS, D), lambda g, s: (s, 0, 0))
    return pl.pallas_call(
        functools.partial(backward_kernel, pieces),
        grid=(groups, seqs),
        in_specs=[
            pl.BlockSpec(memory_space=pltpu.SMEM),
            columns,
            heads,
            rows_block,
            pl.BlockSpec((1, ROWS, QKV), lambda g, s: (s, 0, g + first_group)),
            pl.BlockSpec((1, GROUP, KEYS, ROWS), lambda g, s: (s, g + first_group, 0, 0)),
            heads,
            pl.BlockSpec((D, QKV), lambda g, s: (0, g + first_group)),
            whole((D, 8)),
        ],
        out_specs=[pl.BlockSpec((1, ROWS, QKV), lambda g, s: (s, 0, g))]
        + [whole(s) for s in send_shapes],
        out_shape=[jax.ShapeDtypeStruct((seqs, ROWS, groups * QKV), bf16)]
        + [jax.ShapeDtypeStruct(s, bf16) for s in send_shapes],
        scratch_shapes=[
            pltpu.VMEM((2, KEYS, ROWS), bf16),
            pltpu.VMEM((2, KEYS, ROWS), bf16),
            pltpu.VMEM((WIDE, ROWS), f32),
            pltpu.VMEM((D, QKV), f32),
            pltpu.VMEM((48, 128), f32),
            pltpu.VMEM((8, QKV), f32),
            pltpu.VMEM((D, 128), f32),
        ],
        compiler_params=pltpu.CompilerParams(vmem_limit_bytes=23 * 1024 * 1024),
        cost_estimate=cost(11 * groups),
        name="backward",
    )(me, *operands, norm)


def early_kernel(back_ref, wide_ref, out_ref):
    for s in range(out_ref.shape[0]):
        grad = dot(back_ref[s, :KEYS], wide_ref[...], NT)
        before = jnp.where(pl.program_id(0) == 0, 0.0, out_ref[s])
        out_ref[s] = before + grad


def early_gradient(back, weights):
    seqs, groups = back.shape[0], back.shape[2] // QKV
    return pl.pallas_call(
        early_kernel,
        grid=(groups,),
        in_specs=[
            pl.BlockSpec((seqs, ROWS, QKV), lambda g: (0, 0, g)),
            pl.BlockSpec((D, QKV), lambda g: (0, g)),
        ],
        out_specs=whole((seqs, KEYS, D)),
        out_shape=jax.ShapeDtypeStruct((seqs, KEYS, D), f32),
        compiler_params=pltpu.CompilerParams(vmem_limit_bytes=14 * 1024 * 1024),
        cost_estimate=cost(5),
        name="early_gradient",
    )(back, weights)


def input_kernel(tokens_ref, middle_grad_ref, rows_ref, early_ref, back_ref, wide_ref, out_ref):
    out_ref[...] = tokens_ref[...].astype(f32)
    for s in range(middle_grad_ref.shape[0]):
        grad_first = early_ref[s] + dot(back_ref[s, :KEYS], wide_ref[...], NT)
        given = slice(s * LEN, (s + 1) * LEN)
        scaled, inverse = normalize(out_ref[given])
        out_ref[given] = middle_grad_ref[s, :LEN] + normalize_back(
            grad_first[:LEN], rows_ref[GAIN_ONE], scaled, inverse
        )


def input_gradient(tokens, middle_grad, rows_in, early, back, weights):
    return pl.pallas_call(
        input_kernel,
        grid=(1,),
        in_specs=[
            whole(tokens.shape),
            whole(middle_grad.shape),
            whole(rows_in.shape),
            whole(early.shape),
            whole(back.shape),
            pl.BlockSpec((D, QKV), lambda g: (0, GROUPS - 1)),
        ],
        out_specs=whole(tokens.shape),
        out_shape=jax.ShapeDtypeStruct(tokens.shape, f32),
        compiler_params=pltpu.CompilerParams(vmem_limit_bytes=16 * 1024 * 1024),
        cost_estimate=cost(4),
        name="input_gradient",
    )(tokens, middle_grad, rows_in, early, back, weights)


def join_lines(values):
    return jnp.concatenate([values[k : k + 1] for k in range(values.shape[0])], axis=1)


def hidden_end_kernel(block_ref, rest_ref, arrived_ref, one_ref, two_ref, bias_ref, out_ref, *refs):
    rows, slot = one_ref.shape
    block = block_ref[...] + arrived_ref[:, :BLOCK].astype(f32)
    rest = rest_ref[...] + arrived_ref[:, BLOCK:].astype(f32)
    one_ref[...] = block[:, :slot]
    two_ref[...] = block[:, slot : 2 * slot]
    bias_ref[...] = join_lines(block[: slot // 128, INNER:]).reshape(slot)
    width = out_ref.shape[0]
    parts = [rest[:, r * width : (r + 1) * width] for r in range(INNER // width)]
    out_ref[...] = jnp.concatenate(parts, axis=0).T
    for k, ref in enumerate(refs):
        ref[...] = join_lines(rest[3 * k : 3 * k + 3, INNER:]).reshape(D)


def hidden_end(block, rest, arrived, slot):
    rows = block.shape[0]
    width = INNER // (D // rows)
    vector = jax.ShapeDtypeStruct((D,), f32)
    return pl.pallas_call(
        hidden_end_kernel,
        out_shape=[
            jax.ShapeDtypeStruct((rows, slot), f32),
            jax.ShapeDtypeStruct((rows, slot), f32),
            jax.ShapeDtypeStruct((slot,), f32),
            jax.ShapeDtypeStruct((width, D), f32),
        ]
        + [vector] * 4,
        compiler_params=pltpu.CompilerParams(vmem_limit_bytes=8 * 1024 * 1024),
        cost_estimate=cost(2),
        name="hidden_end",
    )(block, rest, arrived)


def heads_end_kernel(early_ref, early_line_ref, late_ref, late_line_ref, weight_ref, bias_ref, *refs):
    early = early_ref[...] + early_line_ref[...].astype(f32)
    late = late_ref[...] + late_line_ref[...].astype(f32)
    lines = WIDE // 128
    norms, group = 0.0, 0
    for part in (early, late):
        edge = part.shape[1] - SMALL
        for g in range(edge // QKV):
            for k in range(3):
                left = g * QKV + k * WIDE
                to = k * INNER + group * WIDE
                weight_ref[:, to : to + WIDE] = part[:, left : left + WIDE]
            for k in range(2):
                first = (2 * g + k) * lines
                values = join_lines(part[first : first + lines, edge:])
                at = k * INNER + group * WIDE
                bias_ref[at : at + WIDE] = values.reshape(WIDE)
            group += 1
        norms = norms + part[40:48, edge:]
    for k, ref in enumerate(refs):
        ref[...] = join_lines(norms[3 * k : 3 * k + 3]).reshape(D)


def heads_end(early, early_line, late, late_line):
    vector = jax.ShapeDtypeStruct((D,), f32)
    return pl.pallas_call(
        heads_end_kernel,
        out_shape=[
            jax.ShapeDtypeStruct((early.shape[0], 3 * INNER), f32),
            jax.ShapeDtypeStruct((2 * INNER,), f32),
            vector,
            vector,
        ],
        compiler_params=pltpu.CompilerParams(vmem_limit_bytes=8 * 1024 * 1024),
        cost_estimate=cost(2),
        name="heads_end",
    )(early, early_line, late, late_line)


def swap(values, mask):
    size = lax.axis_size("tok")
    return lax.ppermute(values, "tok", [(i, i ^ mask) for i in range(size)])


def swap_half_plane(values, stage):
    size = lax.axis_size("tok")
    pairs = [(t, t ^ (2 if (t % 2 == 0) == (stage == 0) else 4)) for t in range(size)]
    return lax.ppermute(values, "tok", pairs)


def swap_half_line(values, stage):
    tok, mlp = lax.axis_size("tok"), lax.axis_size("mlp")
    pairs = []
    for t in range(tok):
        for z in range(mlp):
            far = (t % 2 == 0) == (stage == 0)
            pairs.append((t * mlp + z, t * mlp + (z ^ (2 if far else 1))))
    return lax.ppermute(values.astype(bf16), ("tok", "mlp"), pairs)


def after(values, *earlier):
    return lax.optimization_barrier((values,) + earlier)


def wide(values):
    return values.astype(f32)


def join(kept, arrived):
    return (wide(kept) + wide(arrived)).astype(bf16)


def body(
    tokens,
    action_mask,
    ln1_gain,
    ln1_bias,
    w_qkv,
    bias_qv,
    w_out,
    bias_out,
    ln2_gain,
    ln2_bias,
    w_fc1,
    bias_fc1,
    w_fc2,
    bias_fc2,
    out_grad,
):
    rows = w_qkv.shape[0]
    tok = lax.axis_size("tok")
    mlp = lax.axis_size("mlp")
    slot = w_fc1.shape[1]
    fast = tok == 8 and mlp == 4
    pieces = tok if fast else 1
    me = lax.axis_index("tok").astype(jnp.int32).reshape(1)
    chips = (2, 4, 6)
    odd = (me[0] & 1) == 1

    def pick(if_odd, if_even):
        return jnp.where(odd, if_odd, if_even)


    vectors = (bias_out, ln2_gain, ln2_bias, bias_fc2, ln1_gain, ln1_bias)
    me_a = me
    if fast:
        first_near = [swap_half_plane(w_qkv, stage) for stage in (0, 1)]
        first_near.append(swap_half_plane(first_near[0], 1))
        first_other = swap(w_qkv, 1)
        hidden_pack, out_block, rows_in, columns_in, bias_pair = prepare(
            w_fc1, w_fc2, bias_fc1, w_out, bias_qv, vectors
        )
        line = jnp.stack([hidden_pack, swap_half_line(hidden_pack, 0)])
        line = jnp.concatenate([line, swap_half_line(line, 1)])
        line = [line[0], pick(line[1], line[2]), pick(line[2], line[1]), line[3]]
        norm_tokens, first_near[0] = after(tokens, first_near[0])
        normed, scaled = first_norm(norm_tokens, rows_in)
        first_parts = [w_qkv] + first_near + [first_other] + [swap(p, 1) for p in first_near]
        hidden_own = jnp.concatenate([out_block] + [part[:rows] for part in line], axis=1)
        me_a, hidden_own = after(me, hidden_own)
        hidden_near = [swap(hidden_own, mask) for mask in chips + (1,)]
        biases = line
    else:
        rows_in = jnp.pad(wide(jnp.stack(vectors)), ((0, 2), (0, 0)))
        columns_in = rows_in.T
        bias_pair = wide(bias_qv).reshape(1, -1)
        normed, scaled = first_norm(tokens, rows_in)
        first_parts = [lax.all_gather(w_qkv, "tok", axis=0, tiled=True)]
        line = lax.all_gather(jnp.concatenate([w_fc1, w_fc2.T], axis=1), "mlp", axis=1, tiled=True)
        line = lax.all_gather(line, "tok", axis=0, tiled=True)
        biases = [lax.all_gather(bias_fc1, "mlp", axis=0, tiled=True).reshape(1, -1)]
        out_all = lax.all_gather(w_out, "tok", axis=0, tiled=True).T
        hidden_parts = [jnp.concatenate([out_all, line], axis=1)]

    saved = list(attend(me_a, normed, first_parts, bias_pair, action_mask))
    weights = saved[4]
    if fast:
        saved[1], *hidden_near = after(saved[1], *hidden_near)
        hidden_other = hidden_near.pop()
        hidden_parts = [hidden_own] + hidden_near + [hidden_other]
        hidden_parts = hidden_parts + [swap(part, 1) for part in hidden_near]

    output, middle_grad, branch, out_wide, *hidden_sends = forward(
        me, tokens, out_grad, rows_in, biases, saved[1], hidden_parts
    )

    grads = list(mixed_gradient(branch, out_wide, saved[1]))

    def back(me, group, count):
        return backward(me, pieces, group, count, grads, scaled, columns_in, saved)

    if not fast:
        back_a, sends_a = back(me, 0, 3)
        back_b, sends_b = back(me, 3, 1)
        early = early_gradient(back_a, weights)
        input_grad = input_gradient(tokens, middle_grad, rows_in, early, back_b, weights)
        return slow_end(output, input_grad, hidden_sends[0], (sends_a, sends_b), slot)

    arrived = swap(hidden_sends[1], 1)
    grads[0], arrived = after(grads[0], arrived)
    hidden = join(hidden_sends[0], arrived)
    me_1, hidden = after(me, hidden)
    near = [swap(hidden[k], chips[k - 1]) for k in (1, 2, 3)]
    back_a, *sends_a = back(me_1, 0, 3)

    back_a, *near = after(back_a, *near)
    hidden = wide(hidden[0]) + wide(near[0]) + wide(near[1]) + wide(near[2])
    sent = jnp.stack([pick(hidden[1], hidden[2]), hidden[3], hidden[4]]).astype(bf16)
    group_a = join(sends_a[0], swap(sends_a[1], 1))
    me_2, group_a, sent = after(me, group_a, sent)
    line_1 = swap_half_line(sent, 0)
    near_a = [swap(group_a[k], chips[k - 1]) for k in (1, 2, 3)]
    back_b, *sends_b = back(me_2, 3, 1)

    back_b, line_1, *near_a = after(back_b, line_1, *near_a)
    total_a = wide(group_a[0]) + wide(near_a[0]) + wide(near_a[1]) + wide(near_a[2])
    sent, kept_b, sent_b = after(total_a.astype(bf16), *sends_b)
    line_a = swap_half_line(sent, 1)
    group_b = join(kept_b, swap(sent_b, 1))
    line_1, group_b = after(line_1, group_b)
    block = hidden[0] + wide(line_1[0])
    middle_block = pick(hidden[2], hidden[1]) + wide(line_1[1])
    rest = hidden[4] + wide(line_1[2])
    sent = jnp.concatenate([middle_block, rest], axis=1).astype(bf16)
    group_b, sent = after(group_b, sent)
    line_2 = swap_half_line(sent, 1)
    near_b = [swap(group_b[k], chips[k - 1]) for k in (1, 2, 3)]
    line_a, *near_b = after(line_a, *near_b)
    total_b = wide(group_b[0]) + wide(near_b[0]) + wide(near_b[1]) + wide(near_b[2])
    total_a = total_a + wide(line_a)
    back_a, sent_b, sent_a = after(back_a, total_b.astype(bf16), total_a.astype(bf16))
    line_b = swap_half_line(sent_b, 0)
    line_a = swap_half_line(sent_a, 0)
    early = early_gradient(back_a, weights)

    early, line_b = after(early, line_b)
    total_b = total_b + wide(line_b)
    early, sent = after(early, total_b.astype(bf16))
    line_b = swap_half_line(sent, 1)
    input_grad = input_gradient(tokens, middle_grad, rows_in, early, back_b, weights)

    input_grad, line_a, line_b, line_2 = after(input_grad, line_a, line_b, line_2)
    hidden_grads = hidden_end(block, rest, line_2, slot)
    one_grad = hidden_grads[0]
    qkv_grad, bias_grad, gain_grad, shift_grad = heads_end(total_a, line_a, total_b, line_b)
    _, two_grad, hidden_bias_grad, out_rows, *vector_grads = hidden_grads
    return (
        output,
        input_grad,
        gain_grad,
        shift_grad,
        qkv_grad,
        bias_grad,
        out_rows,
        vector_grads[2],
        vector_grads[0],
        vector_grads[1],
        one_grad,
        hidden_bias_grad,
        two_grad.T,
        vector_grads[3],
    )


def slow_end(output, input_grad, hidden, sends, slot):
    def scatter(values):
        values = lax.psum_scatter(wide(values), "tok", scatter_dimension=0, tiled=True)
        return lax.psum(values, "mlp")

    hidden = wide(hidden)
    blocks = jnp.concatenate([hidden[k, :, :INNER] for k in range(4)], axis=1)
    blocks = lax.psum_scatter(blocks, "tok", scatter_dimension=0, tiled=True)
    hidden_sum = lax.psum_scatter(blocks, "mlp", scatter_dimension=1, tiled=True)
    out_rows = scatter(hidden[4, :, :INNER].T)
    lines = slot // 128
    small = lax.psum(hidden[:, :48, INNER:], ("tok", "mlp"))
    bias_sum = lax.dynamic_index_in_dim(small[:4, :lines], lax.axis_index("mlp"), 0, False)
    small = small[4]
    weights = [scatter(s[:, :-SMALL]) for s in sends]
    smalls = [lax.psum(wide(s[:48, -SMALL:]), ("tok", "mlp")) for s in sends]
    return results(output, input_grad, weights, smalls, out_rows, small, hidden_sum, bias_sum)


def results(output, input_grad, weights, smalls, out_rows, small, hidden_sum, bias_sum):
    blocks = []
    for part in weights:
        blocks += [part[:, at : at + WIDE] for at in range(0, part.shape[1], WIDE)]
    qkv_grad = jnp.concatenate([block for k in range(3) for block in blocks[k::3]], axis=1)
    lines = WIDE // 128
    biases = []
    for part, weight in zip(smalls, weights):
        count = 2 * (weight.shape[1] // QKV)
        biases += [part[k * lines : (k + 1) * lines] for k in range(count)]
    bias_grad = jnp.concatenate(biases[0::2] + biases[1::2], axis=0).reshape(-1)
    norm_grad = smalls[0][40:46] + smalls[1][40:46]
    vectors = [small[3 * k : 3 * k + 3].reshape(-1) for k in range(4)]
    slot = hidden_sum.shape[1] // 2
    return (
        output,
        input_grad,
        norm_grad[:3].reshape(-1),
        norm_grad[3:].reshape(-1),
        qkv_grad,
        bias_grad,
        out_rows,
        vectors[2],
        vectors[0],
        vectors[1],
        hidden_sum[:, :slot],
        bias_sum.reshape(-1),
        hidden_sum[:, slot:].T,
        vectors[3],
    )


def solution(mesh):
    placed = (
        P(("tok", "mlp"), None),
        P(("tok", "mlp"), None),
        P(),
        P(),
        P("tok", None),
        P(),
        P("tok", None),
        P(),
        P(),
        P(),
        P("tok", "mlp"),
        P("mlp"),
        P("mlp", "tok"),
        P(),
        P(("tok", "mlp"), None),
    )
    return jax.shard_map(
        body,
        mesh=mesh,
        in_specs=placed,
        out_specs=(
            P(("tok", "mlp"), None),
            P(("tok", "mlp"), None),
            P(),
            P(),
            P("tok", None),
            P(),
            P("tok", None),
            P(),
            P(),
            P(),
            P("tok", "mlp"),
            P("mlp"),
            P("mlp", "tok"),
            P(),
        ),
        check_vma=False,
    )
```

```python
import functools

import jax
import jax.numpy as jnp
from jax import lax
from jax.experimental import pallas as pl
from jax.experimental.pallas import tpu as pltpu
from jax.sharding import PartitionSpec as P

HEADS = 16
HEAD_DIM = 64
FRAME_LEN = 196
LEN = 588
D = 384
FF = 2048
INNER = HEADS * HEAD_DIM
KEYS = 592
ROWS = 640
GROUP = 4
WIDE = GROUP * HEAD_DIM
GROUPS = HEADS // GROUP
QKV = 3 * WIDE
SMALL = 128
BLOCK = INNER + SMALL

epsilon = 1e-06
f32 = jnp.float32
bf16 = jnp.bfloat16

NN = (((1,), (0,)), ((), ()))
NT = (((1,), (1,)), ((), ()))
TN = (((0,), (0,)), ((), ()))

QUERY_BLOCKS = ((0, 128, 208), (128, 256, 400), (384, 256, 592))
KEY_RANGES = ((0, 208, 0), (208, 400, 128), (400, 592, 384))

VMEM = 56 * 1024 * 1024

BIAS_OUT, GAIN_TWO, SHIFT_TWO, BIAS_TWO, GAIN_ONE, SHIFT_ONE = (slice(k, k + 1) for k in range(6))


def dot(left, right, dims):
    return lax.dot_general(left, right, dims, preferred_element_type=f32)


def normalize(values):
    center = values - jnp.mean(values, axis=-1, keepdims=True)
    inverse = lax.rsqrt(jnp.mean(center * center, axis=-1, keepdims=True) + epsilon)
    return center * inverse, inverse


def normalize_back(grad_rows, norm_gain, scaled, inverse):
    scaled_grad = grad_rows * norm_gain
    return inverse * (
        scaled_grad
        - jnp.mean(scaled_grad, axis=-1, keepdims=True)
        - scaled * jnp.mean(scaled_grad * scaled, axis=-1, keepdims=True)
    )


def cost(micros):
    return pl.CostEstimate(flops=int(micros * 1.1e9), bytes_accessed=1024, transcendentals=0)


MASKS = (0, 2, 4, 6, 1, 3, 5, 7)


def owners(me, count):
    return [me ^ mask for mask in MASKS[:count]]


def staged_owners(me, count):
    if count == 1:
        return [0]
    first = 2 + 2 * (me & 1)
    second = 6 - first
    other = me ^ 1
    return [me, me ^ first, me ^ second, me ^ 6, other, other ^ second, other ^ first, other ^ 6]


def whole(shape):
    return pl.BlockSpec(
        shape, lambda *step: (0,) * len(shape), pipeline_mode=pl.Buffered(buffer_count=1)
    )


def prepare_kernel(one_ref, two_ref, hidden_bias_ref, out_ref, bias_ref, *refs):
    row_refs, (pack_ref, block_ref, rows_ref, columns_ref, wide_bias_ref) = refs[:6], refs[6:]
    rows, slot = one_ref.shape
    pack_ref[:rows, :slot] = one_ref[...]
    pack_ref[:rows, slot:] = two_ref[...]
    first_row = lax.broadcasted_iota(jnp.int32, (16, 1), 0) == 0
    hidden_bias = hidden_bias_ref[...].astype(f32).reshape(1, slot)
    pack_ref[rows:, :slot] = jnp.where(first_row, hidden_bias, 0.0).astype(bf16)
    pack_ref[rows:, slot:] = jnp.zeros((16, slot), bf16)
    turned = out_ref[...].T
    width = turned.shape[1]
    for r in range(D // rows):
        block_ref[:, r * width : (r + 1) * width] = turned[r * rows : (r + 1) * rows]
    rows_ref[...] = jnp.zeros_like(rows_ref)
    for k, ref in enumerate(row_refs):
        rows_ref[k : k + 1] = ref[...].astype(f32).reshape(1, D)
    columns_ref[...] = rows_ref[...].T
    wide_bias_ref[...] = bias_ref[...].astype(f32).reshape(1, 2 * INNER)


def prepare(w_fc1, w_fc2, bias_fc1, w_out, bias_qv, vectors):
    rows, slot = w_fc1.shape
    return pl.pallas_call(
        prepare_kernel,
        out_shape=[
            jax.ShapeDtypeStruct((rows + 16, 2 * slot), bf16),
            jax.ShapeDtypeStruct((rows, INNER), bf16),
            jax.ShapeDtypeStruct((8, D), f32),
            jax.ShapeDtypeStruct((D, 8), f32),
            jax.ShapeDtypeStruct((1, 2 * INNER), f32),
        ],
        cost_estimate=cost(2),
        name="prepare",
    )(w_fc1, w_fc2.T, bias_fc1, w_out, bias_qv, *vectors)


def sequence_rows(scr_ref, s):
    values = scr_ref[s * LEN : s * LEN + KEYS]
    row = lax.broadcasted_iota(jnp.int32, (KEYS, 1), 0)
    return jnp.where(row < LEN, values, 0.0)


def norm_kernel(tokens_ref, rows_ref, out_ref, scaled_ref, rows_scr):
    count = tokens_ref.shape[0]
    rows_scr[:count] = tokens_ref[...].astype(f32)
    rows_scr[count:] = jnp.zeros_like(rows_scr[count:])
    row = lax.broadcasted_iota(jnp.int32, (KEYS, 1), 0)
    for s in range(out_ref.shape[0]):
        scaled, _ = normalize(sequence_rows(rows_scr, s))
        normed = scaled * rows_ref[GAIN_ONE] + rows_ref[SHIFT_ONE]
        for ref, rows in ((scaled_ref, scaled), (out_ref, normed)):
            ref[s, :KEYS] = jnp.where(row < LEN, rows, 0.0).astype(bf16)
            ref[s, KEYS:] = jnp.zeros((ROWS - KEYS, D), bf16)


def first_norm(tokens, rows_in):
    seqs = tokens.shape[0] // LEN
    shape = jax.ShapeDtypeStruct((seqs, ROWS, D), bf16)
    return pl.pallas_call(
        norm_kernel,
        out_shape=[shape, shape],
        scratch_shapes=[pltpu.VMEM((seqs * KEYS, D), f32)],
        compiler_params=pltpu.CompilerParams(vmem_limit_bytes=14 * 1024 * 1024),
        cost_estimate=cost(2.5),
        name="first_norm",
    )(tokens, rows_in)


def attend_kernel(pieces, me_ref, normed_ref, bias_ref, mask_ref, *refs):
    parts, refs = refs[:pieces], refs[pieces:]
    projected_ref, mixed_ref, exp_ref, inverse_ref, wide_ref = refs[:5]
    hide_scr, score_scr, mixed_scr, total_scr, mask_scr = refs[5:]
    group, seq = pl.program_id(0), pl.program_id(1)

    @pl.when((group == 0) & (seq == 0))
    def _():
        rows = D // pieces
        for j, owner in enumerate(staged_owners(me_ref[0], pieces)):
            to = pl.ds(pl.multiple_of(owner * rows, 16), rows)
            for g in range(GROUPS):
                for k in range(3):
                    left = k * INNER + g * WIDE
                    at = g * QKV + k * WIDE
                    wide_ref[to, at : at + WIDE] = parts[j][:, left : left + WIDE]
        total_scr[...] = jnp.ones_like(total_scr)
        mask_scr[...] = jnp.zeros_like(mask_scr)
        count = hide_scr.shape[0]
        mask_scr[:count, :LEN] = mask_ref[...].astype(f32)
        turned = mask_scr[...].T
        key = lax.broadcasted_iota(jnp.int32, (KEYS, ROWS), 0)
        query = lax.broadcasted_iota(jnp.int32, (KEYS, ROWS), 1)
        later = ((query < FRAME_LEN) & (key >= FRAME_LEN)) | (
            (query < 2 * FRAME_LEN) & (key >= 2 * FRAME_LEN)
        )
        for s in range(count):
            usable = jnp.logical_not(later) & (turned[:KEYS, s : s + 1] > 0.5)
            hide_scr[s] = jnp.where(usable | (key == query), 0.0, -1e30)

    columns = pl.ds(pl.multiple_of(group * QKV, 128), QKV)
    projected = dot(normed_ref[seq, :KEYS], wide_ref[:, columns], NN)
    at = pl.multiple_of(group * WIDE, 128)
    queries = (projected[:, :WIDE] + bias_ref[:, pl.ds(at, WIDE)]).astype(bf16)
    projected_ref[0, :KEYS, :WIDE] = queries * bf16(HEAD_DIM**-0.5)
    projected_ref[0, :KEYS, WIDE : 2 * WIDE] = projected[:, WIDE : 2 * WIDE].astype(bf16)
    values = projected[:, 2 * WIDE :] + bias_ref[:, pl.ds(at + INNER, WIDE)]
    projected_ref[0, :KEYS, 2 * WIDE :] = values.astype(bf16)
    projected_ref[0, KEYS:] = jnp.zeros((ROWS - KEYS, QKV), bf16)
    from_ref = projected_ref.at[0]

    lane = lax.broadcasted_iota(jnp.int32, (1, 128), 1)
    units = [(h, b) for h in range(GROUP) for b in QUERY_BLOCKS]

    largest = {}
    flipped = {}

    def scores(unit):
        head, (start, width, keys) = units[unit]
        pair = head // 2 * 128
        mine = (lane < 64) if head % 2 == 0 else (lane >= 64)
        own_keys = from_ref[:keys, WIDE + pair : WIDE + pair + 128]
        own_keys = jnp.where(mine, own_keys, bf16(0))
        score = dot(own_keys, from_ref[start : start + width, pair : pair + 128], NT)
        score = score + hide_scr[seq, :keys, start : start + width]
        score_scr[unit % 3, :keys, :width] = score
        top = jnp.max(score.reshape(-1, 8, width), axis=0)
        largest[unit] = jnp.max(top, axis=0, keepdims=True)

    def exponents(unit):
        head, (start, width, keys) = units[unit]
        exponent = jnp.exp(score_scr[unit % 3, :keys, :width] - largest[unit])
        exp_ref[0, head, :keys, start : start + width] = exponent.astype(bf16)

    def mix(unit):
        head, (start, width, keys) = units[unit]
        pair = head // 2 * 128
        if head not in flipped:
            turned = from_ref[:KEYS, 2 * WIDE + pair : 2 * WIDE + pair + 128].T
            side = head % 2 * 64
            ones = jnp.ones((16, KEYS), bf16)
            flipped[head] = jnp.concatenate([turned[side : side + 64], ones])
        exponent = exp_ref[0, head, :keys, start : start + width]
        summed = dot(flipped[head][:, :keys], exponent, NN)
        values, total = summed[:64], summed[64:65]
        inverse = 1.0 / total
        mixed_scr[head * 64 : (head + 1) * 64, start : start + width] = values * inverse
        total_scr[head : head + 1, start : start + width] = inverse

    count = len(units)
    scores(0)
    scores(1)
    for unit in range(count + 2):
        if unit + 2 < count:
            scores(unit + 2)
        if unit < count:
            exponents(unit)
        if unit > 1:
            mix(unit - 2)
    mixed_ref[0] = mixed_scr[...].T.astype(bf16)
    inverse_ref[0, 0] = total_scr[...]


def attend(me, normed, parts, bias, mask):
    seqs = normed.shape[0]
    return pl.pallas_call(
        functools.partial(attend_kernel, len(parts)),
        grid=(GROUPS, seqs),
        in_specs=[
            pl.BlockSpec(memory_space=pltpu.SMEM),
            whole(normed.shape),
            whole(bias.shape),
            whole(mask.shape),
        ]
        + [whole(part.shape) for part in parts],
        out_specs=[
            pl.BlockSpec((1, ROWS, QKV), lambda g, s: (s, 0, g)),
            pl.BlockSpec((1, ROWS, WIDE), lambda g, s: (s, 0, g)),
            pl.BlockSpec((1, GROUP, KEYS, ROWS), lambda g, s: (s, g, 0, 0)),
            pl.BlockSpec((1, 1, 8, ROWS), lambda g, s: (s, g, 0, 0)),
            whole((D, GROUPS * QKV)),
        ],
        out_shape=[
            pltpu.HBM((seqs, ROWS, GROUPS * QKV), bf16),
            pltpu.VMEM((seqs, ROWS, INNER), bf16),
            pltpu.HBM((seqs, HEADS, KEYS, ROWS), bf16),
            pltpu.HBM((seqs, GROUPS, 8, ROWS), f32),
            pltpu.HBM((D, GROUPS * QKV), bf16),
        ],
        scratch_shapes=[
            pltpu.VMEM((seqs, KEYS, ROWS), f32),
            pltpu.VMEM((3, KEYS, 256), f32),
            pltpu.VMEM((WIDE, ROWS), f32),
            pltpu.VMEM((8, ROWS), f32),
            pltpu.VMEM((8, ROWS), f32),
        ],
        compiler_params=pltpu.CompilerParams(vmem_limit_bytes=24 * 1024 * 1024),
        cost_estimate=cost(22),
        name="attend",
    )(me, normed, bias, mask, *parts)


def forward_kernel(pieces, n_bias, chunk, me_ref, tokens_ref, grad_ref, rows_ref, *refs):
    bias_refs, refs = refs[:n_bias], refs[n_bias:]
    mixed_ref, refs = refs[0], refs[1:]
    parts, refs = refs[:pieces], refs[pieces:]
    out_ref, middle_grad_ref, branch_ref, out_wide_ref = refs[:4]
    n_out = 2 if pieces > 1 else 1
    send_refs, refs = refs[4 : 4 + n_out], refs[4 + n_out :]
    one_scr, two_scr, middle_scr, scaled_scr, inverse_scr, second_scr, second_t, grad_scr = refs[:8]
    grad_t, total_scr, back_scr, weight_scr, small_scr, bias_scr = refs[8:14]
    stage_scrs = (refs[14:16], refs[16:18])
    seqs = branch_ref.shape[0]
    step = pl.program_id(0)
    rows = D // pieces
    per_slot = FF // 4
    ones = jnp.ones((16, seqs * KEYS), bf16)

    def send(value_ref, at, width, left):
        if pieces == 1:
            send_refs[0][0, :, left : left + width] = value_ref[:, at : at + width].astype(bf16)
            return
        for j, owner in enumerate(owners(me_ref[0], pieces)):
            first = pl.multiple_of(owner * rows, 16)
            send_refs[j // 4][j % 4, 0, :, left : left + width] = value_ref[
                pl.ds(first, rows), at : at + width
            ].astype(bf16)

    def send_vectors():
        vectors = small_scr[...].astype(bf16)
        if pieces == 1:
            send_refs[0][0, :48, INNER:] = vectors
        else:
            for j in range(pieces):
                send_refs[j // 4][j % 4, 0, :, INNER:] = vectors

    def produce(index, stage):
        act_scr, pre_scr = stage_scrs[stage]
        hidden = pl.ds(pl.multiple_of(index * chunk, 128), chunk)
        pre = dot(second_scr[...], one_scr[:, hidden], NN) + bias_scr[:, hidden]
        half = 0.5 + 0.5 * lax.erf(pre * (0.5**0.5))
        act_scr[...] = (pre * half).astype(bf16)
        slope = half + pre * (jnp.exp2(pre * pre * -0.7213475204444817) * 0.3989422804014327)
        grad_act = dot(grad_scr[...], two_scr[:, hidden], NN)
        pre_scr[...] = (grad_act * slope).astype(bf16)

    def consume(index, stage):
        act_scr, pre_scr = stage_scrs[stage]
        hidden = pl.ds(pl.multiple_of(index * chunk, 128), chunk)
        total_scr[...] += dot(act_scr[...], two_scr[:, hidden], NT)
        back_scr[...] += dot(pre_scr[...], one_scr[:, hidden], NT)
        left = stage * chunk
        weight_scr[:, :chunk] = dot(second_t[...], pre_scr[...], NN)
        send(weight_scr, 0, chunk, left)
        weight_scr[:, chunk : 2 * chunk] = dot(grad_t[...], act_scr[...], NN)
        send(weight_scr, chunk, chunk, left + per_slot)
        hidden_sum = dot(ones, pre_scr[...], NN)[0:1]
        for r in range(chunk // 128):
            at = stage * (chunk // 128) + r
            small_scr[at : at + 1] = hidden_sum[:, r * 128 : (r + 1) * 128]

    @pl.when(step == 0)
    def _():
        for j, owner in enumerate(owners(me_ref[0], pieces)):
            first = pl.multiple_of(owner * rows, 16)
            if pieces == 1:
                out_wide_ref[...] = parts[0][:, :INNER]
            else:
                to = pl.ds(pl.multiple_of(owner * 128, 128), 128)
                for r in range(pieces):
                    out_wide_ref[r * rows : (r + 1) * rows, to] = parts[j][
                        :, r * 128 : (r + 1) * 128
                    ]
            for z in range(4):
                left = INNER + 2 * per_slot * z
                slot = slice(z * per_slot, (z + 1) * per_slot)
                one_scr[pl.ds(first, rows), slot] = parts[j][:, left : left + per_slot]
                two_scr[pl.ds(first, rows), slot] = parts[j][
                    :, left + per_slot : left + 2 * per_slot
                ]
        if n_bias == 1:
            bias_scr[...] = bias_refs[0][...].astype(f32)
        else:
            for z in range(4):
                row = bias_refs[z][rows:, :per_slot].astype(f32)[0:1]
                bias_scr[:, z * per_slot : (z + 1) * per_slot] = row
        count = tokens_ref.shape[0]
        for scr, ref in ((total_scr, tokens_ref), (back_scr, grad_ref)):
            scr[:count] = ref[...].astype(f32)
            scr[count:] = jnp.zeros_like(scr[count:])
        for s in range(seqs):
            block = slice(s * KEYS, (s + 1) * KEYS)
            grad_scr[block] = sequence_rows(back_scr, s).astype(bf16)
            middle = sequence_rows(total_scr, s) + rows_ref[BIAS_OUT]
            middle = middle + dot(mixed_ref[s, :KEYS], out_wide_ref[...], NT)
            middle_scr[block] = middle
            scaled, inverse = normalize(middle)
            scaled_scr[block] = scaled
            inverse_scr[block] = inverse
            second_scr[block] = (scaled * rows_ref[GAIN_TWO] + rows_ref[SHIFT_TWO]).astype(bf16)
        second_t[...] = second_scr[...].T
        grad_t[...] = grad_scr[...].T
        total_scr[...] = jnp.zeros_like(total_scr)
        back_scr[...] = jnp.zeros_like(back_scr)
        small_scr[...] = jnp.zeros_like(small_scr)
        produce(0, 0)

    @pl.when(step < 4)
    def _():
        produce(2 * step + 1, 1)
        consume(2 * step, 0)
        produce(jnp.minimum(2 * step + 2, FF // chunk - 1), 0)
        consume(2 * step + 1, 1)
        send_vectors()

    @pl.when(step == 4)
    def _():
        sums = [jnp.zeros((1, D), f32) for _ in range(2)]
        for s in range(seqs):
            block = slice(s * KEYS, (s + 1) * KEYS)
            output = middle_scr[block] + total_scr[block] + rows_ref[BIAS_TWO]
            total_scr[s * LEN : (s + 1) * LEN] = output[:LEN]
        out_ref[...] = total_scr[: seqs * LEN].astype(bf16)
        for s in range(seqs):
            block = slice(s * KEYS, (s + 1) * KEYS)
            scaled, inverse = scaled_scr[block], inverse_scr[block]
            grad_second = back_scr[block]
            grad_middle = grad_scr[block].astype(f32) + normalize_back(
                grad_second, rows_ref[GAIN_TWO], scaled, inverse
            )
            middle_grad_ref[s, :KEYS] = grad_middle
            branch_ref[s, :KEYS] = grad_middle.astype(bf16)
            branch_ref[s, KEYS:] = jnp.zeros((ROWS - KEYS, D), bf16)
            for k, term in enumerate((grad_second * scaled, grad_second)):
                sums[k] = sums[k] + jnp.sum(term, axis=0, keepdims=True)
        branch = jnp.concatenate([branch_ref[s, :KEYS] for s in range(seqs)], axis=0)
        sums.append(dot(ones, branch, NN)[0:1])
        sums.append(dot(ones, grad_scr[...], NN)[0:1])
        for k in range(4):
            for r in range(D // 128):
                at = 3 * k + r
                small_scr[at : at + 1] = sums[k][:, r * 128 : (r + 1) * 128]
        mixed = jnp.concatenate([mixed_ref[s, :KEYS] for s in range(seqs)], axis=0)
        weight_scr[...] = dot(branch, mixed, TN)
        if pieces == 1:
            send_refs[0][0, :, :INNER] = weight_scr[...].astype(bf16)
        else:
            for j, owner in enumerate(owners(me_ref[0], pieces)):
                to = pl.ds(pl.multiple_of(owner * 128, 128), 128)
                for r in range(pieces):
                    send_refs[j // 4][j % 4, 0, :, r * 128 : (r + 1) * 128] = weight_scr[
                        r * rows : (r + 1) * rows, to
                    ].astype(bf16)
        send_vectors()


def forward(me, tokens, cotangent, rows_in, biases, mixed, parts):
    seqs = tokens.shape[0] // LEN
    pieces = len(parts)
    chunk = 256
    if pieces > 1:
        send_shapes = [(pieces // 2, 5, D // pieces, BLOCK)] * 2
        send_specs = [pl.BlockSpec((pieces // 2, 1, D // pieces, BLOCK), lambda c: (0, c, 0, 0))] * 2
    else:
        send_shapes = [(5, D, BLOCK)]
        send_specs = [pl.BlockSpec((1, D, BLOCK), lambda c: (c, 0, 0))]
    rows3 = (seqs, ROWS, D)
    rows2 = (seqs * KEYS, D)
    return pl.pallas_call(
        functools.partial(forward_kernel, pieces, len(biases), chunk),
        grid=(5,),
        in_specs=[
            pl.BlockSpec(memory_space=pltpu.SMEM),
            whole(tokens.shape),
            whole(tokens.shape),
            whole((8, D)),
        ]
        + [whole(b.shape) for b in biases]
        + [whole(mixed.shape)]
        + [whole(p.shape) for p in parts],
        out_specs=[whole(tokens.shape), whole(rows3), whole(rows3), whole((D, INNER))]
        + send_specs,
        out_shape=[
            jax.ShapeDtypeStruct(tokens.shape, bf16),
            jax.ShapeDtypeStruct(rows3, f32),
            pltpu.VMEM(rows3, bf16),
            pltpu.VMEM((D, INNER), bf16),
        ]
        + [pltpu.VMEM(s, bf16) for s in send_shapes],
        scratch_shapes=[
            pltpu.VMEM((D, FF), bf16),
            pltpu.VMEM((D, FF), bf16),
            pltpu.VMEM(rows2, f32),
            pltpu.VMEM(rows2, f32),
            pltpu.VMEM((seqs * KEYS, 1), f32),
            pltpu.VMEM(rows2, bf16),
            pltpu.VMEM((D, seqs * KEYS), bf16),
            pltpu.VMEM(rows2, bf16),
            pltpu.VMEM((D, seqs * KEYS), bf16),
            pltpu.VMEM(rows2, f32),
            pltpu.VMEM(rows2, f32),
            pltpu.VMEM((D, INNER), f32),
            pltpu.VMEM((48, 128), f32),
            pltpu.VMEM((1, FF), f32),
        ]
        + [pltpu.VMEM((seqs * KEYS, chunk), bf16)] * 4,
        compiler_params=pltpu.CompilerParams(vmem_limit_bytes=36 * 1024 * 1024),
        cost_estimate=cost(30),
        name="forward",
    )(me, tokens, cotangent, rows_in, *biases, mixed, *parts)


def mixed_gradient_kernel(branch_ref, out_wide_ref, mixed_ref, grad_ref, delta_ref):
    lane = lax.broadcasted_iota(jnp.int32, (8, WIDE), 1)
    gather = (lane >> 6 == lax.broadcasted_iota(jnp.int32, (8, WIDE), 0)).astype(bf16)
    for g in range(delta_ref.shape[1]):
        columns = slice(g * WIDE, (g + 1) * WIDE)
        grad = dot(branch_ref[0], out_wide_ref[:, columns], NN).astype(bf16)
        grad_ref[0, :, columns] = grad
        product = grad.astype(f32) * mixed_ref[0, :, columns].astype(f32)
        first = product.astype(bf16)
        second = (product - first.astype(f32)).astype(bf16)
        delta_ref[0, g] = dot(gather, first, NT) + dot(gather, second, NT)


def mixed_gradient(branch, out_wide, mixed):
    seqs = branch.shape[0]
    each = 2
    columns = pl.BlockSpec((1, ROWS, each * WIDE), lambda s, g: (s, 0, g))
    return pl.pallas_call(
        mixed_gradient_kernel,
        grid=(seqs, GROUPS // each),
        in_specs=[
            pl.BlockSpec((1, ROWS, D), lambda s, g: (s, 0, 0)),
            pl.BlockSpec((D, each * WIDE), lambda s, g: (0, g)),
            columns,
        ],
        out_specs=[columns, pl.BlockSpec((1, each, 8, ROWS), lambda s, g: (s, g, 0, 0))],
        out_shape=[
            pltpu.HBM((seqs, ROWS, INNER), bf16),
            pltpu.HBM((seqs, GROUPS, 8, ROWS), f32),
        ],
        compiler_params=pltpu.CompilerParams(vmem_limit_bytes=16 * 1024 * 1024),
        cost_estimate=cost(5),
        name="mixed_gradient",
    )(branch, out_wide, mixed)


def backward_kernel(pieces, me_ref, *refs):
    grad_ref, delta_ref, scaled_ref, projected_ref, exp_ref, inverse_ref = refs[:6]
    wide_ref, norm_ref = refs[6:8]
    refs = refs[8:]
    n_out = 2 if pieces > 1 else 1
    back_ref = refs[0]
    send_refs = refs[1 : 1 + n_out]
    grad_scr, prob_scr, turned_scr, weight_scr, small_scr, sum_scr, norm_scr = refs[1 + n_out :]
    group, seq = pl.program_id(0), pl.program_id(1)
    groups, seqs = pl.num_programs(0), pl.num_programs(1)
    rows = D // pieces

    @pl.when((group == 0) & (seq == 0))
    def _():
        small_scr[...] = jnp.zeros_like(small_scr)
        norm_scr[...] = jnp.zeros_like(norm_scr)

    lane = lax.broadcasted_iota(jnp.int32, (1, 128), 1)
    low = lane < 64
    kept = {}
    turned_keys = {}

    def parts(head):
        columns = slice(head // 2 * 128, head // 2 * 128 + 128)
        return columns, head % 2, grad_ref[0, :, columns]

    def score_gradients(head):
        columns, half, grad = parts(head)
        mine = low if half == 0 else jnp.logical_not(low)
        value = projected_ref[0, :KEYS, 2 * WIDE + columns.start : 2 * WIDE + columns.stop]
        own_value = jnp.where(mine, value, bf16(0))
        inverse = inverse_ref[0, 0, head : head + 1].astype(bf16)
        delta = delta_ref[0, 0, head : head + 1]
        for start, width, keys in QUERY_BLOCKS:
            block = slice(start, start + width)
            change = dot(own_value[:keys], grad[block], NT) - delta[:, block]
            probability = exp_ref[0, head, :keys, block] * inverse[:, block]
            prob_scr[half, :keys, block] = probability
            grad_scr[half, :keys, block] = probability * change.astype(bf16)

    def input_gradients(head):
        columns, half, grad = parts(head)
        pair = head // 2
        query = projected_ref[0, :, columns]
        if half == 0:
            turned_keys[pair] = projected_ref[0, :KEYS, WIDE + columns.start : WIDE + columns.stop].T
        turned = turned_keys[pair]
        side = slice(64 * half, 64 * half + 64)
        for start, width, keys in QUERY_BLOCKS:
            block = slice(start, start + width)
            turned_scr[head * 64 : (head + 1) * 64, block] = dot(
                turned[side, :keys], grad_scr[half, :keys, block], NN
            ) * (HEAD_DIM**-0.5)
        for start, stop, seen in KEY_RANGES:
            value_grad = dot(prob_scr[half, start:stop, seen:], grad[seen:], NN)
            key_grad = dot(grad_scr[half, start:stop, seen:], query[seen:], NN)
            if half == 0:
                kept[start] = (value_grad, key_grad)
            else:
                at = slice(WIDE + columns.start, WIDE + columns.stop)
                back_ref[0, start:stop, at] = jnp.where(low, kept[start][1], key_grad).astype(bf16)
                at = slice(2 * WIDE + columns.start, 2 * WIDE + columns.stop)
                back_ref[0, start:stop, at] = jnp.where(low, kept[start][0], value_grad).astype(bf16)

    score_gradients(0)
    for head in range(GROUP):
        if head + 1 < GROUP:
            score_gradients(head + 1)
        input_gradients(head)
    back_ref[0, :KEYS, :WIDE] = turned_scr[...].T[:KEYS].astype(bf16)

    back = back_ref[0, :KEYS]
    weight = dot(scaled_ref[0, :KEYS], back, TN)
    total = dot(jnp.ones((16, KEYS), bf16), back, NN)[0:1]

    @pl.when(seq == 0)
    def _():
        weight_scr[...] = weight
        sum_scr[0:1] = total

    @pl.when(seq > 0)
    def _():
        weight_scr[...] += weight
        sum_scr[0:1] += total

    @pl.when(seq == seqs - 1)
    def _():
        sums = sum_scr[0:1]
        for r in range(WIDE // 128):
            at = group * (2 * WIDE // 128) + r
            small_scr[pl.ds(at, 1)] = sums[:, r * 128 : r * 128 + 128]
            at = at + WIDE // 128
            small_scr[pl.ds(at, 1)] = sums[:, 2 * WIDE + r * 128 : 2 * WIDE + r * 128 + 128]
        wide = wide_ref[...].astype(f32)
        scaled_weight = weight_scr[...]
        norm_scr[:, 0:1] += jnp.sum(scaled_weight * wide, axis=1, keepdims=True)
        norm_scr[:, 1:2] += jnp.sum(sums * wide, axis=1, keepdims=True)
        weight_scr[...] = scaled_weight * norm_ref[:, GAIN_ONE] + sums * norm_ref[:, SHIFT_ONE]
        start = pl.multiple_of(group * QKV, 128)
        if pieces == 1:
            send_refs[0][:, pl.ds(start, QKV)] = weight_scr[...].astype(bf16)
        else:
            for j, owner in enumerate(owners(me_ref[0], pieces)):
                first = pl.multiple_of(owner * rows, 16)
                send_refs[j // 4][j % 4, :, pl.ds(start, QKV)] = weight_scr[
                    pl.ds(first, rows)
                ].astype(bf16)

    @pl.when((group == groups - 1) & (seq == seqs - 1))
    def _():
        turned = norm_scr[...].T
        for k in range(2):
            for r in range(D // 128):
                small_scr[40 + 3 * k + r : 41 + 3 * k + r] = turned[
                    k : k + 1, r * 128 : (r + 1) * 128
                ]
        small = small_scr[...].astype(bf16)
        if pieces == 1:
            send_refs[0][:48, send_refs[0].shape[1] - SMALL :] = small
        else:
            for j in range(pieces):
                edge = send_refs[0].shape[2] - SMALL
                send_refs[j // 4][j % 4, :, edge:] = small


def backward(me, pieces, first_group, groups, grads, scaled, norm, saved):
    operands = [
        pltpu.with_memory_space_constraint(x, pltpu.HBM)
        for x in (*grads, scaled, saved[0], saved[2], saved[3], saved[4])
    ]
    seqs = scaled.shape[0]
    width = groups * QKV + SMALL
    if pieces > 1:
        send_shapes = [(pieces // 2, D // pieces, width)] * 2
    else:
        send_shapes = [(D, width)]
    columns = pl.BlockSpec((1, ROWS, WIDE), lambda g, s: (s, 0, g + first_group))
    heads = pl.BlockSpec((1, 1, 8, ROWS), lambda g, s: (s, g + first_group, 0, 0))
    rows_block = pl.BlockSpec((1, ROWS, D), lambda g, s: (s, 0, 0))
    return pl.pallas_call(
        functools.partial(backward_kernel, pieces),
        grid=(groups, seqs),
        in_specs=[
            pl.BlockSpec(memory_space=pltpu.SMEM),
            columns,
            heads,
            rows_block,
            pl.BlockSpec((1, ROWS, QKV), lambda g, s: (s, 0, g + first_group)),
            pl.BlockSpec((1, GROUP, KEYS, ROWS), lambda g, s: (s, g + first_group, 0, 0)),
            heads,
            pl.BlockSpec((D, QKV), lambda g, s: (0, g + first_group)),
            whole((D, 8)),
        ],
        out_specs=[pl.BlockSpec((1, ROWS, QKV), lambda g, s: (s, 0, g))]
        + [whole(s) for s in send_shapes],
        out_shape=[jax.ShapeDtypeStruct((seqs, ROWS, groups * QKV), bf16)]
        + [jax.ShapeDtypeStruct(s, bf16) for s in send_shapes],
        scratch_shapes=[
            pltpu.VMEM((2, KEYS, ROWS), bf16),
            pltpu.VMEM((2, KEYS, ROWS), bf16),
            pltpu.VMEM((WIDE, ROWS), f32),
            pltpu.VMEM((D, QKV), f32),
            pltpu.VMEM((48, 128), f32),
            pltpu.VMEM((8, QKV), f32),
            pltpu.VMEM((D, 128), f32),
        ],
        compiler_params=pltpu.CompilerParams(vmem_limit_bytes=23 * 1024 * 1024),
        cost_estimate=cost(11 * groups),
        name="backward",
    )(me, *operands, norm)


def early_kernel(back_ref, wide_ref, out_ref):
    for s in range(out_ref.shape[0]):
        grad = dot(back_ref[s, :KEYS], wide_ref[...], NT)
        before = jnp.where(pl.program_id(0) == 0, 0.0, out_ref[s])
        out_ref[s] = before + grad


def early_gradient(back, weights):
    seqs, groups = back.shape[0], back.shape[2] // QKV
    return pl.pallas_call(
        early_kernel,
        grid=(groups,),
        in_specs=[
            pl.BlockSpec((seqs, ROWS, QKV), lambda g: (0, 0, g)),
            pl.BlockSpec((D, QKV), lambda g: (0, g)),
        ],
        out_specs=whole((seqs, KEYS, D)),
        out_shape=jax.ShapeDtypeStruct((seqs, KEYS, D), f32),
        compiler_params=pltpu.CompilerParams(vmem_limit_bytes=14 * 1024 * 1024),
        cost_estimate=cost(5),
        name="early_gradient",
    )(back, weights)


def input_kernel(
    tokens_ref, middle_grad_ref, rows_ref, early_ref, back_ref, wide_ref, out_ref, rows_scr
):
    count = tokens_ref.shape[0]
    rows_scr[:count] = tokens_ref[...].astype(f32)
    for s in range(middle_grad_ref.shape[0]):
        grad_first = early_ref[s] + dot(back_ref[s, :KEYS], wide_ref[...], NT)
        given = slice(s * LEN, (s + 1) * LEN)
        scaled, inverse = normalize(rows_scr[given])
        rows_scr[given] = middle_grad_ref[s, :LEN] + normalize_back(
            grad_first[:LEN], rows_ref[GAIN_ONE], scaled, inverse
        )
    out_ref[...] = rows_scr[:count]


def input_gradient(tokens, middle_grad, rows_in, early, back, weights):
    return pl.pallas_call(
        input_kernel,
        grid=(1,),
        in_specs=[
            whole(tokens.shape),
            whole(middle_grad.shape),
            whole(rows_in.shape),
            whole(early.shape),
            whole(back.shape),
            pl.BlockSpec((D, QKV), lambda g: (0, GROUPS - 1)),
        ],
        out_specs=whole(tokens.shape),
        out_shape=jax.ShapeDtypeStruct(tokens.shape, f32),
        scratch_shapes=[pltpu.VMEM((middle_grad.shape[0] * KEYS, D), f32)],
        compiler_params=pltpu.CompilerParams(vmem_limit_bytes=16 * 1024 * 1024),
        cost_estimate=cost(4),
        name="input_gradient",
    )(tokens, middle_grad, rows_in, early, back, weights)


def join_lines(values):
    return jnp.concatenate([values[k : k + 1] for k in range(values.shape[0])], axis=1)


def hidden_end_kernel(block_ref, rest_ref, arrived_ref, one_ref, two_ref, bias_ref, out_ref, *refs):
    rows, slot = one_ref.shape
    block = block_ref[...] + arrived_ref[:, :BLOCK].astype(f32)
    rest = rest_ref[...] + arrived_ref[:, BLOCK:].astype(f32)
    one_ref[...] = block[:, :slot]
    two_ref[...] = block[:, slot : 2 * slot]
    bias_ref[...] = join_lines(block[: slot // 128, INNER:]).reshape(slot)
    width = out_ref.shape[0]
    parts = [rest[:, r * width : (r + 1) * width] for r in range(INNER // width)]
    out_ref[...] = jnp.concatenate(parts, axis=0).T
    for k, ref in enumerate(refs):
        ref[...] = join_lines(rest[3 * k : 3 * k + 3, INNER:]).reshape(D)


def hidden_end(block, rest, arrived, slot):
    rows = block.shape[0]
    width = INNER // (D // rows)
    vector = jax.ShapeDtypeStruct((D,), f32)
    return pl.pallas_call(
        hidden_end_kernel,
        out_shape=[
            jax.ShapeDtypeStruct((rows, slot), f32),
            jax.ShapeDtypeStruct((rows, slot), f32),
            jax.ShapeDtypeStruct((slot,), f32),
            jax.ShapeDtypeStruct((width, D), f32),
        ]
        + [vector] * 4,
        compiler_params=pltpu.CompilerParams(vmem_limit_bytes=8 * 1024 * 1024),
        cost_estimate=cost(2),
        name="hidden_end",
    )(block, rest, arrived)


def heads_end_kernel(early_ref, early_line_ref, late_ref, late_line_ref, weight_ref, bias_ref, *refs):
    early = early_ref[...] + early_line_ref[...].astype(f32)
    late = late_ref[...] + late_line_ref[...].astype(f32)
    lines = WIDE // 128
    norms, group = 0.0, 0
    for part in (early, late):
        edge = part.shape[1] - SMALL
        for g in range(edge // QKV):
            for k in range(3):
                left = g * QKV + k * WIDE
                to = k * INNER + group * WIDE
                weight_ref[:, to : to + WIDE] = part[:, left : left + WIDE]
            for k in range(2):
                first = (2 * g + k) * lines
                values = join_lines(part[first : first + lines, edge:])
                at = k * INNER + group * WIDE
                bias_ref[at : at + WIDE] = values.reshape(WIDE)
            group += 1
        norms = norms + part[40:48, edge:]
    for k, ref in enumerate(refs):
        ref[...] = join_lines(norms[3 * k : 3 * k + 3]).reshape(D)


def heads_end(early, early_line, late, late_line):
    vector = jax.ShapeDtypeStruct((D,), f32)
    return pl.pallas_call(
        heads_end_kernel,
        out_shape=[
            jax.ShapeDtypeStruct((early.shape[0], 3 * INNER), f32),
            jax.ShapeDtypeStruct((2 * INNER,), f32),
            vector,
            vector,
        ],
        compiler_params=pltpu.CompilerParams(vmem_limit_bytes=8 * 1024 * 1024),
        cost_estimate=cost(2),
        name="heads_end",
    )(early, early_line, late, late_line)


def swap(values, mask):
    size = lax.axis_size("tok")
    return lax.ppermute(values, "tok", [(i, i ^ mask) for i in range(size)])


def swap_half_plane(values, stage):
    size = lax.axis_size("tok")
    pairs = [(t, t ^ (2 if (t % 2 == 0) == (stage == 0) else 4)) for t in range(size)]
    return lax.ppermute(values, "tok", pairs)


def swap_half_line(values, stage):
    tok, mlp = lax.axis_size("tok"), lax.axis_size("mlp")
    pairs = []
    for t in range(tok):
        for z in range(mlp):
            far = (t % 2 == 0) == (stage == 0)
            pairs.append((t * mlp + z, t * mlp + (z ^ (2 if far else 1))))
    return lax.ppermute(values.astype(bf16), ("tok", "mlp"), pairs)


def after(values, *earlier):
    return lax.optimization_barrier((values,) + earlier)


def wide(values):
    return values.astype(f32)


def join(kept, arrived):
    return (wide(kept) + wide(arrived)).astype(bf16)


def body(
    tokens,
    action_mask,
    ln1_gain,
    ln1_bias,
    w_qkv,
    bias_qv,
    w_out,
    bias_out,
    ln2_gain,
    ln2_bias,
    w_fc1,
    bias_fc1,
    w_fc2,
    bias_fc2,
    out_grad,
):
    rows = w_qkv.shape[0]
    tok = lax.axis_size("tok")
    mlp = lax.axis_size("mlp")
    slot = w_fc1.shape[1]
    fast = tok == 8 and mlp == 4
    pieces = tok if fast else 1
    me = lax.axis_index("tok").astype(jnp.int32).reshape(1)
    chips = (2, 4, 6)
    odd = (me[0] & 1) == 1

    def pick(if_odd, if_even):
        return jnp.where(odd, if_odd, if_even)


    vectors = (bias_out, ln2_gain, ln2_bias, bias_fc2, ln1_gain, ln1_bias)
    me_a = me
    if fast:
        first_near = [swap_half_plane(w_qkv, stage) for stage in (0, 1)]
        first_near.append(swap_half_plane(first_near[0], 1))
        first_other = swap(w_qkv, 1)
        hidden_pack, out_block, rows_in, columns_in, bias_pair = prepare(
            w_fc1, w_fc2, bias_fc1, w_out, bias_qv, vectors
        )
        line = jnp.stack([hidden_pack, swap_half_line(hidden_pack, 0)])
        line = jnp.concatenate([line, swap_half_line(line, 1)])
        line = [line[0], pick(line[1], line[2]), pick(line[2], line[1]), line[3]]
        norm_tokens, first_near[0] = after(tokens, first_near[0])
        normed, scaled = first_norm(norm_tokens, rows_in)
        first_parts = [w_qkv] + first_near + [first_other] + [swap(p, 1) for p in first_near]
        hidden_own = jnp.concatenate([out_block] + [part[:rows] for part in line], axis=1)
        me_a, hidden_own = after(me, hidden_own)
        hidden_near = [swap(hidden_own, mask) for mask in chips + (1,)]
        biases = line
    else:
        rows_in = jnp.pad(wide(jnp.stack(vectors)), ((0, 2), (0, 0)))
        columns_in = rows_in.T
        bias_pair = wide(bias_qv).reshape(1, -1)
        normed, scaled = first_norm(tokens, rows_in)
        first_parts = [lax.all_gather(w_qkv, "tok", axis=0, tiled=True)]
        line = lax.all_gather(jnp.concatenate([w_fc1, w_fc2.T], axis=1), "mlp", axis=1, tiled=True)
        line = lax.all_gather(line, "tok", axis=0, tiled=True)
        biases = [lax.all_gather(bias_fc1, "mlp", axis=0, tiled=True).reshape(1, -1)]
        out_all = lax.all_gather(w_out, "tok", axis=0, tiled=True).T
        hidden_parts = [jnp.concatenate([out_all, line], axis=1)]

    saved = list(attend(me_a, normed, first_parts, bias_pair, action_mask))
    weights = saved[4]
    if fast:
        saved[1], *hidden_near = after(saved[1], *hidden_near)
        hidden_other = hidden_near.pop()
        hidden_parts = [hidden_own] + hidden_near + [hidden_other]
        hidden_parts = hidden_parts + [swap(part, 1) for part in hidden_near]

    output, middle_grad, branch, out_wide, *hidden_sends = forward(
        me, tokens, out_grad, rows_in, biases, saved[1], hidden_parts
    )

    grads = list(mixed_gradient(branch, out_wide, saved[1]))

    def back(me, group, count):
        return backward(me, pieces, group, count, grads, scaled, columns_in, saved)

    if not fast:
        back_a, sends_a = back(me, 0, 3)
        back_b, sends_b = back(me, 3, 1)
        early = early_gradient(back_a, weights)
        input_grad = input_gradient(tokens, middle_grad, rows_in, early, back_b, weights)
        return slow_end(output, input_grad, hidden_sends[0], (sends_a, sends_b), slot)

    arrived = swap(hidden_sends[1], 1)
    grads[0], arrived = after(grads[0], arrived)
    hidden = join(hidden_sends[0], arrived)
    me_1, hidden = after(me, hidden)
    near = [swap(hidden[k], chips[k - 1]) for k in (1, 2, 3)]
    back_a, *sends_a = back(me_1, 0, 3)

    back_a, *near = after(back_a, *near)
    hidden = wide(hidden[0]) + wide(near[0]) + wide(near[1]) + wide(near[2])
    sent = jnp.stack([pick(hidden[1], hidden[2]), hidden[3], hidden[4]]).astype(bf16)
    group_a = join(sends_a[0], swap(sends_a[1], 1))
    me_2, group_a, sent = after(me, group_a, sent)
    line_1 = swap_half_line(sent, 0)
    near_a = [swap(group_a[k], chips[k - 1]) for k in (1, 2, 3)]
    back_b, *sends_b = back(me_2, 3, 1)

    back_b, line_1, *near_a = after(back_b, line_1, *near_a)
    total_a = wide(group_a[0]) + wide(near_a[0]) + wide(near_a[1]) + wide(near_a[2])
    sent, kept_b, sent_b = after(total_a.astype(bf16), *sends_b)
    line_a = swap_half_line(sent, 1)
    group_b = join(kept_b, swap(sent_b, 1))
    line_1, group_b = after(line_1, group_b)
    block = hidden[0] + wide(line_1[0])
    middle_block = pick(hidden[2], hidden[1]) + wide(line_1[1])
    rest = hidden[4] + wide(line_1[2])
    sent = jnp.concatenate([middle_block, rest], axis=1).astype(bf16)
    group_b, sent = after(group_b, sent)
    line_2 = swap_half_line(sent, 1)
    near_b = [swap(group_b[k], chips[k - 1]) for k in (1, 2, 3)]
    line_a, *near_b = after(line_a, *near_b)
    total_b = wide(group_b[0]) + wide(near_b[0]) + wide(near_b[1]) + wide(near_b[2])
    total_a = total_a + wide(line_a)
    back_a, sent_b, sent_a = after(back_a, total_b.astype(bf16), total_a.astype(bf16))
    line_b = swap_half_line(sent_b, 0)
    line_a = swap_half_line(sent_a, 0)
    early = early_gradient(back_a, weights)

    early, line_b = after(early, line_b)
    total_b = total_b + wide(line_b)
    early, sent = after(early, total_b.astype(bf16))
    line_b = swap_half_line(sent, 1)
    input_grad = input_gradient(tokens, middle_grad, rows_in, early, back_b, weights)

    input_grad, line_a, line_b, line_2 = after(input_grad, line_a, line_b, line_2)
    hidden_grads = hidden_end(block, rest, line_2, slot)
    one_grad = hidden_grads[0]
    qkv_grad, bias_grad, gain_grad, shift_grad = heads_end(total_a, line_a, total_b, line_b)
    _, two_grad, hidden_bias_grad, out_rows, *vector_grads = hidden_grads
    return (
        output,
        input_grad,
        gain_grad,
        shift_grad,
        qkv_grad,
        bias_grad,
        out_rows,
        vector_grads[2],
        vector_grads[0],
        vector_grads[1],
        one_grad,
        hidden_bias_grad,
        two_grad.T,
        vector_grads[3],
    )


def slow_end(output, input_grad, hidden, sends, slot):
    def scatter(values):
        values = lax.psum_scatter(wide(values), "tok", scatter_dimension=0, tiled=True)
        return lax.psum(values, "mlp")

    hidden = wide(hidden)
    blocks = jnp.concatenate([hidden[k, :, :INNER] for k in range(4)], axis=1)
    blocks = lax.psum_scatter(blocks, "tok", scatter_dimension=0, tiled=True)
    hidden_sum = lax.psum_scatter(blocks, "mlp", scatter_dimension=1, tiled=True)
    out_rows = scatter(hidden[4, :, :INNER].T)
    lines = slot // 128
    small = lax.psum(hidden[:, :48, INNER:], ("tok", "mlp"))
    bias_sum = lax.dynamic_index_in_dim(small[:4, :lines], lax.axis_index("mlp"), 0, False)
    small = small[4]
    weights = [scatter(s[:, :-SMALL]) for s in sends]
    smalls = [lax.psum(wide(s[:48, -SMALL:]), ("tok", "mlp")) for s in sends]
    return results(output, input_grad, weights, smalls, out_rows, small, hidden_sum, bias_sum)


def results(output, input_grad, weights, smalls, out_rows, small, hidden_sum, bias_sum):
    blocks = []
    for part in weights:
        blocks += [part[:, at : at + WIDE] for at in range(0, part.shape[1], WIDE)]
    qkv_grad = jnp.concatenate([block for k in range(3) for block in blocks[k::3]], axis=1)
    lines = WIDE // 128
    biases = []
    for part, weight in zip(smalls, weights):
        count = 2 * (weight.shape[1] // QKV)
        biases += [part[k * lines : (k + 1) * lines] for k in range(count)]
    bias_grad = jnp.concatenate(biases[0::2] + biases[1::2], axis=0).reshape(-1)
    norm_grad = smalls[0][40:46] + smalls[1][40:46]
    vectors = [small[3 * k : 3 * k + 3].reshape(-1) for k in range(4)]
    slot = hidden_sum.shape[1] // 2
    return (
        output,
        input_grad,
        norm_grad[:3].reshape(-1),
        norm_grad[3:].reshape(-1),
        qkv_grad,
        bias_grad,
        out_rows,
        vectors[2],
        vectors[0],
        vectors[1],
        hidden_sum[:, :slot],
        bias_sum.reshape(-1),
        hidden_sum[:, slot:].T,
        vectors[3],
    )


def solution(mesh):
    placed = (
        P(("tok", "mlp"), None),
        P(("tok", "mlp"), None),
        P(),
        P(),
        P("tok", None),
        P(),
        P("tok", None),
        P(),
        P(),
        P(),
        P("tok", "mlp"),
        P("mlp"),
        P("mlp", "tok"),
        P(),
        P(("tok", "mlp"), None),
    )
    return jax.shard_map(
        body,
        mesh=mesh,
        in_specs=placed,
        out_specs=(
            P(("tok", "mlp"), None),
            P(("tok", "mlp"), None),
            P(),
            P(),
            P("tok", None),
            P(),
            P("tok", None),
            P(),
            P(),
            P(),
            P("tok", "mlp"),
            P("mlp"),
            P("mlp", "tok"),
            P(),
        ),
        check_vma=False,
    )
```

```python
import functools

import jax
import jax.numpy as jnp
from jax import lax
from jax.experimental import pallas as pl
from jax.experimental.pallas import tpu as pltpu
from jax.sharding import PartitionSpec as P

HEADS = 16
HEAD_DIM = 64
FRAME_LEN = 196
LEN = 588
D = 384
FF = 2048
INNER = HEADS * HEAD_DIM
KEYS = 592
ROWS = 640
GROUP = 4
WIDE = GROUP * HEAD_DIM
GROUPS = HEADS // GROUP
QKV = 3 * WIDE
SMALL = 128
BLOCK = INNER + SMALL

epsilon = 1e-06
f32 = jnp.float32
bf16 = jnp.bfloat16

NN = (((1,), (0,)), ((), ()))
NT = (((1,), (1,)), ((), ()))
TN = (((0,), (0,)), ((), ()))

QUERY_BLOCKS = ((0, 128, 208), (128, 256, 400), (384, 256, 592))
KEY_RANGES = ((0, 208, 0), (208, 400, 128), (400, 592, 384))

VMEM = 56 * 1024 * 1024

BIAS_OUT, GAIN_TWO, SHIFT_TWO, BIAS_TWO, GAIN_ONE, SHIFT_ONE = (slice(k, k + 1) for k in range(6))


def dot(left, right, dims):
    return lax.dot_general(left, right, dims, preferred_element_type=f32)


def normalize(values):
    center = values - jnp.mean(values, axis=-1, keepdims=True)
    inverse = lax.rsqrt(jnp.mean(center * center, axis=-1, keepdims=True) + epsilon)
    return center * inverse, inverse


def normalize_back(grad_rows, norm_gain, scaled, inverse):
    scaled_grad = grad_rows * norm_gain
    return inverse * (
        scaled_grad
        - jnp.mean(scaled_grad, axis=-1, keepdims=True)
        - scaled * jnp.mean(scaled_grad * scaled, axis=-1, keepdims=True)
    )


def cost(micros):
    return pl.CostEstimate(flops=int(micros * 1.1e9), bytes_accessed=1024, transcendentals=0)


MASKS = (0, 2, 4, 6, 1, 3, 5, 7)


def owners(me, count):
    return [me ^ mask for mask in MASKS[:count]]


def staged_owners(me, count):
    if count == 1:
        return [0]
    first = 2 + 2 * (me & 1)
    second = 6 - first
    other = me ^ 1
    return [me, me ^ first, me ^ second, me ^ 6, other, other ^ second, other ^ first, other ^ 6]


def whole(shape):
    return pl.BlockSpec(
        shape, lambda *step: (0,) * len(shape), pipeline_mode=pl.Buffered(buffer_count=1)
    )


def prepare_kernel(one_ref, two_ref, hidden_bias_ref, out_ref, bias_ref, *refs):
    row_refs, (pack_ref, block_ref, rows_ref, columns_ref, wide_bias_ref) = refs[:6], refs[6:]
    rows, slot = one_ref.shape
    pack_ref[:rows, :slot] = one_ref[...]
    pack_ref[:rows, slot:] = two_ref[...]
    first_row = lax.broadcasted_iota(jnp.int32, (16, 1), 0) == 0
    hidden_bias = hidden_bias_ref[...].astype(f32).reshape(1, slot)
    pack_ref[rows:, :slot] = jnp.where(first_row, hidden_bias, 0.0).astype(bf16)
    pack_ref[rows:, slot:] = jnp.zeros((16, slot), bf16)
    turned = out_ref[...].T
    width = turned.shape[1]
    for r in range(D // rows):
        block_ref[:, r * width : (r + 1) * width] = turned[r * rows : (r + 1) * rows]
    rows_ref[...] = jnp.zeros_like(rows_ref)
    for k, ref in enumerate(row_refs):
        rows_ref[k : k + 1] = ref[...].astype(f32).reshape(1, D)
    columns_ref[...] = rows_ref[...].T
    wide_bias_ref[...] = bias_ref[...].astype(f32).reshape(1, 2 * INNER)


def prepare(w_fc1, w_fc2, bias_fc1, w_out, bias_qv, vectors):
    rows, slot = w_fc1.shape
    return pl.pallas_call(
        prepare_kernel,
        out_shape=[
            jax.ShapeDtypeStruct((rows + 16, 2 * slot), bf16),
            jax.ShapeDtypeStruct((rows, INNER), bf16),
            jax.ShapeDtypeStruct((8, D), f32),
            jax.ShapeDtypeStruct((D, 8), f32),
            jax.ShapeDtypeStruct((1, 2 * INNER), f32),
        ],
        cost_estimate=cost(2),
        name="prepare",
    )(w_fc1, w_fc2.T, bias_fc1, w_out, bias_qv, *vectors)


def sequence_rows(scr_ref, s):
    values = scr_ref[s * LEN : s * LEN + KEYS]
    row = lax.broadcasted_iota(jnp.int32, (KEYS, 1), 0)
    return jnp.where(row < LEN, values, 0.0)


def norm_kernel(tokens_ref, rows_ref, out_ref, scaled_ref, rows_scr):
    count = tokens_ref.shape[0]
    rows_scr[:count] = tokens_ref[...].astype(f32)
    rows_scr[count:] = jnp.zeros_like(rows_scr[count:])
    row = lax.broadcasted_iota(jnp.int32, (KEYS, 1), 0)
    for s in range(out_ref.shape[0]):
        scaled, _ = normalize(sequence_rows(rows_scr, s))
        normed = scaled * rows_ref[GAIN_ONE] + rows_ref[SHIFT_ONE]
        for ref, rows in ((scaled_ref, scaled), (out_ref, normed)):
            ref[s, :KEYS] = jnp.where(row < LEN, rows, 0.0).astype(bf16)
            ref[s, KEYS:] = jnp.zeros((ROWS - KEYS, D), bf16)


def first_norm(tokens, rows_in):
    seqs = tokens.shape[0] // LEN
    shape = jax.ShapeDtypeStruct((seqs, ROWS, D), bf16)
    return pl.pallas_call(
        norm_kernel,
        out_shape=[shape, shape],
        scratch_shapes=[pltpu.VMEM((seqs * KEYS, D), f32)],
        compiler_params=pltpu.CompilerParams(vmem_limit_bytes=14 * 1024 * 1024),
        cost_estimate=cost(2.5),
        name="first_norm",
    )(tokens, rows_in)


def attend_kernel(pieces, me_ref, normed_ref, bias_ref, mask_ref, *refs):
    parts, refs = refs[:pieces], refs[pieces:]
    projected_ref, mixed_ref, exp_ref, inverse_ref, wide_ref = refs[:5]
    hide_scr, score_scr, mixed_scr, total_scr, mask_scr = refs[5:]
    group, seq = pl.program_id(0), pl.program_id(1)

    @pl.when((group == 0) & (seq == 0))
    def _():
        rows = D // pieces
        for j, owner in enumerate(staged_owners(me_ref[0], pieces)):
            to = pl.ds(pl.multiple_of(owner * rows, 16), rows)
            for g in range(GROUPS):
                for k in range(3):
                    left = k * INNER + g * WIDE
                    at = g * QKV + k * WIDE
                    wide_ref[to, at : at + WIDE] = parts[j][:, left : left + WIDE]
        total_scr[...] = jnp.ones_like(total_scr)
        mask_scr[...] = jnp.zeros_like(mask_scr)
        count = hide_scr.shape[0]
        mask_scr[:count, :LEN] = mask_ref[...].astype(f32)
        turned = mask_scr[...].T
        key = lax.broadcasted_iota(jnp.int32, (KEYS, ROWS), 0)
        query = lax.broadcasted_iota(jnp.int32, (KEYS, ROWS), 1)
        later = ((query < FRAME_LEN) & (key >= FRAME_LEN)) | (
            (query < 2 * FRAME_LEN) & (key >= 2 * FRAME_LEN)
        )
        for s in range(count):
            usable = jnp.logical_not(later) & (turned[:KEYS, s : s + 1] > 0.5)
            hide_scr[s] = jnp.where(usable | (key == query), 0.0, -1e30)

    columns = pl.ds(pl.multiple_of(group * QKV, 128), QKV)
    projected = dot(normed_ref[seq, :KEYS], wide_ref[:, columns], NN)
    at = pl.multiple_of(group * WIDE, 128)
    queries = (projected[:, :WIDE] + bias_ref[:, pl.ds(at, WIDE)]).astype(bf16)
    projected_ref[0, :KEYS, :WIDE] = queries * bf16(HEAD_DIM**-0.5)
    projected_ref[0, :KEYS, WIDE : 2 * WIDE] = projected[:, WIDE : 2 * WIDE].astype(bf16)
    values = projected[:, 2 * WIDE :] + bias_ref[:, pl.ds(at + INNER, WIDE)]
    projected_ref[0, :KEYS, 2 * WIDE :] = values.astype(bf16)
    projected_ref[0, KEYS:] = jnp.zeros((ROWS - KEYS, QKV), bf16)
    from_ref = projected_ref.at[0]

    lane = lax.broadcasted_iota(jnp.int32, (1, 128), 1)
    units = [(h, b) for h in range(GROUP) for b in QUERY_BLOCKS]

    largest = {}
    flipped = {}

    def scores(unit):
        head, (start, width, keys) = units[unit]
        pair = head // 2 * 128
        mine = (lane < 64) if head % 2 == 0 else (lane >= 64)
        own_keys = from_ref[:keys, WIDE + pair : WIDE + pair + 128]
        own_keys = jnp.where(mine, own_keys, bf16(0))
        score = dot(own_keys, from_ref[start : start + width, pair : pair + 128], NT)
        score = score + hide_scr[seq, :keys, start : start + width]
        score_scr[unit % 3, :keys, :width] = score
        top = jnp.max(score.reshape(-1, 8, width), axis=0)
        largest[unit] = jnp.max(top, axis=0, keepdims=True)

    def exponents(unit):
        head, (start, width, keys) = units[unit]
        exponent = jnp.exp(score_scr[unit % 3, :keys, :width] - largest[unit])
        exp_ref[0, head, :keys, start : start + width] = exponent.astype(bf16)

    def mix(unit):
        head, (start, width, keys) = units[unit]
        pair = head // 2 * 128
        if head not in flipped:
            turned = from_ref[:KEYS, 2 * WIDE + pair : 2 * WIDE + pair + 128].T
            side = head % 2 * 64
            ones = jnp.ones((16, KEYS), bf16)
            flipped[head] = jnp.concatenate([turned[side : side + 64], ones])
        exponent = exp_ref[0, head, :keys, start : start + width]
        summed = dot(flipped[head][:, :keys], exponent, NN)
        values, total = summed[:64], summed[64:65]
        inverse = 1.0 / total
        mixed_scr[head * 64 : (head + 1) * 64, start : start + width] = values * inverse
        total_scr[head : head + 1, start : start + width] = inverse

    count = len(units)
    scores(0)
    scores(1)
    for unit in range(count + 2):
        if unit + 2 < count:
            scores(unit + 2)
        if unit < count:
            exponents(unit)
        if unit > 1:
            mix(unit - 2)
    mixed_ref[0] = mixed_scr[...].T.astype(bf16)
    inverse_ref[0, 0] = total_scr[...]


def attend(me, normed, parts, bias, mask):
    seqs = normed.shape[0]
    return pl.pallas_call(
        functools.partial(attend_kernel, len(parts)),
        grid=(GROUPS, seqs),
        in_specs=[
            pl.BlockSpec(memory_space=pltpu.SMEM),
            whole(normed.shape),
            whole(bias.shape),
            whole(mask.shape),
        ]
        + [whole(part.shape) for part in parts],
        out_specs=[
            pl.BlockSpec((1, ROWS, QKV), lambda g, s: (s, 0, g)),
            pl.BlockSpec((1, ROWS, WIDE), lambda g, s: (s, 0, g)),
            pl.BlockSpec((1, GROUP, KEYS, ROWS), lambda g, s: (s, g, 0, 0)),
            pl.BlockSpec((1, 1, 8, ROWS), lambda g, s: (s, g, 0, 0)),
            whole((D, GROUPS * QKV)),
        ],
        out_shape=[
            pltpu.HBM((seqs, ROWS, GROUPS * QKV), bf16),
            pltpu.VMEM((seqs, ROWS, INNER), bf16),
            pltpu.HBM((seqs, HEADS, KEYS, ROWS), bf16),
            pltpu.HBM((seqs, GROUPS, 8, ROWS), f32),
            pltpu.HBM((D, GROUPS * QKV), bf16),
        ],
        scratch_shapes=[
            pltpu.VMEM((seqs, KEYS, ROWS), f32),
            pltpu.VMEM((3, KEYS, 256), f32),
            pltpu.VMEM((WIDE, ROWS), f32),
            pltpu.VMEM((8, ROWS), f32),
            pltpu.VMEM((8, ROWS), f32),
        ],
        compiler_params=pltpu.CompilerParams(vmem_limit_bytes=24 * 1024 * 1024),
        cost_estimate=cost(22),
        name="attend",
    )(me, normed, bias, mask, *parts)


def forward_kernel(pieces, n_bias, chunk, me_ref, tokens_ref, grad_ref, rows_ref, *refs):
    bias_refs, refs = refs[:n_bias], refs[n_bias:]
    mixed_ref, refs = refs[0], refs[1:]
    parts, refs = refs[:pieces], refs[pieces:]
    out_ref, middle_grad_ref, branch_ref, out_wide_ref = refs[:4]
    n_out = 2 if pieces > 1 else 1
    send_refs, refs = refs[4 : 4 + n_out], refs[4 + n_out :]
    one_scr, two_scr, middle_scr, scaled_scr, inverse_scr, second_scr, second_t, grad_scr = refs[:8]
    grad_t, total_scr, back_scr, weight_scr, small_scr, bias_scr = refs[8:14]
    stage_scrs = (refs[14:16], refs[16:18])
    seqs = branch_ref.shape[0]
    step = pl.program_id(0)
    rows = D // pieces
    per_slot = FF // 4
    ones = jnp.ones((16, seqs * KEYS), bf16)

    def send(value_ref, at, width, left):
        if pieces == 1:
            send_refs[0][0, :, left : left + width] = value_ref[:, at : at + width].astype(bf16)
            return
        for j, owner in enumerate(owners(me_ref[0], pieces)):
            first = pl.multiple_of(owner * rows, 16)
            send_refs[j // 4][j % 4, 0, :, left : left + width] = value_ref[
                pl.ds(first, rows), at : at + width
            ].astype(bf16)

    def send_vectors():
        vectors = small_scr[...].astype(bf16)
        if pieces == 1:
            send_refs[0][0, :48, INNER:] = vectors
        else:
            for j in range(pieces):
                send_refs[j // 4][j % 4, 0, :, INNER:] = vectors

    def produce(index, stage):
        act_scr, pre_scr = stage_scrs[stage]
        hidden = pl.ds(pl.multiple_of(index * chunk, 128), chunk)
        pre = dot(second_scr[...], one_scr[:, hidden], NN) + bias_scr[:, hidden]
        half = 0.5 + 0.5 * lax.erf(pre * (0.5**0.5))
        act_scr[...] = (pre * half).astype(bf16)
        slope = half + pre * (jnp.exp2(pre * pre * -0.7213475204444817) * 0.3989422804014327)
        grad_act = dot(grad_scr[...], two_scr[:, hidden], NN)
        pre_scr[...] = (grad_act * slope).astype(bf16)

    def consume(index, stage):
        act_scr, pre_scr = stage_scrs[stage]
        hidden = pl.ds(pl.multiple_of(index * chunk, 128), chunk)
        total_scr[...] += dot(act_scr[...], two_scr[:, hidden], NT)
        back_scr[...] += dot(pre_scr[...], one_scr[:, hidden], NT)
        left = stage * chunk
        weight_scr[:, :chunk] = dot(second_t[...], pre_scr[...], NN)
        send(weight_scr, 0, chunk, left)
        weight_scr[:, chunk : 2 * chunk] = dot(grad_t[...], act_scr[...], NN)
        send(weight_scr, chunk, chunk, left + per_slot)
        hidden_sum = dot(ones, pre_scr[...], NN)[0:1]
        for r in range(chunk // 128):
            at = stage * (chunk // 128) + r
            small_scr[at : at + 1] = hidden_sum[:, r * 128 : (r + 1) * 128]

    @pl.when(step == 0)
    def _():
        for j, owner in enumerate(owners(me_ref[0], pieces)):
            first = pl.multiple_of(owner * rows, 16)
            if pieces == 1:
                out_wide_ref[...] = parts[0][:, :INNER]
            else:
                to = pl.ds(pl.multiple_of(owner * 128, 128), 128)
                for r in range(pieces):
                    out_wide_ref[r * rows : (r + 1) * rows, to] = parts[j][
                        :, r * 128 : (r + 1) * 128
                    ]
            for z in range(4):
                left = INNER + 2 * per_slot * z
                slot = slice(z * per_slot, (z + 1) * per_slot)
                one_scr[pl.ds(first, rows), slot] = parts[j][:, left : left + per_slot]
                two_scr[pl.ds(first, rows), slot] = parts[j][
                    :, left + per_slot : left + 2 * per_slot
                ]
        if n_bias == 1:
            bias_scr[...] = bias_refs[0][...].astype(f32)
        else:
            for z in range(4):
                row = bias_refs[z][rows:, :per_slot].astype(f32)[0:1]
                bias_scr[:, z * per_slot : (z + 1) * per_slot] = row
        count = tokens_ref.shape[0]
        for scr, ref in ((total_scr, tokens_ref), (back_scr, grad_ref)):
            scr[:count] = ref[...].astype(f32)
            scr[count:] = jnp.zeros_like(scr[count:])
        for s in range(seqs):
            block = slice(s * KEYS, (s + 1) * KEYS)
            grad_scr[block] = sequence_rows(back_scr, s).astype(bf16)
            middle = sequence_rows(total_scr, s) + rows_ref[BIAS_OUT]
            middle = middle + dot(mixed_ref[s, :KEYS], out_wide_ref[...], NT)
            middle_scr[block] = middle
            scaled, inverse = normalize(middle)
            scaled_scr[block] = scaled
            inverse_scr[block] = inverse
            second_scr[block] = (scaled * rows_ref[GAIN_TWO] + rows_ref[SHIFT_TWO]).astype(bf16)
        second_t[...] = second_scr[...].T
        grad_t[...] = grad_scr[...].T
        total_scr[...] = jnp.zeros_like(total_scr)
        back_scr[...] = jnp.zeros_like(back_scr)
        small_scr[...] = jnp.zeros_like(small_scr)
        produce(0, 0)

    @pl.when(step < 4)
    def _():
        produce(2 * step + 1, 1)
        consume(2 * step, 0)
        produce(jnp.minimum(2 * step + 2, FF // chunk - 1), 0)
        consume(2 * step + 1, 1)
        send_vectors()

    @pl.when(step == 4)
    def _():
        sums = [jnp.zeros((1, D), f32) for _ in range(2)]
        for s in range(seqs):
            block = slice(s * KEYS, (s + 1) * KEYS)
            output = middle_scr[block] + total_scr[block] + rows_ref[BIAS_TWO]
            total_scr[s * LEN : (s + 1) * LEN] = output[:LEN]
        out_ref[...] = total_scr[: seqs * LEN].astype(bf16)
        for s in range(seqs):
            block = slice(s * KEYS, (s + 1) * KEYS)
            scaled, inverse = scaled_scr[block], inverse_scr[block]
            grad_second = back_scr[block]
            grad_middle = grad_scr[block].astype(f32) + normalize_back(
                grad_second, rows_ref[GAIN_TWO], scaled, inverse
            )
            middle_grad_ref[s, :KEYS] = grad_middle
            branch_ref[s, :KEYS] = grad_middle.astype(bf16)
            branch_ref[s, KEYS:] = jnp.zeros((ROWS - KEYS, D), bf16)
            for k, term in enumerate((grad_second * scaled, grad_second)):
                sums[k] = sums[k] + jnp.sum(term, axis=0, keepdims=True)
        branch = jnp.concatenate([branch_ref[s, :KEYS] for s in range(seqs)], axis=0)
        sums.append(dot(ones, branch, NN)[0:1])
        sums.append(dot(ones, grad_scr[...], NN)[0:1])
        for k in range(4):
            for r in range(D // 128):
                at = 3 * k + r
                small_scr[at : at + 1] = sums[k][:, r * 128 : (r + 1) * 128]
        mixed = jnp.concatenate([mixed_ref[s, :KEYS] for s in range(seqs)], axis=0)
        weight_scr[...] = dot(branch, mixed, TN)
        if pieces == 1:
            send_refs[0][0, :, :INNER] = weight_scr[...].astype(bf16)
        else:
            for j, owner in enumerate(owners(me_ref[0], pieces)):
                to = pl.ds(pl.multiple_of(owner * 128, 128), 128)
                for r in range(pieces):
                    send_refs[j // 4][j % 4, 0, :, r * 128 : (r + 1) * 128] = weight_scr[
                        r * rows : (r + 1) * rows, to
                    ].astype(bf16)
        send_vectors()


def forward(me, tokens, cotangent, rows_in, biases, mixed, parts):
    seqs = tokens.shape[0] // LEN
    pieces = len(parts)
    chunk = 256
    if pieces > 1:
        send_shapes = [(pieces // 2, 5, D // pieces, BLOCK)] * 2
        send_specs = [pl.BlockSpec((pieces // 2, 1, D // pieces, BLOCK), lambda c: (0, c, 0, 0))] * 2
    else:
        send_shapes = [(5, D, BLOCK)]
        send_specs = [pl.BlockSpec((1, D, BLOCK), lambda c: (c, 0, 0))]
    rows3 = (seqs, ROWS, D)
    rows2 = (seqs * KEYS, D)
    return pl.pallas_call(
        functools.partial(forward_kernel, pieces, len(biases), chunk),
        grid=(5,),
        in_specs=[
            pl.BlockSpec(memory_space=pltpu.SMEM),
            whole(tokens.shape),
            whole(tokens.shape),
            whole((8, D)),
        ]
        + [whole(b.shape) for b in biases]
        + [whole(mixed.shape)]
        + [whole(p.shape) for p in parts],
        out_specs=[whole(tokens.shape), whole(rows3), whole(rows3), whole((D, INNER))]
        + send_specs,
        out_shape=[
            jax.ShapeDtypeStruct(tokens.shape, bf16),
            jax.ShapeDtypeStruct(rows3, f32),
            pltpu.VMEM(rows3, bf16),
            pltpu.VMEM((D, INNER), bf16),
        ]
        + [pltpu.VMEM(s, bf16) for s in send_shapes],
        scratch_shapes=[
            pltpu.VMEM((D, FF), bf16),
            pltpu.VMEM((D, FF), bf16),
            pltpu.VMEM(rows2, f32),
            pltpu.VMEM(rows2, f32),
            pltpu.VMEM((seqs * KEYS, 1), f32),
            pltpu.VMEM(rows2, bf16),
            pltpu.VMEM((D, seqs * KEYS), bf16),
            pltpu.VMEM(rows2, bf16),
            pltpu.VMEM((D, seqs * KEYS), bf16),
            pltpu.VMEM(rows2, f32),
            pltpu.VMEM(rows2, f32),
            pltpu.VMEM((D, INNER), f32),
            pltpu.VMEM((48, 128), f32),
            pltpu.VMEM((1, FF), f32),
        ]
        + [pltpu.VMEM((seqs * KEYS, chunk), bf16)] * 4,
        compiler_params=pltpu.CompilerParams(vmem_limit_bytes=36 * 1024 * 1024),
        cost_estimate=cost(30),
        name="forward",
    )(me, tokens, cotangent, rows_in, *biases, mixed, *parts)


def mixed_gradient_kernel(branch_ref, out_wide_ref, mixed_ref, grad_ref, delta_ref):
    lane = lax.broadcasted_iota(jnp.int32, (8, WIDE), 1)
    gather = (lane >> 6 == lax.broadcasted_iota(jnp.int32, (8, WIDE), 0)).astype(bf16)
    for g in range(delta_ref.shape[1]):
        columns = slice(g * WIDE, (g + 1) * WIDE)
        grad = dot(branch_ref[0], out_wide_ref[:, columns], NN).astype(bf16)
        grad_ref[0, :, columns] = grad
        product = grad.astype(f32) * mixed_ref[0, :, columns].astype(f32)
        first = product.astype(bf16)
        second = (product - first.astype(f32)).astype(bf16)
        delta_ref[0, g] = dot(gather, first, NT) + dot(gather, second, NT)


def mixed_gradient(branch, out_wide, mixed):
    seqs = branch.shape[0]
    each = 2
    columns = pl.BlockSpec((1, ROWS, each * WIDE), lambda s, g: (s, 0, g))
    return pl.pallas_call(
        mixed_gradient_kernel,
        grid=(seqs, GROUPS // each),
        in_specs=[
            pl.BlockSpec((1, ROWS, D), lambda s, g: (s, 0, 0)),
            pl.BlockSpec((D, each * WIDE), lambda s, g: (0, g)),
            columns,
        ],
        out_specs=[columns, pl.BlockSpec((1, each, 8, ROWS), lambda s, g: (s, g, 0, 0))],
        out_shape=[
            pltpu.HBM((seqs, ROWS, INNER), bf16),
            pltpu.HBM((seqs, GROUPS, 8, ROWS), f32),
        ],
        compiler_params=pltpu.CompilerParams(vmem_limit_bytes=16 * 1024 * 1024),
        cost_estimate=cost(5),
        name="mixed_gradient",
    )(branch, out_wide, mixed)


def backward_kernel(pieces, me_ref, *refs):
    grad_ref, delta_ref, scaled_ref, projected_ref, exp_ref, inverse_ref = refs[:6]
    wide_ref, norm_ref = refs[6:8]
    refs = refs[8:]
    n_out = 2 if pieces > 1 else 1
    back_ref = refs[0]
    send_refs = refs[1 : 1 + n_out]
    grad_scr, prob_scr, turned_scr, weight_scr, small_scr, sum_scr, norm_scr = refs[1 + n_out :]
    group, seq = pl.program_id(0), pl.program_id(1)
    groups, seqs = pl.num_programs(0), pl.num_programs(1)
    rows = D // pieces

    @pl.when((group == 0) & (seq == 0))
    def _():
        small_scr[...] = jnp.zeros_like(small_scr)
        norm_scr[...] = jnp.zeros_like(norm_scr)

    lane = lax.broadcasted_iota(jnp.int32, (1, 128), 1)
    low = lane < 64
    kept = {}
    turned_keys = {}

    def parts(head):
        columns = slice(head // 2 * 128, head // 2 * 128 + 128)
        return columns, head % 2, grad_ref[0, :, columns]

    def score_gradients(head):
        columns, half, grad = parts(head)
        mine = low if half == 0 else jnp.logical_not(low)
        value = projected_ref[0, :KEYS, 2 * WIDE + columns.start : 2 * WIDE + columns.stop]
        own_value = jnp.where(mine, value, bf16(0))
        inverse = inverse_ref[0, 0, head : head + 1].astype(bf16)
        delta = delta_ref[0, 0, head : head + 1]
        for start, width, keys in QUERY_BLOCKS:
            block = slice(start, start + width)
            change = dot(own_value[:keys], grad[block], NT) - delta[:, block]
            probability = exp_ref[0, head, :keys, block] * inverse[:, block]
            prob_scr[half, :keys, block] = probability
            grad_scr[half, :keys, block] = probability * change.astype(bf16)

    def input_gradients(head):
        columns, half, grad = parts(head)
        pair = head // 2
        query = projected_ref[0, :, columns]
        if half == 0:
            turned_keys[pair] = projected_ref[0, :KEYS, WIDE + columns.start : WIDE + columns.stop].T
        turned = turned_keys[pair]
        side = slice(64 * half, 64 * half + 64)
        for start, width, keys in QUERY_BLOCKS:
            block = slice(start, start + width)
            turned_scr[head * 64 : (head + 1) * 64, block] = dot(
                turned[side, :keys], grad_scr[half, :keys, block], NN
            ) * (HEAD_DIM**-0.5)
        for start, stop, seen in KEY_RANGES:
            value_grad = dot(prob_scr[half, start:stop, seen:], grad[seen:], NN)
            key_grad = dot(grad_scr[half, start:stop, seen:], query[seen:], NN)
            if half == 0:
                kept[start] = (value_grad, key_grad)
            else:
                at = slice(WIDE + columns.start, WIDE + columns.stop)
                back_ref[0, start:stop, at] = jnp.where(low, kept[start][1], key_grad).astype(bf16)
                at = slice(2 * WIDE + columns.start, 2 * WIDE + columns.stop)
                back_ref[0, start:stop, at] = jnp.where(low, kept[start][0], value_grad).astype(bf16)

    score_gradients(0)
    for head in range(GROUP):
        if head + 1 < GROUP:
            score_gradients(head + 1)
        input_gradients(head)
    back_ref[0, :KEYS, :WIDE] = turned_scr[...].T[:KEYS].astype(bf16)

    back = back_ref[0, :KEYS]
    weight = dot(scaled_ref[0, :KEYS], back, TN)
    total = dot(jnp.ones((16, KEYS), bf16), back, NN)[0:1]

    @pl.when(seq == 0)
    def _():
        weight_scr[...] = weight
        sum_scr[0:1] = total

    @pl.when(seq > 0)
    def _():
        weight_scr[...] += weight
        sum_scr[0:1] += total

    @pl.when(seq == seqs - 1)
    def _():
        sums = sum_scr[0:1]
        for r in range(WIDE // 128):
            at = group * (2 * WIDE // 128) + r
            small_scr[pl.ds(at, 1)] = sums[:, r * 128 : r * 128 + 128]
            at = at + WIDE // 128
            small_scr[pl.ds(at, 1)] = sums[:, 2 * WIDE + r * 128 : 2 * WIDE + r * 128 + 128]
        wide = wide_ref[...].astype(f32)
        scaled_weight = weight_scr[...]
        norm_scr[:, 0:1] += jnp.sum(scaled_weight * wide, axis=1, keepdims=True)
        norm_scr[:, 1:2] += jnp.sum(sums * wide, axis=1, keepdims=True)
        weight_scr[...] = scaled_weight * norm_ref[:, GAIN_ONE] + sums * norm_ref[:, SHIFT_ONE]
        start = pl.multiple_of(group * QKV, 128)
        if pieces == 1:
            send_refs[0][:, pl.ds(start, QKV)] = weight_scr[...].astype(bf16)
        else:
            for j, owner in enumerate(owners(me_ref[0], pieces)):
                first = pl.multiple_of(owner * rows, 16)
                send_refs[j // 4][j % 4, :, pl.ds(start, QKV)] = weight_scr[
                    pl.ds(first, rows)
                ].astype(bf16)

    @pl.when((group == groups - 1) & (seq == seqs - 1))
    def _():
        turned = norm_scr[...].T
        for k in range(2):
            for r in range(D // 128):
                small_scr[40 + 3 * k + r : 41 + 3 * k + r] = turned[
                    k : k + 1, r * 128 : (r + 1) * 128
                ]
        small = small_scr[...].astype(bf16)
        if pieces == 1:
            send_refs[0][:48, send_refs[0].shape[1] - SMALL :] = small
        else:
            for j in range(pieces):
                edge = send_refs[0].shape[2] - SMALL
                send_refs[j // 4][j % 4, :, edge:] = small


def backward(me, pieces, first_group, groups, grads, scaled, norm, saved):
    operands = [
        pltpu.with_memory_space_constraint(x, pltpu.HBM)
        for x in (*grads, scaled, saved[0], saved[2], saved[3], saved[4])
    ]
    seqs = scaled.shape[0]
    width = groups * QKV + SMALL
    if pieces > 1:
        send_shapes = [(pieces // 2, D // pieces, width)] * 2
    else:
        send_shapes = [(D, width)]
    columns = pl.BlockSpec((1, ROWS, WIDE), lambda g, s: (s, 0, g + first_group))
    heads = pl.BlockSpec((1, 1, 8, ROWS), lambda g, s: (s, g + first_group, 0, 0))
    rows_block = pl.BlockSpec((1, ROWS, D), lambda g, s: (s, 0, 0))
    return pl.pallas_call(
        functools.partial(backward_kernel, pieces),
        grid=(groups, seqs),
        in_specs=[
            pl.BlockSpec(memory_space=pltpu.SMEM),
            columns,
            heads,
            rows_block,
            pl.BlockSpec((1, ROWS, QKV), lambda g, s: (s, 0, g + first_group)),
            pl.BlockSpec((1, GROUP, KEYS, ROWS), lambda g, s: (s, g + first_group, 0, 0)),
            heads,
            pl.BlockSpec((D, QKV), lambda g, s: (0, g + first_group)),
            whole((D, 8)),
        ],
        out_specs=[pl.BlockSpec((1, ROWS, QKV), lambda g, s: (s, 0, g))]
        + [whole(s) for s in send_shapes],
        out_shape=[jax.ShapeDtypeStruct((seqs, ROWS, groups * QKV), bf16)]
        + [jax.ShapeDtypeStruct(s, bf16) for s in send_shapes],
        scratch_shapes=[
            pltpu.VMEM((2, KEYS, ROWS), bf16),
            pltpu.VMEM((2, KEYS, ROWS), bf16),
            pltpu.VMEM((WIDE, ROWS), f32),
            pltpu.VMEM((D, QKV), f32),
            pltpu.VMEM((48, 128), f32),
            pltpu.VMEM((8, QKV), f32),
            pltpu.VMEM((D, 128), f32),
        ],
        compiler_params=pltpu.CompilerParams(vmem_limit_bytes=23 * 1024 * 1024),
        cost_estimate=cost(11 * groups),
        name="backward",
    )(me, *operands, norm)


def early_kernel(back_ref, wide_ref, out_ref):
    for s in range(out_ref.shape[0]):
        grad = dot(back_ref[s, :KEYS], wide_ref[...], NT)
        before = jnp.where(pl.program_id(0) == 0, 0.0, out_ref[s])
        out_ref[s] = before + grad


def early_gradient(back, weights):
    seqs, groups = back.shape[0], back.shape[2] // QKV
    return pl.pallas_call(
        early_kernel,
        grid=(groups,),
        in_specs=[
            pl.BlockSpec((seqs, ROWS, QKV), lambda g: (0, 0, g)),
            pl.BlockSpec((D, QKV), lambda g: (0, g)),
        ],
        out_specs=whole((seqs, KEYS, D)),
        out_shape=jax.ShapeDtypeStruct((seqs, KEYS, D), f32),
        compiler_params=pltpu.CompilerParams(vmem_limit_bytes=14 * 1024 * 1024),
        cost_estimate=cost(5),
        name="early_gradient",
    )(back, weights)


def input_kernel(
    tokens_ref, middle_grad_ref, rows_ref, early_ref, back_ref, wide_ref, out_ref, rows_scr
):
    count = tokens_ref.shape[0]
    rows_scr[:count] = tokens_ref[...].astype(f32)
    for s in range(middle_grad_ref.shape[0]):
        grad_first = early_ref[s] + dot(back_ref[s, :KEYS], wide_ref[...], NT)
        given = slice(s * LEN, (s + 1) * LEN)
        scaled, inverse = normalize(rows_scr[given])
        rows_scr[given] = middle_grad_ref[s, :LEN] + normalize_back(
            grad_first[:LEN], rows_ref[GAIN_ONE], scaled, inverse
        )
    out_ref[...] = rows_scr[:count]


def input_gradient(tokens, middle_grad, rows_in, early, back, weights):
    return pl.pallas_call(
        input_kernel,
        grid=(1,),
        in_specs=[
            whole(tokens.shape),
            whole(middle_grad.shape),
            whole(rows_in.shape),
            whole(early.shape),
            whole(back.shape),
            pl.BlockSpec((D, QKV), lambda g: (0, GROUPS - 1)),
        ],
        out_specs=whole(tokens.shape),
        out_shape=jax.ShapeDtypeStruct(tokens.shape, f32),
        scratch_shapes=[pltpu.VMEM((middle_grad.shape[0] * KEYS, D), f32)],
        compiler_params=pltpu.CompilerParams(vmem_limit_bytes=16 * 1024 * 1024),
        cost_estimate=cost(4),
        name="input_gradient",
    )(tokens, middle_grad, rows_in, early, back, weights)


def join_lines(values):
    return jnp.concatenate([values[k : k + 1] for k in range(values.shape[0])], axis=1)


def hidden_end_kernel(block_ref, rest_ref, arrived_ref, one_ref, two_ref, bias_ref, out_ref, *refs):
    rows, slot = one_ref.shape
    block = block_ref[...] + arrived_ref[:, :BLOCK].astype(f32)
    rest = rest_ref[...] + arrived_ref[:, BLOCK:].astype(f32)
    one_ref[...] = block[:, :slot]
    two_ref[...] = block[:, slot : 2 * slot]
    bias_ref[...] = join_lines(block[: slot // 128, INNER:]).reshape(slot)
    width = out_ref.shape[0]
    parts = [rest[:, r * width : (r + 1) * width] for r in range(INNER // width)]
    out_ref[...] = jnp.concatenate(parts, axis=0).T
    for k, ref in enumerate(refs):
        ref[...] = join_lines(rest[3 * k : 3 * k + 3, INNER:]).reshape(D)


def hidden_end(block, rest, arrived, slot):
    rows = block.shape[0]
    width = INNER // (D // rows)
    vector = jax.ShapeDtypeStruct((D,), f32)
    return pl.pallas_call(
        hidden_end_kernel,
        out_shape=[
            jax.ShapeDtypeStruct((rows, slot), f32),
            jax.ShapeDtypeStruct((rows, slot), f32),
            jax.ShapeDtypeStruct((slot,), f32),
            jax.ShapeDtypeStruct((width, D), f32),
        ]
        + [vector] * 4,
        compiler_params=pltpu.CompilerParams(vmem_limit_bytes=8 * 1024 * 1024),
        cost_estimate=cost(2),
        name="hidden_end",
    )(block, rest, arrived)


def heads_end_kernel(early_ref, early_line_ref, late_ref, late_line_ref, weight_ref, bias_ref, *refs):
    early = early_ref[...] + early_line_ref[...].astype(f32)
    late = late_ref[...] + late_line_ref[...].astype(f32)
    lines = WIDE // 128
    norms, group = 0.0, 0
    for part in (early, late):
        edge = part.shape[1] - SMALL
        for g in range(edge // QKV):
            for k in range(3):
                left = g * QKV + k * WIDE
                to = k * INNER + group * WIDE
                weight_ref[:, to : to + WIDE] = part[:, left : left + WIDE]
            for k in range(2):
                first = (2 * g + k) * lines
                values = join_lines(part[first : first + lines, edge:])
                at = k * INNER + group * WIDE
                bias_ref[at : at + WIDE] = values.reshape(WIDE)
            group += 1
        norms = norms + part[40:48, edge:]
    for k, ref in enumerate(refs):
        ref[...] = join_lines(norms[3 * k : 3 * k + 3]).reshape(D)


def heads_end(early, early_line, late, late_line):
    vector = jax.ShapeDtypeStruct((D,), f32)
    return pl.pallas_call(
        heads_end_kernel,
        out_shape=[
            jax.ShapeDtypeStruct((early.shape[0], 3 * INNER), f32),
            jax.ShapeDtypeStruct((2 * INNER,), f32),
            vector,
            vector,
        ],
        compiler_params=pltpu.CompilerParams(vmem_limit_bytes=8 * 1024 * 1024),
        cost_estimate=cost(2),
        name="heads_end",
    )(early, early_line, late, late_line)


def swap(values, mask):
    size = lax.axis_size("tok")
    return lax.ppermute(values, "tok", [(i, i ^ mask) for i in range(size)])


def swap_half_plane(values, stage):
    size = lax.axis_size("tok")
    pairs = [(t, t ^ (2 if (t % 2 == 0) == (stage == 0) else 4)) for t in range(size)]
    return lax.ppermute(values, "tok", pairs)


def swap_half_line(values, stage):
    tok, mlp = lax.axis_size("tok"), lax.axis_size("mlp")
    pairs = []
    for t in range(tok):
        for z in range(mlp):
            far = (t % 2 == 0) == (stage == 0)
            pairs.append((t * mlp + z, t * mlp + (z ^ (2 if far else 1))))
    return lax.ppermute(values.astype(bf16), ("tok", "mlp"), pairs)


def after(values, *earlier):
    return lax.optimization_barrier((values,) + earlier)


def wide(values):
    return values.astype(f32)


def join(kept, arrived):
    return (wide(kept) + wide(arrived)).astype(bf16)


def body(
    tokens,
    action_mask,
    ln1_gain,
    ln1_bias,
    w_qkv,
    bias_qv,
    w_out,
    bias_out,
    ln2_gain,
    ln2_bias,
    w_fc1,
    bias_fc1,
    w_fc2,
    bias_fc2,
    out_grad,
):
    rows = w_qkv.shape[0]
    tok = lax.axis_size("tok")
    mlp = lax.axis_size("mlp")
    slot = w_fc1.shape[1]
    fast = tok == 8 and mlp == 4
    pieces = tok if fast else 1
    me = lax.axis_index("tok").astype(jnp.int32).reshape(1)
    chips = (2, 4, 6)
    odd = (me[0] & 1) == 1

    def pick(if_odd, if_even):
        return jnp.where(odd, if_odd, if_even)


    vectors = (bias_out, ln2_gain, ln2_bias, bias_fc2, ln1_gain, ln1_bias)
    me_a = me
    if fast:
        first_near = [swap_half_plane(w_qkv, stage) for stage in (0, 1)]
        first_near.append(swap_half_plane(first_near[0], 1))
        first_other = swap(w_qkv, 1)
        hidden_pack, out_block, rows_in, columns_in, bias_pair = prepare(
            w_fc1, w_fc2, bias_fc1, w_out, bias_qv, vectors
        )
        line = jnp.stack([hidden_pack, swap_half_line(hidden_pack, 0)])
        line = jnp.concatenate([line, swap_half_line(line, 1)])
        line = [line[0], pick(line[1], line[2]), pick(line[2], line[1]), line[3]]
        norm_tokens, first_near[0] = after(tokens, first_near[0])
        normed, scaled = first_norm(norm_tokens, rows_in)
        first_parts = [w_qkv] + first_near + [first_other] + [swap(p, 1) for p in first_near]
        hidden_own = jnp.concatenate([out_block] + [part[:rows] for part in line], axis=1)
        me_a, hidden_own = after(me, hidden_own)
        hidden_near = [swap(hidden_own, mask) for mask in chips + (1,)]
        biases = line
    else:
        rows_in = jnp.pad(wide(jnp.stack(vectors)), ((0, 2), (0, 0)))
        columns_in = rows_in.T
        bias_pair = wide(bias_qv).reshape(1, -1)
        normed, scaled = first_norm(tokens, rows_in)
        first_parts = [lax.all_gather(w_qkv, "tok", axis=0, tiled=True)]
        line = lax.all_gather(jnp.concatenate([w_fc1, w_fc2.T], axis=1), "mlp", axis=1, tiled=True)
        line = lax.all_gather(line, "tok", axis=0, tiled=True)
        biases = [lax.all_gather(bias_fc1, "mlp", axis=0, tiled=True).reshape(1, -1)]
        out_all = lax.all_gather(w_out, "tok", axis=0, tiled=True).T
        hidden_parts = [jnp.concatenate([out_all, line], axis=1)]

    saved = list(attend(me_a, normed, first_parts, bias_pair, action_mask))
    weights = saved[4]
    if fast:
        saved[1], *hidden_near = after(saved[1], *hidden_near)
        hidden_other = hidden_near.pop()
        hidden_parts = [hidden_own] + hidden_near + [hidden_other]
        hidden_parts = hidden_parts + [swap(part, 1) for part in hidden_near]

    output, middle_grad, branch, out_wide, *hidden_sends = forward(
        me, tokens, out_grad, rows_in, biases, saved[1], hidden_parts
    )

    grads = list(mixed_gradient(branch, out_wide, saved[1]))

    def back(me, group, count):
        return backward(me, pieces, group, count, grads, scaled, columns_in, saved)

    if not fast:
        back_a, sends_a = back(me, 0, 3)
        back_b, sends_b = back(me, 3, 1)
        early = early_gradient(back_a, weights)
        input_grad = input_gradient(tokens, middle_grad, rows_in, early, back_b, weights)
        return slow_end(output, input_grad, hidden_sends[0], (sends_a, sends_b), slot)

    arrived = swap(hidden_sends[1], 1)
    grads[0], arrived = after(grads[0], arrived)
    hidden = join(hidden_sends[0], arrived)
    me_1, hidden = after(me, hidden)
    near = [swap(hidden[k], chips[k - 1]) for k in (1, 2, 3)]
    back_a, *sends_a = back(me_1, 0, 3)

    back_a, *near = after(back_a, *near)
    hidden = wide(hidden[0]) + wide(near[0]) + wide(near[1]) + wide(near[2])
    sent = jnp.stack([pick(hidden[1], hidden[2]), hidden[3], hidden[4]]).astype(bf16)
    group_a = join(sends_a[0], swap(sends_a[1], 1))
    me_2, group_a, sent = after(me, group_a, sent)
    line_1 = swap_half_line(sent, 0)
    near_a = [swap(group_a[k], chips[k - 1]) for k in (1, 2, 3)]
    back_b, *sends_b = back(me_2, 3, 1)

    back_b, line_1, *near_a = after(back_b, line_1, *near_a)
    total_a = wide(group_a[0]) + wide(near_a[0]) + wide(near_a[1]) + wide(near_a[2])
    sent, kept_b, sent_b = after(total_a.astype(bf16), *sends_b)
    line_a = swap_half_line(sent, 1)
    group_b = join(kept_b, swap(sent_b, 1))
    line_1, group_b = after(line_1, group_b)
    block = hidden[0] + wide(line_1[0])
    middle_block = pick(hidden[2], hidden[1]) + wide(line_1[1])
    rest = hidden[4] + wide(line_1[2])
    sent = jnp.concatenate([middle_block, rest], axis=1).astype(bf16)
    group_b, sent = after(group_b, sent)
    line_2 = swap_half_line(sent, 1)
    near_b = [swap(group_b[k], chips[k - 1]) for k in (1, 2, 3)]
    line_a, *near_b = after(line_a, *near_b)
    total_b = wide(group_b[0]) + wide(near_b[0]) + wide(near_b[1]) + wide(near_b[2])
    total_a = total_a + wide(line_a)
    back_a, sent_b, sent_a = after(back_a, total_b.astype(bf16), total_a.astype(bf16))
    line_b = swap_half_line(sent_b, 0)
    line_a = swap_half_line(sent_a, 0)
    early = early_gradient(back_a, weights)

    early, line_b = after(early, line_b)
    total_b = total_b + wide(line_b)
    early, sent = after(early, total_b.astype(bf16))
    line_b = swap_half_line(sent, 1)
    input_grad = input_gradient(tokens, middle_grad, rows_in, early, back_b, weights)

    input_grad, line_2 = after(input_grad, line_2)
    hidden_grads = hidden_end(block, rest, line_2, slot)
    one_grad, line_a, line_b = after(hidden_grads[0], line_a, line_b)
    qkv_grad, bias_grad, gain_grad, shift_grad = heads_end(total_a, line_a, total_b, line_b)
    _, two_grad, hidden_bias_grad, out_rows, *vector_grads = hidden_grads
    return (
        output,
        input_grad,
        gain_grad,
        shift_grad,
        qkv_grad,
        bias_grad,
        out_rows,
        vector_grads[2],
        vector_grads[0],
        vector_grads[1],
        one_grad,
        hidden_bias_grad,
        two_grad.T,
        vector_grads[3],
    )


def slow_end(output, input_grad, hidden, sends, slot):
    def scatter(values):
        values = lax.psum_scatter(wide(values), "tok", scatter_dimension=0, tiled=True)
        return lax.psum(values, "mlp")

    hidden = wide(hidden)
    blocks = jnp.concatenate([hidden[k, :, :INNER] for k in range(4)], axis=1)
    blocks = lax.psum_scatter(blocks, "tok", scatter_dimension=0, tiled=True)
    hidden_sum = lax.psum_scatter(blocks, "mlp", scatter_dimension=1, tiled=True)
    out_rows = scatter(hidden[4, :, :INNER].T)
    lines = slot // 128
    small = lax.psum(hidden[:, :48, INNER:], ("tok", "mlp"))
    bias_sum = lax.dynamic_index_in_dim(small[:4, :lines], lax.axis_index("mlp"), 0, False)
    small = small[4]
    weights = [scatter(s[:, :-SMALL]) for s in sends]
    smalls = [lax.psum(wide(s[:48, -SMALL:]), ("tok", "mlp")) for s in sends]
    return results(output, input_grad, weights, smalls, out_rows, small, hidden_sum, bias_sum)


def results(output, input_grad, weights, smalls, out_rows, small, hidden_sum, bias_sum):
    blocks = []
    for part in weights:
        blocks += [part[:, at : at + WIDE] for at in range(0, part.shape[1], WIDE)]
    qkv_grad = jnp.concatenate([block for k in range(3) for block in blocks[k::3]], axis=1)
    lines = WIDE // 128
    biases = []
    for part, weight in zip(smalls, weights):
        count = 2 * (weight.shape[1] // QKV)
        biases += [part[k * lines : (k + 1) * lines] for k in range(count)]
    bias_grad = jnp.concatenate(biases[0::2] + biases[1::2], axis=0).reshape(-1)
    norm_grad = smalls[0][40:46] + smalls[1][40:46]
    vectors = [small[3 * k : 3 * k + 3].reshape(-1) for k in range(4)]
    slot = hidden_sum.shape[1] // 2
    return (
        output,
        input_grad,
        norm_grad[:3].reshape(-1),
        norm_grad[3:].reshape(-1),
        qkv_grad,
        bias_grad,
        out_rows,
        vectors[2],
        vectors[0],
        vectors[1],
        hidden_sum[:, :slot],
        bias_sum.reshape(-1),
        hidden_sum[:, slot:].T,
        vectors[3],
    )


def solution(mesh):
    placed = (
        P(("tok", "mlp"), None),
        P(("tok", "mlp"), None),
        P(),
        P(),
        P("tok", None),
        P(),
        P("tok", None),
        P(),
        P(),
        P(),
        P("tok", "mlp"),
        P("mlp"),
        P("mlp", "tok"),
        P(),
        P(("tok", "mlp"), None),
    )
    return jax.shard_map(
        body,
        mesh=mesh,
        in_specs=placed,
        out_specs=(
            P(("tok", "mlp"), None),
            P(("tok", "mlp"), None),
            P(),
            P(),
            P("tok", None),
            P(),
            P("tok", None),
            P(),
            P(),
            P(),
            P("tok", "mlp"),
            P("mlp"),
            P("mlp", "tok"),
            P(),
        ),
        check_vma=False,
    )
```
